32 devices in a mesh: groups: 2 (over x), tensor: 16 (over z, y, core).
Axes of the slice: x: 2, y: 2, z: 4, core: 2. Of those that a mesh axis runs over, the one named last changes fastest.
Arguments:
- hidden: bfloat16 [768, 26624], P('groups', 'tensor'), parts along dimension 0, may hold values from -6 to 6
- down_matrix: bfloat16 [26624, 8192], P('tensor'), may hold values from -0.0546875 to 0.0546875
- shrink_matrices: bfloat16 [32, 26624, 64], P(None, 'tensor'), may hold values from -0.0390625 to 0.0390625
- expand_matrices: bfloat16 [32, 64, 8192], P(None, None, 'tensor'), may hold values from -0.75 to 0.75
- row_adapter_index: int32 [768], P('groups'), parts along dimension 0, may hold values from 0 to 31, as said below
- segment_first_row: int32 [64], P('groups'), parts along dimension 0, may hold values from 0 to 383, as said below
- segment_length: int32 [64], P('groups'), parts along dimension 0, may hold values from 1 to 48, as said below
Outputs:
- mixed: bfloat16 [768, 8192], P('groups', 'tensor'), parts along dimension 0
The draws below stay inside these ranges and needn't reach their ends.
There are 2 independent parts, one for each index of `groups`. The reference program is written for one: setup_inputs(seed, part) draws one part's arguments, and reference() takes and returns one part's arrays. A program takes and returns all parts, laid end to end along the dimension named above; an argument that names none is the same for every part. Nothing has to cross between parts.
Inputs may be any that keep to these rules, and one draw needn't show every extreme that they name: `row_adapter_index`: row r carries the adapter a with segment_first_row[a] <= r < segment_first_row[a] + segment_length[a]. segment_first_row[0] = 0 and segment_first_row[a + 1] = segment_first_row[a] + segment_length[a]. `segment_length`: every adapter has a row; the lengths sum to 384; the longest is exactly 48.
All inputs are finite; a program needn't handle non-finite values.
Results may differ from the reference program's by a relative error of at most 0.004.
Values may be sent and summed in bfloat16 or wider, within the bound.
No kernel may reach another device: no remote copies, remote signals or barrier semaphores. Data moves between devices by JAX's collectives and lax.ppermute only.
A program may use at most 128 MiB of HBM per device.

```python
import jax
import jax.numpy as jnp
from jax import lax

FEATURE_WIDTH = 8192
HIDDEN_WIDTH = 26624
ADAPTER_RANK = 64
ADAPTER_COUNT = 32
ROWS = 384
MOST = 48


def segment_plan(key):
    first, second = jax.random.split(key)
    biggest = jax.random.randint(first, (), 0, ADAPTER_COUNT - 1)
    weights = jax.random.randint(second, (ADAPTER_COUNT,), 500, 1000)
    places = jnp.arange(ADAPTER_COUNT, dtype=jnp.int32)
    is_big = places == biggest
    is_final = places == ADAPTER_COUNT - 1
    eligible = ~is_big & ~is_final
    weights = jnp.where(eligible, weights, 0)
    spare = ROWS - MOST - (ADAPTER_COUNT - 1)
    shares = spare * weights // jnp.sum(weights)
    leftover = spare - jnp.sum(shares)
    others = jnp.cumsum(jnp.where(eligible, 1, 0)) - 1
    shares = shares + jnp.where(eligible & (others < leftover), 1, 0)
    lengths = jnp.where(is_big, MOST, 1 + shares).astype(jnp.int32)
    starts = (jnp.cumsum(lengths) - lengths).astype(jnp.int32)
    rows = jnp.arange(ROWS, dtype=jnp.int32)
    owners = jnp.sum((rows[:, None] >= starts[None, :]).astype(jnp.int32), axis=1) - 1
    return (owners.astype(jnp.int32), starts, lengths)


def draw_row_adapter_index(key, part):
    owners, starts, lengths = segment_plan(key)
    return owners


def draw_segment_first_row(key, part):
    owners, starts, lengths = segment_plan(key)
    return starts


def draw_segment_length(key, part):
    owners, starts, lengths = segment_plan(key)
    return lengths


def strengthened(entries, key, source, target, blocks, factor):
    def block_of(dim):
        return (jnp.arange(entries.shape[dim]) // (entries.shape[dim] // blocks)).reshape((-1,) + (1,) * (entries.ndim - 1 - dim))

    near = jax.random.permutation(key, blocks)[block_of(target)]
    far = (block_of(target) + blocks // 2) % blocks
    return jnp.where((block_of(source) == near) | (block_of(source) == far), factor * entries, entries)


def shard_levels(stream_key, extent, pieces, least, top_value):
    loudness, own = 1.0, jax.random.fold_in(stream_key, 6)
    for axis_at, shards_of in pieces:
        draws = jnp.exp(jax.random.uniform(jax.random.fold_in(own, axis_at), (shards_of,), jnp.float32, least / len(pieces), top_value / len(pieces)))
        loudness = loudness * jnp.repeat(draws, extent[axis_at] // shards_of).reshape([-1 if axis == axis_at else 1 for axis in range(len(extent))])
    return loudness


def noise(stream_key, extent, width, bound, shards=(), kind=jnp.bfloat16):
    values = jax.random.normal(stream_key, extent, jnp.float32) * width
    if len(shards) > 0:
        values = shard_levels(stream_key, extent, shards, -0.22, 0.18) * values
    return jnp.clip(values, min=-bound, max=bound).astype(kind)


def bell_draw_with(stream_key, shape, scale, most, cuts, heavy, held_as=jnp.bfloat16):
    entries = scale * jax.random.normal(stream_key, shape, jnp.float32)
    if cuts:
        entries = entries * shard_levels(stream_key, shape, cuts, -0.22, 0.18)
    return jnp.clip(strengthened(entries, jax.random.fold_in(stream_key, 3), *heavy), -most, most).astype(held_as)


def setup_inputs(seed: int = 0, part: int = 0) -> dict:
    arg_keys = jax.random.split(jax.random.key(seed), 8)
    part_splits = jax.random.split(jax.random.fold_in(arg_keys[7], part), 8)
    hidden = noise(part_splits[0], (ROWS, HIDDEN_WIDTH), 1.0, 6.0, ((1, 16),))
    down_matrix = bell_draw_with(arg_keys[1], (HIDDEN_WIDTH, FEATURE_WIDTH), HIDDEN_WIDTH ** -0.5, 0.0546875, ((0, 16),), (0, 1, 16, 2.0))
    shrink_matrices = noise(arg_keys[2], (ADAPTER_COUNT, HIDDEN_WIDTH, ADAPTER_RANK), HIDDEN_WIDTH ** -0.5, 0.0390625, ((1, 16),))
    expand_matrices = noise(arg_keys[3], (ADAPTER_COUNT, ADAPTER_RANK, FEATURE_WIDTH), ADAPTER_RANK ** -0.5, 0.75, ((2, 16),))
    row_adapter_index = draw_row_adapter_index(jax.random.fold_in(jax.random.fold_in(arg_keys[7], part), 71), part)
    segment_first_row = draw_segment_first_row(jax.random.fold_in(jax.random.fold_in(arg_keys[7], part), 71), part)
    segment_length = draw_segment_length(jax.random.fold_in(jax.random.fold_in(arg_keys[7], part), 71), part)
    return {"hidden": hidden, "down_matrix": down_matrix, "shrink_matrices": shrink_matrices, "expand_matrices": expand_matrices, "row_adapter_index": row_adapter_index, "segment_first_row": segment_first_row, "segment_length": segment_length}


def reference(hidden, down_matrix, shrink_matrices, expand_matrices, row_adapter_index, segment_first_row, segment_length):
    base_output = jnp.dot(hidden, down_matrix, preferred_element_type=jnp.float32)
    rows = jnp.arange(hidden.shape[0], dtype=jnp.int32)
    row_ordering = jnp.arange(ADAPTER_COUNT, dtype=jnp.int32)

    def shrink_step(total, chosen_adapter):
        part = jnp.dot(hidden, shrink_matrices[chosen_adapter], preferred_element_type=jnp.float32)
        return total + jnp.where((row_adapter_index == chosen_adapter)[:, None], part, 0.0), None

    shrink, unused_value = lax.scan(shrink_step, jnp.zeros((hidden.shape[0], ADAPTER_RANK), jnp.float32), row_ordering)
    shrunk_rows = shrink.astype(jnp.bfloat16)

    def expand_iteration(total, chosen_adapter):
        inside = (rows >= segment_first_row[chosen_adapter]) & (rows < segment_first_row[chosen_adapter] + segment_length[chosen_adapter])
        part = jnp.dot(shrunk_rows, expand_matrices[chosen_adapter], preferred_element_type=jnp.float32)
        return total + jnp.where(inside[:, None], part, 0.0), None

    adapter_output, unused_value = lax.scan(expand_iteration, jnp.zeros((hidden.shape[0], FEATURE_WIDTH), jnp.float32), row_ordering)
    return (base_output + adapter_output).astype(jnp.bfloat16)
```

```python
import functools

import jax
import jax.numpy as jnp
from jax import lax
from jax.experimental import pallas as pl
from jax.experimental.pallas import tpu as pltpu
from jax.sharding import PartitionSpec as P

LANES = 128


def product_body(order_ref, hidden_ref, *refs, pairs):
    kept_weights, sent_weights = refs[:pairs], refs[pairs:2 * pairs]
    kept_ref, sent_ref = refs[2 * pairs:]
    width = kept_ref.shape[2]
    weights = jnp.concatenate([ref[...] for ref in (*kept_weights, *sent_weights)], axis=1)
    total = jnp.dot(hidden_ref[...], weights, preferred_element_type=jnp.float32)
    for at in range(pairs):
        kept_ref[at] = total[:, at * width:(at + 1) * width]
        sent_ref[at] = total[:, (pairs + at) * width:(pairs + at + 1) * width].astype(jnp.bfloat16)


def product(hidden, down_matrix, order, width, chunk, chunks, pairs=2):
    rows, depth = hidden.shape
    half = order.shape[0] // 2

    def weight_spec(offset):
        return pl.BlockSpec(
            (depth, width), lambda step, order: (0, order[step * pairs + offset] * chunks + chunk)
        )

    return pl.pallas_call(
        functools.partial(product_body, pairs=pairs),
        grid_spec=pltpu.PrefetchScalarGridSpec(
            num_scalar_prefetch=1,
            grid=(half // pairs,),
            in_specs=[pl.BlockSpec((rows, depth), lambda step, order: (0, 0))]
            + [weight_spec(at) for at in range(pairs)]
            + [weight_spec(half + at) for at in range(pairs)],
            out_specs=[pl.BlockSpec((pairs, rows, width), lambda step, order: (step, 0, 0))] * 2,
        ),
        out_shape=[
            jax.ShapeDtypeStruct((half, rows, width), jnp.float32),
            jax.ShapeDtypeStruct((half, rows, width), jnp.bfloat16),
        ],
        compiler_params=pltpu.CompilerParams(vmem_limit_bytes=48 * 1024 * 1024),
    )(order, hidden, *([down_matrix] * (2 * pairs)))


def swap(value, bit, total):
    return lax.ppermute(value, "tensor", [(place, place ^ bit) for place in range(total)])


def shrink_partial(hidden, shrink_matrices, row_adapter_index):
    adapter_total = shrink_matrices.shape[0]
    every_adapter = jnp.einsum(
        "hq,gqu->hgu", hidden, shrink_matrices, preferred_element_type=jnp.float32
    )
    picked = row_adapter_index[:, None] == jnp.arange(adapter_total, dtype=jnp.int32)[None, :]
    return jnp.sum(jnp.where(picked[:, :, None], every_adapter, 0.0), axis=1)


def expand_partial(shrunk_rows, expand_matrices, segment_first_row, segment_length):
    rows_total = shrunk_rows.shape[0]
    adapter_total = expand_matrices.shape[0]
    rows = jnp.arange(rows_total, dtype=jnp.int32)
    inside = (rows[:, None] >= segment_first_row[None, :]) & (
        rows[:, None] < (segment_first_row + segment_length)[None, :]
    )
    spread = jnp.where(inside[:, :, None], shrunk_rows[:, None, :], jnp.zeros((), jnp.bfloat16))
    spread = spread.reshape(rows_total, adapter_total * shrunk_rows.shape[1])
    adapter_table = expand_matrices.reshape(
        adapter_total * expand_matrices.shape[1], expand_matrices.shape[2]
    )
    return jnp.dot(spread, adapter_table, preferred_element_type=jnp.float32)


def chunk_bits(total, chunk, chunks):
    bits = [1 << at for at in range(total.bit_length() - 1)]
    if chunks > 1 and chunk == 1:
        bits[1], bits[2] = bits[2], bits[1]
    return bits


def target_order(me, bits):
    relative = [0]
    for bit in reversed(bits):
        relative = relative + [place | bit for place in relative]
    return jnp.array(relative, dtype=jnp.int32) ^ me


def on_device(
    total,
    hidden,
    down_matrix,
    shrink_matrices,
    expand_matrices,
    row_adapter_index,
    segment_first_row,
    segment_length,
):
    me = lax.axis_index("tensor").astype(jnp.int32)
    own_width = down_matrix.shape[1] // total
    width = min(LANES, own_width)
    chunks = own_width // width
    every_bits = [chunk_bits(total, chunk, chunks) for chunk in range(chunks)]

    kept, sent = [], []
    for chunk in range(chunks):
        first, second = product(
            hidden, down_matrix, target_order(me, every_bits[chunk]), width, chunk, chunks
        )
        kept.append(first)
        sent.append(second)

    shrunk = jnp.swapaxes(shrink_partial(hidden, shrink_matrices, row_adapter_index), 0, 1)
    for bit in every_bits[0]:
        shrunk = shrunk + swap(shrunk, bit, total)
    shrunk_rows = jnp.swapaxes(shrunk, 0, 1).astype(jnp.bfloat16)

    parts = []
    for chunk in range(chunks):
        bits = every_bits[chunk]
        for level, bit in enumerate(bits):
            arrived = swap(sent[chunk], bit, total)
            summed = kept[chunk] + arrived.astype(jnp.float32)
            if level + 1 < len(bits):
                half = summed.shape[0] // 2
                kept[chunk] = summed[:half]
                sent[chunk] = summed[half:].astype(jnp.bfloat16)
            else:
                parts.append(summed[0])
    base = jnp.concatenate(parts, axis=1)
    adapter_output = expand_partial(shrunk_rows, expand_matrices, segment_first_row, segment_length)
    return (base + adapter_output).astype(jnp.bfloat16)


def solution(mesh):
    in_specs = (
        P("groups", "tensor"),
        P("tensor", None),
        P(None, "tensor", None),
        P(None, None, "tensor"),
        P("groups"),
        P("groups"),
        P("groups"),
    )
    out_specs = P("groups", "tensor")
    return jax.shard_map(
        functools.partial(on_device, mesh.shape["tensor"]),
        mesh=mesh,
        in_specs=in_specs,
        out_specs=out_specs,
        check_vma=False,
    )
```

```python
import functools

import jax
import jax.numpy as jnp
from jax import lax
from jax.experimental import pallas as pl
from jax.experimental.pallas import tpu as pltpu
from jax.sharding import PartitionSpec as P

BLOCK = 256


def product_body(order_ref, hidden_ref, kept_weights, sent_weights, kept_ref, sent_ref):
    hidden = hidden_ref[...]
    sent_ref[0] = jnp.dot(
        hidden, sent_weights[...], preferred_element_type=jnp.float32
    ).astype(jnp.bfloat16)
    kept_ref[0] = jnp.dot(hidden, kept_weights[...], preferred_element_type=jnp.float32)


def product(hidden, down_matrix, order, width):
    rows, depth = hidden.shape
    half = order.shape[0] // 2
    block = min(BLOCK, width)
    blocks = width // block

    def weight_spec(offset):
        return pl.BlockSpec(
            (depth, block), lambda at, part, order: (0, order[offset + at] * blocks + part)
        )

    return pl.pallas_call(
        product_body,
        grid_spec=pltpu.PrefetchScalarGridSpec(
            num_scalar_prefetch=1,
            grid=(half, blocks),
            in_specs=[
                pl.BlockSpec((rows, depth), lambda at, part, order: (0, 0)),
                weight_spec(0),
                weight_spec(half),
            ],
            out_specs=[pl.BlockSpec((1, rows, block), lambda at, part, order: (at, 0, part))] * 2,
        ),
        out_shape=[
            jax.ShapeDtypeStruct((half, rows, width), jnp.float32),
            jax.ShapeDtypeStruct((half, rows, width), jnp.bfloat16),
        ],
        compiler_params=pltpu.CompilerParams(vmem_limit_bytes=48 * 1024 * 1024),
    )(order, hidden, down_matrix, down_matrix)


def swap(value, bit, total):
    return lax.ppermute(value, "tensor", [(place, place ^ bit) for place in range(total)])


def after(value, earlier):
    return lax.optimization_barrier((value, earlier))[0]


def shrink_partial(hidden, shrink_matrices, row_adapter_index):
    adapter_total = shrink_matrices.shape[0]
    every_adapter = jnp.einsum(
        "hq,gqu->hgu", hidden, shrink_matrices, preferred_element_type=jnp.float32
    )
    picked = row_adapter_index[:, None] == jnp.arange(adapter_total, dtype=jnp.int32)[None, :]
    return jnp.sum(jnp.where(picked[:, :, None], every_adapter, 0.0), axis=1)


def expand_partial(shrunk_rows, expand_matrices, segment_first_row, segment_length):
    rows_total = shrunk_rows.shape[0]
    adapter_total = expand_matrices.shape[0]
    rows = jnp.arange(rows_total, dtype=jnp.int32)
    inside = (rows[:, None] >= segment_first_row[None, :]) & (
        rows[:, None] < (segment_first_row + segment_length)[None, :]
    )
    spread = jnp.where(inside[:, :, None], shrunk_rows[:, None, :], jnp.zeros((), jnp.bfloat16))
    spread = spread.reshape(rows_total, adapter_total * shrunk_rows.shape[1])
    adapter_table = expand_matrices.reshape(
        adapter_total * expand_matrices.shape[1], expand_matrices.shape[2]
    )
    return jnp.dot(spread, adapter_table, preferred_element_type=jnp.float32)


def on_device(
    total,
    hidden,
    down_matrix,
    shrink_matrices,
    expand_matrices,
    row_adapter_index,
    segment_first_row,
    segment_length,
):
    me = lax.axis_index("tensor").astype(jnp.int32)
    width = down_matrix.shape[1] // total
    core, near = 1, 2
    units = total // 4

    kept, sent, ready = {}, {}, []
    for unit in reversed(range(units)):
        far = unit * 4
        order = jnp.array([far, far | near, far | core, far | near | core], dtype=jnp.int32) ^ me
        if len(ready) > 1:
            order = after(order, ready[-2])
        first, second = product(hidden, down_matrix, order, width)
        arrived = swap(second, core, total)
        kept[unit] = first[0] + arrived[0].astype(jnp.float32)
        sent[unit] = (first[1] + arrived[1].astype(jnp.float32)).astype(jnp.bfloat16)
        ready.append(sent[unit])

    late_hidden = after(hidden, ready[-2])
    shrunk = jnp.swapaxes(shrink_partial(late_hidden, shrink_matrices, row_adapter_index), 0, 1)
    for level in range(total.bit_length() - 1):
        shrunk = shrunk + swap(shrunk, 1 << level, total)
    shrunk_rows = jnp.swapaxes(shrunk, 0, 1).astype(jnp.bfloat16)
    adapter_output = expand_partial(shrunk_rows, expand_matrices, segment_first_row, segment_length)

    for unit in reversed(range(units)):
        kept[unit] = kept[unit] + swap(sent[unit], near, total).astype(jnp.float32)
    bit = 1
    while bit < units:
        for unit in reversed(range(0, units, 2 * bit)):
            moved = swap(kept[unit | bit].astype(jnp.bfloat16), 4 * bit, total)
            kept[unit] = kept[unit] + moved.astype(jnp.float32)
        bit *= 2
    return (kept[0] + adapter_output).astype(jnp.bfloat16)


def solution(mesh):
    in_specs = (
        P("groups", "tensor"),
        P("tensor", None),
        P(None, "tensor", None),
        P(None, None, "tensor"),
        P("groups"),
        P("groups"),
        P("groups"),
    )
    out_specs = P("groups", "tensor")
    return jax.shard_map(
        functools.partial(on_device, mesh.shape["tensor"]),
        mesh=mesh,
        in_specs=in_specs,
        out_specs=out_specs,
        check_vma=False,
    )
```

```python
import functools

import jax
import jax.numpy as jnp
from jax import lax
from jax.experimental import pallas as pl
from jax.experimental.pallas import tpu as pltpu
from jax.sharding import PartitionSpec as P

BLOCK = 256
DEEP = 256
WINDOW = 64
TOGETHER = 4
VMEM_LIMIT = 48 * 1024 * 1024


def deep_dot(left, right_ref, transposed=False):
    depth = left.shape[1]
    cut = depth // DEEP * DEEP
    total = None
    for first, last in ((0, cut), (cut, depth)):
        if first == last:
            continue
        right = right_ref[:, first:last] if transposed else right_ref[first:last, :]
        part = lax.dot_general(
            left[:, first:last],
            right,
            (((1,), (1 if transposed else 0,)), ((), ())),
            preferred_element_type=jnp.float32,
        )
        total = part if total is None else total + part
    return total


def product_body(order_ref, hidden_ref, weights_ref, result_ref):
    result_ref[0] = deep_dot(hidden_ref[...], weights_ref).astype(result_ref.dtype)


def product(hidden, down_matrix, order, width, dtype):
    rows, depth = hidden.shape
    targets = order.shape[0]
    block = min(BLOCK, width)
    blocks = width // block
    return pl.pallas_call(
        product_body,
        grid_spec=pltpu.PrefetchScalarGridSpec(
            num_scalar_prefetch=1,
            grid=(targets, blocks),
            in_specs=[
                pl.BlockSpec((rows, depth), lambda at, part, order: (0, 0)),
                pl.BlockSpec((depth, block), lambda at, part, order: (0, order[at] * blocks + part)),
            ],
            out_specs=pl.BlockSpec((1, rows, block), lambda at, part, order: (at, 0, part)),
        ),
        out_shape=jax.ShapeDtypeStruct((targets, rows, width), dtype),
        compiler_params=pltpu.CompilerParams(vmem_limit_bytes=VMEM_LIMIT),
        cost_estimate=pl.CostEstimate(flops=1, bytes_accessed=1, transcendentals=0),
    )(order, hidden, down_matrix)


def for_each_window(first_ref, length_ref, group, rows, body):
    window = min(WINDOW, rows)
    adapters = [group * TOGETHER + at for at in range(TOGETHER)]
    begins = [first_ref[adapter] for adapter in adapters]
    ends = [first_ref[adapter] + length_ref[adapter] for adapter in adapters]
    base = begins[0] // 16 * 16

    def step(at, carry):
        low = base + at * window
        start = pl.multiple_of(jnp.minimum(low, rows - window), 16)
        places = start + lax.broadcasted_iota(jnp.int32, (window, 1), 0)
        masks = [
            (places >= jnp.maximum(begin, low)) & (places < end) for begin, end in zip(begins, ends)
        ]
        body(pl.ds(start, window), masks)
        return carry

    lax.fori_loop(0, (ends[-1] - base + window - 1) // window, step, 0)


def shrink_body(first_ref, length_ref, hidden_ref, table_ref, packed_ref, total_ref):
    group = pl.program_id(0)
    rank = total_ref.shape[1]
    rows = total_ref.shape[0]

    @pl.when(group == 0)
    def _():
        total_ref[...] = jnp.zeros_like(total_ref)

    def body(window, masks):
        every = deep_dot(hidden_ref[window, :], table_ref, transposed=True)
        picked = total_ref[window, :]
        for at, mask in enumerate(masks):
            picked = picked + jnp.where(mask, every[:, at * rank:(at + 1) * rank], 0.0)
        total_ref[window, :] = picked

    for_each_window(first_ref, length_ref, group, rows, body)

    @pl.when(group == pl.num_programs(0) - 1)
    def _():
        packed_ref[:, :rank] = total_ref[:rows // 2, :]
        packed_ref[:, rank:] = total_ref[rows // 2:, :]


def shrink(hidden, shrink_matrices, segment_first_row, segment_length):
    rows, depth = hidden.shape
    adapters, _, rank = shrink_matrices.shape
    table = jnp.swapaxes(shrink_matrices, 1, 2).reshape(adapters * rank, depth)
    return pl.pallas_call(
        shrink_body,
        grid_spec=pltpu.PrefetchScalarGridSpec(
            num_scalar_prefetch=2,
            grid=(adapters // TOGETHER,),
            in_specs=[
                pl.BlockSpec((rows, depth), lambda group, *_: (0, 0)),
                pl.BlockSpec((TOGETHER * rank, depth), lambda group, *_: (group, 0)),
            ],
            out_specs=pl.BlockSpec((rows // 2, 2 * rank), lambda group, *_: (0, 0)),
            scratch_shapes=[pltpu.VMEM((rows, rank), jnp.float32)],
        ),
        out_shape=jax.ShapeDtypeStruct((rows // 2, 2 * rank), jnp.float32),
        compiler_params=pltpu.CompilerParams(vmem_limit_bytes=VMEM_LIMIT),
        cost_estimate=pl.CostEstimate(flops=1, bytes_accessed=1, transcendentals=0),
    )(segment_first_row, segment_length, hidden, table)


def expand_body(first_ref, length_ref, packed_ref, table_ref, result_ref, shrunk_ref):
    group = pl.program_id(0)
    rows, rank = shrunk_ref.shape

    @pl.when(group == 0)
    def _():
        shrunk_ref[:rows // 2, :] = packed_ref[:, :rank].astype(jnp.bfloat16)
        shrunk_ref[rows // 2:, :] = packed_ref[:, rank:].astype(jnp.bfloat16)
        result_ref[...] = jnp.zeros_like(result_ref)

    def body(window, masks):
        shrunk = shrunk_ref[window, :]
        spread = [jnp.where(mask, shrunk, jnp.zeros((), jnp.bfloat16)) for mask in masks]
        part = jnp.dot(
            jnp.concatenate(spread, axis=1), table_ref[...], preferred_element_type=jnp.float32
        )
        result_ref[window, :] = result_ref[window, :] + part

    for_each_window(first_ref, length_ref, group, rows, body)


def expand(packed, expand_matrices, segment_first_row, segment_length):
    rows = 2 * packed.shape[0]
    adapters, rank, width = expand_matrices.shape
    table = expand_matrices.reshape(adapters * rank, width)
    return pl.pallas_call(
        expand_body,
        grid_spec=pltpu.PrefetchScalarGridSpec(
            num_scalar_prefetch=2,
            grid=(adapters // TOGETHER,),
            in_specs=[
                pl.BlockSpec((rows // 2, 2 * rank), lambda group, *_: (0, 0)),
                pl.BlockSpec((TOGETHER * rank, width), lambda group, *_: (group, 0)),
            ],
            out_specs=pl.BlockSpec((rows, width), lambda group, *_: (0, 0)),
            scratch_shapes=[pltpu.VMEM((rows, rank), jnp.bfloat16)],
        ),
        out_shape=jax.ShapeDtypeStruct((rows, width), jnp.float32),
        compiler_params=pltpu.CompilerParams(vmem_limit_bytes=VMEM_LIMIT),
        cost_estimate=pl.CostEstimate(flops=1, bytes_accessed=1, transcendentals=0),
    )(segment_first_row, segment_length, packed, table)


def swap(value, bit, total):
    return lax.ppermute(value, "tensor", [(place, place ^ bit) for place in range(total)])


def after(value, earlier):
    return lax.optimization_barrier((value, earlier))[0]


def on_device(
    total,
    hidden,
    down_matrix,
    shrink_matrices,
    expand_matrices,
    row_adapter_index,
    segment_first_row,
    segment_length,
):
    me = lax.axis_index("tensor").astype(jnp.int32)
    width = down_matrix.shape[1] // total
    core, near = 1, 2
    units = total // 4

    kept, sent, packed, done = {}, {}, None, None
    for unit in reversed(range(units)):
        far = unit * 4
        away = jnp.array([far | core, far | near | core], dtype=jnp.int32) ^ me
        home = jnp.array([far, far | near], dtype=jnp.int32) ^ me
        if done is not None:
            away = after(away, done)
        second = product(hidden, down_matrix, away, width, jnp.bfloat16)
        first = product(hidden, down_matrix, after(home, second), width, jnp.float32)
        arrived = swap(second, core, total)
        kept[unit] = first[0] + arrived[0].astype(jnp.float32)
        sent[unit] = (first[1] + arrived[1].astype(jnp.float32)).astype(jnp.bfloat16)
        done = sent[unit]
        if packed is None:
            packed = shrink(
                hidden, shrink_matrices, after(segment_first_row, done), segment_length
            )
            done = packed

    levels = [1 << level for level in range(total.bit_length() - 1)]
    for bit in [core, *levels[2:], near]:
        packed = packed + swap(packed, bit, total)
    adapter_output = expand(packed, expand_matrices, segment_first_row, segment_length)

    for unit in reversed(range(units)):
        kept[unit] = kept[unit] + swap(sent[unit], near, total).astype(jnp.float32)
    bit = 1
    while bit < units:
        for unit in reversed(range(0, units, 2 * bit)):
            moved = swap(kept[unit | bit].astype(jnp.bfloat16), 4 * bit, total)
            kept[unit] = kept[unit] + moved.astype(jnp.float32)
        bit *= 2
    return (kept[0] + adapter_output).astype(jnp.bfloat16)


def solution(mesh):
    in_specs = (
        P("groups", "tensor"),
        P("tensor", None),
        P(None, "tensor", None),
        P(None, None, "tensor"),
        P("groups"),
        P("groups"),
        P("groups"),
    )
    out_specs = P("groups", "tensor")
    return jax.shard_map(
        functools.partial(on_device, mesh.shape["tensor"]),
        mesh=mesh,
        in_specs=in_specs,
        out_specs=out_specs,
        check_vma=False,
    )
```

```python
import functools

import jax
import jax.numpy as jnp
from jax import lax
from jax.experimental import pallas as pl
from jax.experimental.pallas import tpu as pltpu
from jax.sharding import PartitionSpec as P

BLOCK = 256
VMEM_LIMIT = 48 * 1024 * 1024
WINDOW = 128
TOGETHER = 4
FLOPS = 1_000_000


def product_body(targets_ref, hidden_ref, down_ref, *refs, sent, earlier):
    *result_refs, buffer, arrived = refs[earlier:]
    width = result_refs[0].shape[-1]
    block = buffer.shape[2]
    blocks = width // block
    targets = buffer.shape[0] // blocks
    copies = []
    for at in range(targets):
        for part in range(blocks):
            slot = at * blocks + part
            column = pl.multiple_of(targets_ref[at] * width + part * block, block)
            copies.append(
                pltpu.make_async_copy(
                    down_ref.at[:, pl.ds(column, block)], buffer.at[slot], arrived.at[slot]
                )
            )
            copies[-1].start()
    for at in range(targets):
        for part in range(blocks):
            slot = at * blocks + part
            copies[slot].wait()
            total = jnp.dot(hidden_ref[...], buffer[slot], preferred_element_type=jnp.float32)
            columns = slice(part * block, (part + 1) * block)
            if at < sent:
                result_refs[0][at, :, columns] = total.astype(jnp.bfloat16)
            else:
                result_refs[(1 if sent else 0) + at - sent][:, columns] = total


def product(hidden, down_matrix, sent, kept, width, earlier):
    rows, depth = hidden.shape
    block = min(BLOCK, width)
    slots = (len(sent) + len(kept)) * (width // block)
    vmem = pl.BlockSpec(memory_space=pltpu.VMEM)
    out_shape = [jax.ShapeDtypeStruct((rows, width), jnp.float32)] * len(kept)
    if sent:
        out_shape = [jax.ShapeDtypeStruct((len(sent), rows, width), jnp.bfloat16)] + out_shape
    results = pl.pallas_call(
        functools.partial(product_body, sent=len(sent), earlier=len(earlier)),
        in_specs=[pl.BlockSpec(memory_space=pltpu.SMEM), vmem]
        + [pl.BlockSpec(memory_space=pl.ANY)] * (1 + len(earlier)),
        out_specs=[vmem] * len(out_shape),
        out_shape=out_shape,
        scratch_shapes=[
            pltpu.VMEM((slots, depth, block), jnp.bfloat16),
            pltpu.SemaphoreType.DMA((slots,)),
        ],
        compiler_params=pltpu.CompilerParams(vmem_limit_bytes=VMEM_LIMIT),
        cost_estimate=pl.CostEstimate(flops=FLOPS, bytes_accessed=1024, transcendentals=0),
    )(jnp.stack(sent + kept), hidden, down_matrix, *earlier)
    return (results[0], list(results[1:])) if sent else (None, list(results))


def swap(value, bit, total):
    return lax.ppermute(value, "tensor", [(place, place ^ bit) for place in range(total)])


def for_each_window(first_ref, length_ref, group, rows, body):
    window = min(WINDOW, rows)
    adapters = [group * TOGETHER + at for at in range(TOGETHER)]
    begins = [first_ref[adapter] for adapter in adapters]
    ends = [first_ref[adapter] + length_ref[adapter] for adapter in adapters]
    base = begins[0] // 16 * 16

    def step(at, carry):
        low = base + at * window
        start = pl.multiple_of(jnp.minimum(low, rows - window), 16)
        places = start + lax.broadcasted_iota(jnp.int32, (window, 1), 0)
        masks = [
            (places >= jnp.maximum(begin, low)) & (places < end) for begin, end in zip(begins, ends)
        ]
        body(pl.ds(start, window), masks)
        return carry

    lax.fori_loop(0, (ends[-1] - base + window - 1) // window, step, 0)


def shrink_body(first_ref, length_ref, hidden_ref, table_ref, earlier_ref, packed_ref, total_ref):
    group = pl.program_id(0)
    rank = total_ref.shape[1]
    rows = total_ref.shape[0]

    @pl.when(group == 0)
    def _():
        total_ref[...] = jnp.zeros_like(total_ref)

    def body(window, masks):
        every = lax.dot_general(
            hidden_ref[window, :],
            table_ref[...],
            (((1,), (1,)), ((), ())),
            preferred_element_type=jnp.float32,
        )
        picked = total_ref[window, :]
        for at, mask in enumerate(masks):
            picked = picked + jnp.where(mask, every[:, at * rank:(at + 1) * rank], 0.0)
        total_ref[window, :] = picked

    for_each_window(first_ref, length_ref, group, rows, body)

    @pl.when(group == pl.num_programs(0) - 1)
    def _():
        packed_ref[:, :rank] = total_ref[:rows // 2, :]
        packed_ref[:, rank:] = total_ref[rows // 2:, :]


def shrink(hidden, shrink_matrices, segment_first_row, segment_length, earlier):
    rows, depth = hidden.shape
    adapters, _, rank = shrink_matrices.shape
    table = jnp.swapaxes(shrink_matrices, 1, 2).reshape(adapters * rank, depth)
    return pl.pallas_call(
        shrink_body,
        grid_spec=pltpu.PrefetchScalarGridSpec(
            num_scalar_prefetch=2,
            grid=(adapters // TOGETHER,),
            in_specs=[
                pl.BlockSpec((rows, depth), lambda group, *_: (0, 0)),
                pl.BlockSpec((TOGETHER * rank, depth), lambda group, *_: (group, 0)),
                pl.BlockSpec(memory_space=pl.ANY),
            ],
            out_specs=pl.BlockSpec((rows // 2, 2 * rank), lambda group, *_: (0, 0)),
            scratch_shapes=[pltpu.VMEM((rows, rank), jnp.float32)],
        ),
        out_shape=jax.ShapeDtypeStruct((rows // 2, 2 * rank), jnp.float32),
        compiler_params=pltpu.CompilerParams(vmem_limit_bytes=VMEM_LIMIT),
        cost_estimate=pl.CostEstimate(flops=FLOPS, bytes_accessed=1, transcendentals=0),
    )(segment_first_row, segment_length, hidden, table, earlier)


def expand_body(first_ref, length_ref, packed_ref, table_ref, result_ref, shrunk_ref):
    group = pl.program_id(0)
    rows, rank = shrunk_ref.shape

    @pl.when(group == 0)
    def _():
        shrunk_ref[:rows // 2, :] = packed_ref[:, :rank].astype(jnp.bfloat16)
        shrunk_ref[rows // 2:, :] = packed_ref[:, rank:].astype(jnp.bfloat16)
        result_ref[...] = jnp.zeros_like(result_ref)

    def body(window, masks):
        shrunk = shrunk_ref[window, :]
        spread = [jnp.where(mask, shrunk, jnp.zeros((), jnp.bfloat16)) for mask in masks]
        part = jnp.dot(
            jnp.concatenate(spread, axis=1), table_ref[...], preferred_element_type=jnp.float32
        )
        result_ref[window, :] = result_ref[window, :] + part

    for_each_window(first_ref, length_ref, group, rows, body)


def expand(packed, expand_matrices, segment_first_row, segment_length):
    rows = 2 * packed.shape[0]
    adapters, rank, width = expand_matrices.shape
    table = expand_matrices.reshape(adapters * rank, width)
    return pl.pallas_call(
        expand_body,
        grid_spec=pltpu.PrefetchScalarGridSpec(
            num_scalar_prefetch=2,
            grid=(adapters // TOGETHER,),
            in_specs=[
                pl.BlockSpec((rows // 2, 2 * rank), lambda group, *_: (0, 0)),
                pl.BlockSpec((TOGETHER * rank, width), lambda group, *_: (group, 0)),
            ],
            out_specs=pl.BlockSpec((rows, width), lambda group, *_: (0, 0)),
            scratch_shapes=[pltpu.VMEM((rows, rank), jnp.bfloat16)],
        ),
        out_shape=jax.ShapeDtypeStruct((rows, width), jnp.float32),
        compiler_params=pltpu.CompilerParams(vmem_limit_bytes=VMEM_LIMIT),
        cost_estimate=pl.CostEstimate(flops=FLOPS, bytes_accessed=1, transcendentals=0),
    )(segment_first_row, segment_length, packed, table)


def on_device(
    total,
    hidden,
    down_matrix,
    shrink_matrices,
    expand_matrices,
    row_adapter_index,
    segment_first_row,
    segment_length,
):
    me = lax.axis_index("tensor").astype(jnp.int32)
    width = down_matrix.shape[1] // total
    core, near = 1, 2
    units = total // 4

    def out_of(unit):
        return me ^ (unit * 4 | near)

    def home_of(unit):
        return me ^ (unit * 4)

    kept_out, kept_home, crossed, incoming = {}, {}, {}, {}

    def settle(unit, arrived):
        value = kept_home[unit] + arrived.astype(jnp.float32) + crossed[unit].astype(jnp.float32)
        for moved in incoming.pop(unit, []):
            value = value + moved.astype(jnp.float32)
        if not unit:
            return value
        bit = unit & -unit
        moving = value.astype(jnp.bfloat16)
        incoming.setdefault(unit ^ bit, []).append(swap(moving, 4 * bit, total))
        return moving

    top = units - 1
    values, _ = product(hidden, down_matrix, [out_of(top) ^ core], [], width, [])
    packed, ready = None, [values]
    steps = [near, *(4 << at for at in range(top.bit_length())), core]
    for unit in reversed(range(units)):
        arrived = swap(values, core, total)
        sent, kept = [], [out_of(unit)]
        if unit:
            sent.append(out_of(unit - 1) ^ core)
        sent.append(home_of(unit) ^ core)
        if unit < top:
            kept.append(home_of(unit + 1))
        if not unit:
            kept.append(home_of(0))
        values, results = product(hidden, down_matrix, sent, kept, width, ready)
        kept_out[unit] = results[0]
        if unit < top:
            kept_home[unit + 1] = results[1]
        if not unit:
            kept_home[0] = results[-1]
        if packed is not None and steps:
            moved, kept_out[unit] = lax.optimization_barrier(
                (swap(packed, steps.pop(0), total), kept_out[unit])
            )
            packed = packed + moved
        leaving = (kept_out[unit] + arrived[0].astype(jnp.float32)).astype(jnp.bfloat16)
        ready = [leaving]
        if unit < top:
            ready.append(settle(unit + 1, arrived[1]))
        crossed[unit] = swap(leaving, near, total)
        if packed is None:
            packed = shrink(
                hidden, shrink_matrices, segment_first_row, segment_length, leaving
            )
        ready.append(packed)
    kept = [settle(0, swap(values, core, total)[0])]

    for bit in steps:
        packed = packed + swap(packed, bit, total)
    adapter_output = expand(packed, expand_matrices, segment_first_row, segment_length)
    return (kept[0] + adapter_output).astype(jnp.bfloat16)


def solution(mesh):
    in_specs = (
        P("groups", "tensor"),
        P("tensor", None),
        P(None, "tensor", None),
        P(None, None, "tensor"),
        P("groups"),
        P("groups"),
        P("groups"),
    )
    out_specs = P("groups", "tensor")
    return jax.shard_map(
        functools.partial(on_device, mesh.shape["tensor"]),
        mesh=mesh,
        in_specs=in_specs,
        out_specs=out_specs,
        check_vma=False,
    )
```

```python
import functools

import jax
import jax.numpy as jnp
from jax import lax
from jax.experimental import pallas as pl
from jax.experimental.pallas import tpu as pltpu
from jax.sharding import PartitionSpec as P

BLOCK = 256
SLOTS = 3
PIECES = 2
VMEM_LIMIT = 40 * 1024 * 1024
WINDOW = 128
TOGETHER = 4
FLOPS = 1_000_000


def product_body(targets_ref, hidden_ref, down_ref, *refs, sent, earlier):
    *result_refs, buffer, arrived = refs[earlier:]
    width = result_refs[0].shape[-1]
    block = buffer.shape[2]
    blocks = width // block
    steps = [(at, part) for at in range(targets_ref.shape[0]) for part in range(blocks)]
    slots, pieces = arrived.shape
    deep = buffer.shape[1] // pieces

    def copies(step):
        at, part = steps[step]
        column = pl.multiple_of(targets_ref[at] * width + part * block, block)
        for piece in range(pieces):
            rows = pl.ds(piece * deep, deep)
            yield pltpu.make_async_copy(
                down_ref.at[rows, pl.ds(column, block)],
                buffer.at[step % slots, rows],
                arrived.at[step % slots, piece],
            )

    for step in range(min(slots - 1, len(steps))):
        for copy in copies(step):
            copy.start()
    for step, (at, part) in enumerate(steps):
        if step + slots - 1 < len(steps):
            for copy in copies(step + slots - 1):
                copy.start()
        for copy in copies(step):
            copy.wait()
        total = jnp.dot(
            hidden_ref[...], buffer[step % slots], preferred_element_type=jnp.float32
        )
        columns = slice(part * block, (part + 1) * block)
        if at < sent:
            result_refs[0][at, :, columns] = total.astype(jnp.bfloat16)
        else:
            result_refs[(1 if sent else 0) + at - sent][:, columns] = total


def product(hidden, down_matrix, sent, kept, width, earlier):
    rows, depth = hidden.shape
    block = min(BLOCK, width)
    pieces = PIECES if depth % (16 * PIECES) == 0 else 1
    vmem = pl.BlockSpec(memory_space=pltpu.VMEM)
    out_shape = [jax.ShapeDtypeStruct((rows, width), jnp.float32)] * len(kept)
    if sent:
        out_shape = [jax.ShapeDtypeStruct((len(sent), rows, width), jnp.bfloat16)] + out_shape
    results = pl.pallas_call(
        functools.partial(product_body, sent=len(sent), earlier=len(earlier)),
        in_specs=[
            pl.BlockSpec(memory_space=pltpu.SMEM), vmem, pl.BlockSpec(memory_space=pltpu.HBM)
        ]
        + [pl.BlockSpec(memory_space=pl.ANY)] * len(earlier),
        out_specs=[vmem] * len(out_shape),
        out_shape=out_shape,
        scratch_shapes=[
            pltpu.VMEM((SLOTS, depth, block), jnp.bfloat16),
            pltpu.SemaphoreType.DMA((SLOTS, pieces)),
        ],
        compiler_params=pltpu.CompilerParams(vmem_limit_bytes=VMEM_LIMIT),
        cost_estimate=pl.CostEstimate(flops=FLOPS, bytes_accessed=1024, transcendentals=0),
    )(jnp.stack(sent + kept), hidden, down_matrix, *earlier)
    return (results[0], list(results[1:])) if sent else (None, list(results))


def swap(value, bit, total):
    return lax.ppermute(value, "tensor", [(place, place ^ bit) for place in range(total)])


def for_each_window(first_ref, length_ref, group, rows, body):
    window = min(WINDOW, rows)
    adapters = [group * TOGETHER + at for at in range(TOGETHER)]
    begins = [first_ref[adapter] for adapter in adapters]
    ends = [first_ref[adapter] + length_ref[adapter] for adapter in adapters]
    base = begins[0] // 16 * 16

    def step(at, carry):
        low = base + at * window
        start = pl.multiple_of(jnp.minimum(low, rows - window), 16)
        places = start + lax.broadcasted_iota(jnp.int32, (window, 1), 0)
        masks = [
            (places >= jnp.maximum(begin, low)) & (places < end) for begin, end in zip(begins, ends)
        ]
        body(pl.ds(start, window), masks)
        return carry

    lax.fori_loop(0, (ends[-1] - base + window - 1) // window, step, 0)


def shrink(hidden, shrink_matrices, row_adapter_index):
    adapters = shrink_matrices.shape[0]
    every_adapter = jnp.einsum(
        "hq,gqu->hgu", hidden, shrink_matrices, preferred_element_type=jnp.float32
    )
    picked = row_adapter_index[:, None] == jnp.arange(adapters, dtype=jnp.int32)[None, :]
    partial = jnp.sum(jnp.where(picked[:, :, None], every_adapter, 0.0), axis=1)
    half = hidden.shape[0] // 2
    return jnp.concatenate([partial[:half], partial[half:]], axis=1)


def expand_body(first_ref, length_ref, packed_ref, table_ref, result_ref, shrunk_ref):
    group = pl.program_id(0)
    rows, rank = shrunk_ref.shape

    @pl.when(group == 0)
    def _():
        shrunk_ref[:rows // 2, :] = packed_ref[:, :rank].astype(jnp.bfloat16)
        shrunk_ref[rows // 2:, :] = packed_ref[:, rank:].astype(jnp.bfloat16)
        result_ref[...] = jnp.zeros_like(result_ref)

    def body(window, masks):
        shrunk = shrunk_ref[window, :]
        spread = [jnp.where(mask, shrunk, jnp.zeros((), jnp.bfloat16)) for mask in masks]
        part = jnp.dot(
            jnp.concatenate(spread, axis=1), table_ref[...], preferred_element_type=jnp.float32
        )
        result_ref[window, :] = result_ref[window, :] + part

    for_each_window(first_ref, length_ref, group, rows, body)


def expand(packed, expand_matrices, segment_first_row, segment_length):
    rows = 2 * packed.shape[0]
    adapters, rank, width = expand_matrices.shape
    table = expand_matrices.reshape(adapters * rank, width)
    return pl.pallas_call(
        expand_body,
        grid_spec=pltpu.PrefetchScalarGridSpec(
            num_scalar_prefetch=2,
            grid=(adapters // TOGETHER,),
            in_specs=[
                pl.BlockSpec((rows // 2, 2 * rank), lambda group, *_: (0, 0)),
                pl.BlockSpec((TOGETHER * rank, width), lambda group, *_: (group, 0)),
            ],
            out_specs=pl.BlockSpec((rows, width), lambda group, *_: (0, 0)),
            scratch_shapes=[pltpu.VMEM((rows, rank), jnp.bfloat16)],
        ),
        out_shape=jax.ShapeDtypeStruct((rows, width), jnp.float32),
        compiler_params=pltpu.CompilerParams(vmem_limit_bytes=VMEM_LIMIT),
        cost_estimate=pl.CostEstimate(flops=FLOPS, bytes_accessed=1, transcendentals=0),
    )(segment_first_row, segment_length, packed, table)


def on_device(
    total,
    hidden,
    down_matrix,
    shrink_matrices,
    expand_matrices,
    row_adapter_index,
    segment_first_row,
    segment_length,
):
    me = lax.axis_index("tensor").astype(jnp.int32)
    width = down_matrix.shape[1] // total
    core, near = 1, 2
    units = total // 4

    def out_of(unit):
        return me ^ (unit * 4 | near)

    def home_of(unit):
        return me ^ (unit * 4)

    kept_out, kept_home, crossed, incoming = {}, {}, {}, {}

    def settle(unit, arrived):
        value = kept_home[unit] + arrived.astype(jnp.float32) + crossed[unit].astype(jnp.float32)
        for moved in incoming.pop(unit, []):
            value = value + moved.astype(jnp.float32)
        if not unit:
            return value
        bit = unit & -unit
        moving = value.astype(jnp.bfloat16)
        incoming.setdefault(unit ^ bit, []).append(swap(moving, 4 * bit, total))
        return moving

    top = units - 1
    values, _ = product(hidden, down_matrix, [out_of(top) ^ core], [], width, [])
    packed, ready = None, [values]
    steps = [*(4 << at for at in reversed(range(top.bit_length()))), near, core]
    for unit in reversed(range(units)):
        arrived = swap(values, core, total)
        sent, kept = [], [out_of(unit)]
        if unit:
            sent.append(out_of(unit - 1) ^ core)
        sent.append(home_of(unit) ^ core)
        if unit < top:
            kept.append(home_of(unit + 1))
        if not unit:
            kept.append(home_of(0))
        values, results = product(hidden, down_matrix, sent, kept, width, ready)
        kept_out[unit] = results[0]
        if unit < top:
            kept_home[unit + 1] = results[1]
        if not unit:
            kept_home[0] = results[-1]
        if packed is not None and steps:
            moved, kept_out[unit] = lax.optimization_barrier(
                (swap(packed, steps.pop(0), total), kept_out[unit])
            )
            packed = packed + moved.astype(jnp.float32)
        leaving = (kept_out[unit] + arrived[0].astype(jnp.float32)).astype(jnp.bfloat16)
        ready = [leaving]
        if unit < top:
            ready.append(settle(unit + 1, arrived[1]))
        if packed is None:
            late, leaving = lax.optimization_barrier((hidden, leaving))
            packed = shrink(late, shrink_matrices, row_adapter_index)
        crossed[unit] = swap(leaving, near, total)
        ready.append(packed)
    kept = [settle(0, swap(values, core, total)[0])]

    for bit in steps:
        packed = packed + swap(packed, bit, total)
    adapter_output = expand(packed, expand_matrices, segment_first_row, segment_length)
    return (kept[0] + adapter_output).astype(jnp.bfloat16)


def solution(mesh):
    in_specs = (
        P("groups", "tensor"),
        P("tensor", None),
        P(None, "tensor", None),
        P(None, None, "tensor"),
        P("groups"),
        P("groups"),
        P("groups"),
    )
    out_specs = P("groups", "tensor")
    return jax.shard_map(
        functools.partial(on_device, mesh.shape["tensor"]),
        mesh=mesh,
        in_specs=in_specs,
        out_specs=out_specs,
        check_vma=False,
    )
```

```python
import functools

import jax
import jax.numpy as jnp
from jax import lax
from jax.experimental import pallas as pl
from jax.experimental.pallas import tpu as pltpu
from jax.sharding import PartitionSpec as P

VMEM_LIMIT = 39 * 1024 * 1024
WINDOW = 128
TOGETHER = 4
FLOPS = 1_000_000


def product_body(targets_ref, hidden_ref, down_ref, *refs, sent, kept, earlier):
    *result_refs, buffer, arrived = refs[earlier:]
    width = buffer.shape[2]

    def copy(at):
        column = pl.multiple_of(targets_ref[at] * width, width)
        return pltpu.make_async_copy(
            down_ref.at[:, pl.ds(column, width)], buffer.at[at % 2], arrived.at[at % 2]
        )

    copy(0).start()

    def step(at, carry):
        @pl.when(at + 1 < sent + kept)
        def _():
            copy(at + 1).start()

        copy(at).wait()
        total = jnp.dot(hidden_ref[...], buffer[at % 2], preferred_element_type=jnp.float32)
        if sent:

            @pl.when(at < sent)
            def _():
                result_refs[0][jnp.minimum(at, sent - 1)] = total.astype(jnp.bfloat16)

        if kept:

            @pl.when(at >= sent)
            def _():
                result_refs[-1][jnp.maximum(at - sent, 0)] = total

        return carry

    lax.fori_loop(0, sent + kept, step, 0)


def product(hidden, down_matrix, sent, kept, width, earlier):
    rows, depth = hidden.shape
    vmem = pl.BlockSpec(memory_space=pltpu.VMEM)
    out_shape = []
    if sent:
        out_shape.append(jax.ShapeDtypeStruct((len(sent), rows, width), jnp.bfloat16))
    if kept:
        out_shape.append(jax.ShapeDtypeStruct((len(kept), rows, width), jnp.float32))
    results = pl.pallas_call(
        functools.partial(
            product_body, sent=len(sent), kept=len(kept), earlier=len(earlier)
        ),
        in_specs=[
            pl.BlockSpec(memory_space=pltpu.SMEM), vmem, pl.BlockSpec(memory_space=pltpu.HBM)
        ]
        + [pl.BlockSpec(memory_space=pl.ANY)] * len(earlier),
        out_specs=[vmem] * len(out_shape),
        out_shape=out_shape,
        scratch_shapes=[
            pltpu.VMEM((2, depth, width), jnp.bfloat16),
            pltpu.SemaphoreType.DMA((2,)),
        ],
        compiler_params=pltpu.CompilerParams(vmem_limit_bytes=VMEM_LIMIT),
        cost_estimate=pl.CostEstimate(flops=FLOPS, bytes_accessed=1024, transcendentals=0),
    )(jnp.stack(sent + kept), hidden, down_matrix, *earlier)
    return (results[0] if sent else None), (results[-1] if kept else None)


def swap(value, bit, total):
    return lax.ppermute(value, "tensor", [(place, place ^ bit) for place in range(total)])


def for_each_window(first_ref, length_ref, group, rows, body):
    window = min(WINDOW, rows)
    adapters = [group * TOGETHER + at for at in range(TOGETHER)]
    begins = [first_ref[adapter] for adapter in adapters]
    ends = [first_ref[adapter] + length_ref[adapter] for adapter in adapters]
    base = begins[0] // 16 * 16

    def step(at, carry):
        low = base + at * window
        start = pl.multiple_of(jnp.minimum(low, rows - window), 16)
        places = start + lax.broadcasted_iota(jnp.int32, (window, 1), 0)
        masks = [
            (places >= jnp.maximum(begin, low)) & (places < end) for begin, end in zip(begins, ends)
        ]
        body(pl.ds(start, window), masks)
        return carry

    lax.fori_loop(0, (ends[-1] - base + window - 1) // window, step, 0)


def shrink(hidden, shrink_matrices, row_adapter_index):
    adapters = shrink_matrices.shape[0]
    every_adapter = jnp.einsum(
        "hq,gqu->hgu", hidden, shrink_matrices, preferred_element_type=jnp.float32
    )
    picked = row_adapter_index[:, None] == jnp.arange(adapters, dtype=jnp.int32)[None, :]
    partial = jnp.sum(jnp.where(picked[:, :, None], every_adapter, 0.0), axis=1)
    half = hidden.shape[0] // 2
    return jnp.concatenate([partial[:half], partial[half:]], axis=1)


def expand_body(first_ref, length_ref, packed_ref, table_ref, result_ref, shrunk_ref):
    group = pl.program_id(0)
    rows, rank = shrunk_ref.shape

    @pl.when(group == 0)
    def _():
        shrunk_ref[:rows // 2, :] = packed_ref[:, :rank].astype(jnp.bfloat16)
        shrunk_ref[rows // 2:, :] = packed_ref[:, rank:].astype(jnp.bfloat16)
        result_ref[...] = jnp.zeros_like(result_ref)

    def body(window, masks):
        shrunk = shrunk_ref[window, :]
        spread = [jnp.where(mask, shrunk, jnp.zeros((), jnp.bfloat16)) for mask in masks]
        part = jnp.dot(
            jnp.concatenate(spread, axis=1), table_ref[...], preferred_element_type=jnp.float32
        )
        result_ref[window, :] = result_ref[window, :] + part

    for_each_window(first_ref, length_ref, group, rows, body)


def expand(packed, expand_matrices, segment_first_row, segment_length):
    rows = 2 * packed.shape[0]
    adapters, rank, width = expand_matrices.shape
    table = expand_matrices.reshape(adapters * rank, width)
    return pl.pallas_call(
        expand_body,
        grid_spec=pltpu.PrefetchScalarGridSpec(
            num_scalar_prefetch=2,
            grid=(adapters // TOGETHER,),
            in_specs=[
                pl.BlockSpec((rows // 2, 2 * rank), lambda group, *_: (0, 0)),
                pl.BlockSpec((TOGETHER * rank, width), lambda group, *_: (group, 0)),
            ],
            out_specs=pl.BlockSpec((rows, width), lambda group, *_: (0, 0)),
            scratch_shapes=[pltpu.VMEM((rows, rank), jnp.bfloat16)],
        ),
        out_shape=jax.ShapeDtypeStruct((rows, width), jnp.float32),
        compiler_params=pltpu.CompilerParams(vmem_limit_bytes=VMEM_LIMIT),
        cost_estimate=pl.CostEstimate(flops=FLOPS, bytes_accessed=1, transcendentals=0),
    )(segment_first_row, segment_length, packed, table)


def on_device(
    total,
    hidden,
    down_matrix,
    shrink_matrices,
    expand_matrices,
    row_adapter_index,
    segment_first_row,
    segment_length,
):
    me = lax.axis_index("tensor").astype(jnp.int32)
    width = down_matrix.shape[1] // total
    core, near = 1, 2
    units = total // 4

    def out_of(unit):
        return me ^ (unit * 4 | near)

    def home_of(unit):
        return me ^ (unit * 4)

    kept_out, kept_home, crossed, incoming = {}, {}, {}, {}

    def settle(unit, arrived):
        value = kept_home[unit] + arrived.astype(jnp.float32) + crossed[unit].astype(jnp.float32)
        for moved in incoming.pop(unit, []):
            value = value + moved.astype(jnp.float32)
        if not unit:
            return value
        bit = unit & -unit
        moving = value.astype(jnp.bfloat16)
        incoming.setdefault(unit ^ bit, []).append(swap(moving, 4 * bit, total))
        return moving

    top = units - 1
    values, _ = product(hidden, down_matrix, [out_of(top) ^ core], [], width, [])
    packed, ready = None, [values]
    steps = [*(4 << at for at in reversed(range(top.bit_length()))), near, core]
    for unit in reversed(range(units)):
        arrived = swap(values, core, total)
        sent, kept = [], [out_of(unit)]
        if unit:
            sent.append(out_of(unit - 1) ^ core)
        sent.append(home_of(unit) ^ core)
        if unit < top:
            kept.append(home_of(unit + 1))
        if not unit:
            kept.append(home_of(0))
        values, results = product(hidden, down_matrix, sent, kept, width, ready)
        kept_out[unit] = results[0]
        if unit < top:
            kept_home[unit + 1] = results[1]
        if not unit:
            kept_home[0] = results[-1]
        if packed is not None and steps:
            moved, kept_out[unit] = lax.optimization_barrier(
                (swap(packed, steps.pop(0), total), kept_out[unit])
            )
            packed = packed + moved.astype(jnp.float32)
        leaving = (kept_out[unit] + arrived[0].astype(jnp.float32)).astype(jnp.bfloat16)
        ready = [leaving]
        if unit < top:
            ready.append(settle(unit + 1, arrived[1]))
        if packed is None:
            late, leaving = lax.optimization_barrier((hidden, leaving))
            packed = shrink(late, shrink_matrices, row_adapter_index)
        crossed[unit] = swap(leaving, near, total)
        ready.append(packed)
    kept = [settle(0, swap(values, core, total)[0])]

    for bit in steps:
        packed = packed + swap(packed, bit, total)
    adapter_output = expand(packed, expand_matrices, segment_first_row, segment_length)
    return (kept[0] + adapter_output).astype(jnp.bfloat16)


def solution(mesh):
    in_specs = (
        P("groups", "tensor"),
        P("tensor", None),
        P(None, "tensor", None),
        P(None, None, "tensor"),
        P("groups"),
        P("groups"),
        P("groups"),
    )
    out_specs = P("groups", "tensor")
    return jax.shard_map(
        functools.partial(on_device, mesh.shape["tensor"]),
        mesh=mesh,
        in_specs=in_specs,
        out_specs=out_specs,
        check_vma=False,
    )
```

```python
import functools

import jax
import jax.numpy as jnp
from jax import lax
from jax.experimental import pallas as pl
from jax.experimental.pallas import tpu as pltpu
from jax.sharding import PartitionSpec as P

PIECES = 4
VMEM_LIMIT = 39 * 1024 * 1024
WINDOW = 128
TOGETHER = 4
FLOPS = 10_000_000_000


def product_body(targets_ref, hidden_ref, down_ref, *refs, sent, kept, earlier):
    *result_refs, buffer, arrived = refs[earlier:]
    width = buffer.shape[2]

    pieces = arrived.shape[1]
    deep = buffer.shape[1] // pieces

    def copies(at):
        column = pl.multiple_of(targets_ref[at] * width, width)
        for piece in range(pieces):
            rows = pl.ds(piece * deep, deep)
            yield pltpu.make_async_copy(
                down_ref.at[rows, pl.ds(column, width)],
                buffer.at[at % 2, rows],
                arrived.at[at % 2, piece],
            )

    for copy in copies(0):
        copy.start()

    def step(at, carry):
        @pl.when(at + 1 < sent + kept)
        def _():
            for copy in copies(at + 1):
                copy.start()

        for copy in copies(at):
            copy.wait()
        total = jnp.dot(hidden_ref[...], buffer[at % 2], preferred_element_type=jnp.float32)
        if sent:

            @pl.when(at < sent)
            def _():
                result_refs[0][jnp.minimum(at, sent - 1)] = total.astype(jnp.bfloat16)

        if kept:

            @pl.when(at >= sent)
            def _():
                result_refs[-1][jnp.maximum(at - sent, 0)] = total

        return carry

    lax.fori_loop(0, sent + kept, step, 0)


def product(hidden, down_matrix, sent, kept, width, earlier):
    rows, depth = hidden.shape
    pieces = PIECES if depth % (16 * PIECES) == 0 else 1
    vmem = pl.BlockSpec(memory_space=pltpu.VMEM)
    out_shape = []
    if sent:
        out_shape.append(jax.ShapeDtypeStruct((len(sent), rows, width), jnp.bfloat16))
    if kept:
        out_shape.append(jax.ShapeDtypeStruct((len(kept), rows, width), jnp.float32))
    results = pl.pallas_call(
        functools.partial(
            product_body, sent=len(sent), kept=len(kept), earlier=len(earlier)
        ),
        in_specs=[
            pl.BlockSpec(memory_space=pltpu.SMEM), vmem, pl.BlockSpec(memory_space=pltpu.HBM)
        ]
        + [pl.BlockSpec(memory_space=pl.ANY)] * len(earlier),
        out_specs=[vmem] * len(out_shape),
        out_shape=out_shape,
        scratch_shapes=[
            pltpu.VMEM((2, depth, width), jnp.bfloat16),
            pltpu.SemaphoreType.DMA((2, pieces)),
        ],
        compiler_params=pltpu.CompilerParams(vmem_limit_bytes=VMEM_LIMIT),
        cost_estimate=pl.CostEstimate(flops=FLOPS, bytes_accessed=1024, transcendentals=0),
    )(jnp.stack(sent + kept), hidden, down_matrix, *earlier)
    return (results[0] if sent else None), (results[-1] if kept else None)


def swap(value, bit, total):
    return lax.ppermute(value, "tensor", [(place, place ^ bit) for place in range(total)])


def for_each_window(first_ref, length_ref, group, rows, body):
    window = min(WINDOW, rows)
    adapters = [group * TOGETHER + at for at in range(TOGETHER)]
    begins = [first_ref[adapter] for adapter in adapters]
    ends = [first_ref[adapter] + length_ref[adapter] for adapter in adapters]
    base = begins[0] // 16 * 16

    def step(at, carry):
        low = base + at * window
        start = pl.multiple_of(jnp.minimum(low, rows - window), 16)
        places = start + lax.broadcasted_iota(jnp.int32, (window, 1), 0)
        masks = [
            (places >= jnp.maximum(begin, low)) & (places < end) for begin, end in zip(begins, ends)
        ]
        body(pl.ds(start, window), masks)
        return carry

    lax.fori_loop(0, (ends[-1] - base + window - 1) // window, step, 0)


def shrink(hidden, shrink_matrices, row_adapter_index):
    adapters = shrink_matrices.shape[0]
    every_adapter = jnp.einsum(
        "hq,gqu->hgu", hidden, shrink_matrices, preferred_element_type=jnp.float32
    )
    picked = row_adapter_index[:, None] == jnp.arange(adapters, dtype=jnp.int32)[None, :]
    partial = jnp.sum(jnp.where(picked[:, :, None], every_adapter, 0.0), axis=1)
    half = hidden.shape[0] // 2
    return jnp.concatenate([partial[:half], partial[half:]], axis=1)


def expand_body(first_ref, length_ref, packed_ref, table_ref, result_ref, shrunk_ref):
    group = pl.program_id(0)
    rows, rank = shrunk_ref.shape

    @pl.when(group == 0)
    def _():
        shrunk_ref[:rows // 2, :] = packed_ref[:, :rank].astype(jnp.bfloat16)
        shrunk_ref[rows // 2:, :] = packed_ref[:, rank:].astype(jnp.bfloat16)
        result_ref[...] = jnp.zeros_like(result_ref)

    def body(window, masks):
        shrunk = shrunk_ref[window, :]
        spread = [jnp.where(mask, shrunk, jnp.zeros((), jnp.bfloat16)) for mask in masks]
        part = jnp.dot(
            jnp.concatenate(spread, axis=1), table_ref[...], preferred_element_type=jnp.float32
        )
        result_ref[window, :] = result_ref[window, :] + part

    for_each_window(first_ref, length_ref, group, rows, body)


def expand(packed, expand_matrices, segment_first_row, segment_length):
    rows = 2 * packed.shape[0]
    adapters, rank, width = expand_matrices.shape
    table = expand_matrices.reshape(adapters * rank, width)
    return pl.pallas_call(
        expand_body,
        grid_spec=pltpu.PrefetchScalarGridSpec(
            num_scalar_prefetch=2,
            grid=(adapters // TOGETHER,),
            in_specs=[
                pl.BlockSpec((rows // 2, 2 * rank), lambda group, *_: (0, 0)),
                pl.BlockSpec((TOGETHER * rank, width), lambda group, *_: (group, 0)),
            ],
            out_specs=pl.BlockSpec((rows, width), lambda group, *_: (0, 0)),
            scratch_shapes=[pltpu.VMEM((rows, rank), jnp.bfloat16)],
        ),
        out_shape=jax.ShapeDtypeStruct((rows, width), jnp.float32),
        compiler_params=pltpu.CompilerParams(vmem_limit_bytes=VMEM_LIMIT),
        cost_estimate=pl.CostEstimate(flops=FLOPS, bytes_accessed=1, transcendentals=0),
    )(segment_first_row, segment_length, packed, table)


def on_device(
    total,
    hidden,
    down_matrix,
    shrink_matrices,
    expand_matrices,
    row_adapter_index,
    segment_first_row,
    segment_length,
):
    me = lax.axis_index("tensor").astype(jnp.int32)
    width = down_matrix.shape[1] // total
    core, near = 1, 2
    units = total // 4

    def out_of(unit):
        return me ^ (unit * 4 | near)

    def home_of(unit):
        return me ^ (unit * 4)

    kept_home, crossed, incoming = {}, {}, {}

    def settle(unit, arrived):
        value = kept_home[unit] + arrived.astype(jnp.float32) + crossed[unit].astype(jnp.float32)
        for moved in incoming.pop(unit, []):
            value = value + moved.astype(jnp.float32)
        return value.astype(jnp.bfloat16) if unit else value

    def send_on(unit, moving):
        bit = unit & -unit
        incoming.setdefault(unit ^ bit, []).append(swap(moving, 4 * bit, total))
        return moving

    top = units - 1
    packed = shrink(hidden, shrink_matrices, row_adapter_index)
    steps = [near, *(4 << at for at in reversed(range(top.bit_length()))), core]

    def gather(value):
        nonlocal packed
        if steps:
            moved, value = lax.optimization_barrier((swap(packed, steps.pop(0), total), value))
            packed = packed + moved
        return value

    values, _ = product(hidden, down_matrix, [out_of(top) ^ core], [], width, [packed])
    values = gather(values)
    ready = [values]
    for unit in reversed(range(units)):
        arrived = swap(values, core, total)
        sent, kept = [], [out_of(unit)]
        if unit:
            sent.append(out_of(unit - 1) ^ core)
        sent.append(home_of(unit) ^ core)
        if unit < top:
            kept.append(home_of(unit + 1))
        if not unit:
            kept.append(home_of(0))
        values, results = product(hidden, down_matrix, sent, kept, width, ready + [packed])
        results = gather(results)
        if unit < top:
            kept_home[unit + 1] = results[1]
        if not unit:
            kept_home[0] = results[-1]
        ready = []
        if unit < top:
            moving, arrived = lax.optimization_barrier((settle(unit + 1, arrived[1]), arrived))
            ready.append(send_on(unit + 1, moving))
        leaving = (results[0] + arrived[0].astype(jnp.float32)).astype(jnp.bfloat16)
        ready.append(leaving)
        crossed[unit] = swap(leaving, near, total)
    kept = [settle(0, swap(values, core, total)[0])]

    for bit in steps:
        packed = packed + swap(packed, bit, total)
    adapter_output = expand(packed, expand_matrices, segment_first_row, segment_length)
    return (kept[0] + adapter_output).astype(jnp.bfloat16)


def solution(mesh):
    in_specs = (
        P("groups", "tensor"),
        P("tensor", None),
        P(None, "tensor", None),
        P(None, None, "tensor"),
        P("groups"),
        P("groups"),
        P("groups"),
    )
    out_specs = P("groups", "tensor")
    return jax.shard_map(
        functools.partial(on_device, mesh.shape["tensor"]),
        mesh=mesh,
        in_specs=in_specs,
        out_specs=out_specs,
        check_vma=False,
    )
```

```python
import functools

import jax
import jax.numpy as jnp
from jax import lax
from jax.experimental import pallas as pl
from jax.experimental.pallas import tpu as pltpu
from jax.sharding import PartitionSpec as P

PIECES = 4
VMEM_LIMIT = 39 * 1024 * 1024
WINDOW = 128
TOGETHER = 4
FLOPS = 10_000_000_000
EXPAND_FLOPS = 1_000_000


def product_body(targets_ref, hidden_ref, down_ref, *refs, sent, kept, earlier):
    *result_refs, buffer, arrived = refs[earlier:]
    width = buffer.shape[2]

    pieces = arrived.shape[1]
    deep = buffer.shape[1] // pieces

    def copies(at):
        column = pl.multiple_of(targets_ref[at] * width, width)
        for piece in range(pieces):
            rows = pl.ds(piece * deep, deep)
            yield pltpu.make_async_copy(
                down_ref.at[rows, pl.ds(column, width)],
                buffer.at[at % 2, rows],
                arrived.at[at % 2, piece],
            )

    for copy in copies(0):
        copy.start()

    def step(at, carry):
        @pl.when(at + 1 < sent + kept)
        def _():
            for copy in copies(at + 1):
                copy.start()

        for copy in copies(at):
            copy.wait()
        total = jnp.dot(hidden_ref[...], buffer[at % 2], preferred_element_type=jnp.float32)
        if sent:

            @pl.when(at < sent)
            def _():
                result_refs[0][jnp.minimum(at, sent - 1)] = total.astype(jnp.bfloat16)

        if kept:

            @pl.when(at >= sent)
            def _():
                result_refs[-1][jnp.maximum(at - sent, 0)] = total

        return carry

    lax.fori_loop(0, sent + kept, step, 0)


def product(hidden, down_matrix, sent, kept, width, earlier):
    rows, depth = hidden.shape
    pieces = PIECES if depth % (16 * PIECES) == 0 else 1
    vmem = pl.BlockSpec(memory_space=pltpu.VMEM)
    out_shape = []
    if sent:
        out_shape.append(jax.ShapeDtypeStruct((len(sent), rows, width), jnp.bfloat16))
    if kept:
        out_shape.append(jax.ShapeDtypeStruct((len(kept), rows, width), jnp.float32))
    results = pl.pallas_call(
        functools.partial(
            product_body, sent=len(sent), kept=len(kept), earlier=len(earlier)
        ),
        in_specs=[
            pl.BlockSpec(memory_space=pltpu.SMEM), vmem, pl.BlockSpec(memory_space=pltpu.HBM)
        ]
        + [pl.BlockSpec(memory_space=pl.ANY)] * len(earlier),
        out_specs=[vmem] * len(out_shape),
        out_shape=out_shape,
        scratch_shapes=[
            pltpu.VMEM((2, depth, width), jnp.bfloat16),
            pltpu.SemaphoreType.DMA((2, pieces)),
        ],
        compiler_params=pltpu.CompilerParams(vmem_limit_bytes=VMEM_LIMIT),
        cost_estimate=pl.CostEstimate(flops=FLOPS, bytes_accessed=1024, transcendentals=0),
    )(jnp.stack(sent + kept), hidden, down_matrix, *earlier)
    return (results[0] if sent else None), (results[-1] if kept else None)


def swap(value, bit, total):
    return lax.ppermute(value, "tensor", [(place, place ^ bit) for place in range(total)])


def attach(value, packed):
    high = packed.astype(jnp.bfloat16)
    low = (packed - high.astype(jnp.float32)).astype(jnp.bfloat16)
    both = jnp.concatenate([high, low])
    pieces = value.shape[1] // both.shape[1]
    return jnp.concatenate([value, jnp.concatenate(jnp.split(both, pieces), axis=1)])


def detach(value, packed):
    rows, columns = packed.shape
    pieces = value.shape[1] // columns
    below = 2 * rows // pieces
    above = value.shape[0] - below
    both = jnp.concatenate(jnp.split(value[above:], pieces, axis=1)).astype(jnp.float32)
    return value[:above], both[:rows] + both[rows:]


def for_each_window(first_ref, length_ref, group, rows, body):
    window = min(WINDOW, rows)
    adapters = [group * TOGETHER + at for at in range(TOGETHER)]
    begins = [first_ref[adapter] for adapter in adapters]
    ends = [first_ref[adapter] + length_ref[adapter] for adapter in adapters]
    base = begins[0] // 16 * 16

    def step(at, carry):
        low = base + at * window
        start = pl.multiple_of(jnp.minimum(low, rows - window), 16)
        places = start + lax.broadcasted_iota(jnp.int32, (window, 1), 0)
        masks = [
            (places >= jnp.maximum(begin, low)) & (places < end) for begin, end in zip(begins, ends)
        ]
        body(pl.ds(start, window), masks)
        return carry

    lax.fori_loop(0, (ends[-1] - base + window - 1) // window, step, 0)


def shrink(hidden, shrink_matrices, row_adapter_index):
    adapters = shrink_matrices.shape[0]
    every_adapter = jnp.einsum(
        "hq,gqu->hgu", hidden, shrink_matrices, preferred_element_type=jnp.float32
    )
    picked = row_adapter_index[:, None] == jnp.arange(adapters, dtype=jnp.int32)[None, :]
    partial = jnp.sum(jnp.where(picked[:, :, None], every_adapter, 0.0), axis=1)
    half = hidden.shape[0] // 2
    return jnp.concatenate([partial[:half], partial[half:]], axis=1)


def expand_body(first_ref, length_ref, packed_ref, table_ref, result_ref, shrunk_ref):
    group = pl.program_id(0)
    rows, rank = shrunk_ref.shape

    @pl.when(group == 0)
    def _():
        shrunk_ref[:rows // 2, :] = packed_ref[:, :rank].astype(jnp.bfloat16)
        shrunk_ref[rows // 2:, :] = packed_ref[:, rank:].astype(jnp.bfloat16)
        result_ref[...] = jnp.zeros_like(result_ref)

    def body(window, masks):
        shrunk = shrunk_ref[window, :]
        spread = [jnp.where(mask, shrunk, jnp.zeros((), jnp.bfloat16)) for mask in masks]
        part = jnp.dot(
            jnp.concatenate(spread, axis=1), table_ref[...], preferred_element_type=jnp.float32
        )
        result_ref[window, :] = result_ref[window, :] + part

    for_each_window(first_ref, length_ref, group, rows, body)


def expand(packed, expand_matrices, segment_first_row, segment_length):
    rows = 2 * packed.shape[0]
    adapters, rank, width = expand_matrices.shape
    table = expand_matrices.reshape(adapters * rank, width)
    return pl.pallas_call(
        expand_body,
        grid_spec=pltpu.PrefetchScalarGridSpec(
            num_scalar_prefetch=2,
            grid=(adapters // TOGETHER,),
            in_specs=[
                pl.BlockSpec((rows // 2, 2 * rank), lambda group, *_: (0, 0)),
                pl.BlockSpec((TOGETHER * rank, width), lambda group, *_: (group, 0)),
            ],
            out_specs=pl.BlockSpec((rows, width), lambda group, *_: (0, 0)),
            scratch_shapes=[pltpu.VMEM((rows, rank), jnp.bfloat16)],
        ),
        out_shape=jax.ShapeDtypeStruct((rows, width), jnp.float32),
        compiler_params=pltpu.CompilerParams(vmem_limit_bytes=VMEM_LIMIT),
        cost_estimate=pl.CostEstimate(flops=EXPAND_FLOPS, bytes_accessed=1, transcendentals=0),
    )(segment_first_row, segment_length, packed, table)


def on_device(
    total,
    hidden,
    down_matrix,
    shrink_matrices,
    expand_matrices,
    row_adapter_index,
    segment_first_row,
    segment_length,
):
    me = lax.axis_index("tensor").astype(jnp.int32)
    width = down_matrix.shape[1] // total
    core, near = 1, 2
    units = total // 4

    def out_of(unit):
        return me ^ (unit * 4 | near)

    def home_of(unit):
        return me ^ (unit * 4)

    kept_home, crossed, incoming = {}, {}, {}

    packed, steps = None, [*(4 << at for at in reversed(range((units - 1).bit_length()))), near, core]

    def send(value, bit, carry):
        nonlocal packed
        if not carry or packed is None or steps[:1] != [bit]:
            return swap(value, bit, total), None
        steps.pop(0)
        own, packed = packed, None
        arrived, shrinks = detach(swap(attach(value, own), bit, total), own)
        return arrived, own + shrinks

    def settle(unit, arrived):
        nonlocal packed
        value = kept_home[unit] + arrived.astype(jnp.float32) + crossed[unit].astype(jnp.float32)
        for moved, shrinks in incoming.pop(unit, []):
            value = value + moved.astype(jnp.float32)
            packed = packed if shrinks is None else shrinks
        if not unit:
            return value
        bit = unit & -unit
        moving = value.astype(jnp.bfloat16)
        incoming.setdefault(unit ^ bit, []).append(send(moving, 4 * bit, unit == top))
        return moving

    top = units - 1
    values, _ = product(hidden, down_matrix, [out_of(top) ^ core], [], width, [])
    ready = [values]
    for unit in reversed(range(units)):
        arrived = swap(values, core, total)
        sent, kept = [], [out_of(unit)]
        if unit:
            sent.append(out_of(unit - 1) ^ core)
        sent.append(home_of(unit) ^ core)
        if unit < top:
            kept.append(home_of(unit + 1))
        if not unit:
            kept.append(home_of(0))
        values, results = product(hidden, down_matrix, sent, kept, width, ready)
        if packed is not None and steps and steps[0] != core:
            moved, results = lax.optimization_barrier((swap(packed, steps.pop(0), total), results))
            packed = packed + moved
        if unit < top:
            kept_home[unit + 1] = results[1]
        if not unit:
            kept_home[0] = results[-1]
        leaving = (results[0] + arrived[0].astype(jnp.float32)).astype(jnp.bfloat16)
        ready = [leaving]
        if unit < top:
            leaving, arrived = lax.optimization_barrier((leaving, arrived))
            ready.append(settle(unit + 1, arrived[1]))
        if unit == top:
            late, ready[-1] = lax.optimization_barrier((hidden, ready[-1]))
            packed = shrink(late, shrink_matrices, row_adapter_index)
        if packed is not None:
            ready.append(packed)
        crossed[unit] = swap(leaving, near, total)
    kept = [settle(0, swap(values, core, total)[0])]

    for bit in steps:
        packed = packed + swap(packed, bit, total)
    adapter_output = expand(packed, expand_matrices, segment_first_row, segment_length)
    return (kept[0] + adapter_output).astype(jnp.bfloat16)


def solution(mesh):
    in_specs = (
        P("groups", "tensor"),
        P("tensor", None),
        P(None, "tensor", None),
        P(None, None, "tensor"),
        P("groups"),
        P("groups"),
        P("groups"),
    )
    out_specs = P("groups", "tensor")
    return jax.shard_map(
        functools.partial(on_device, mesh.shape["tensor"]),
        mesh=mesh,
        in_specs=in_specs,
        out_specs=out_specs,
        check_vma=False,
    )
```

```python
import functools

import jax
import jax.numpy as jnp
from jax import lax
from jax.experimental import pallas as pl
from jax.experimental.pallas import tpu as pltpu
from jax.sharding import PartitionSpec as P

VMEM_LIMIT = 39 * 1024 * 1024
WINDOW = 128
TOGETHER = 4
FLOPS = 2_500_000_000
EXPAND_FLOPS = 1_000_000


def product_body(table_ref, hidden_ref, down_ref, *refs, base, sent, kept, first, last, earlier):
    sent_ref = kept_ref = None
    refs = list(refs[earlier + (0 if first else 1):])
    if sent:
        sent_ref = refs.pop(0)
    if kept:
        kept_ref = refs.pop(0)
    buffer = refs.pop(0)
    arrived = refs.pop()
    width = buffer.shape[2]
    targets = sent + kept

    def copy(at):
        column = pl.multiple_of(table_ref[base + at] * width, width)
        slot = (base + at) % 2
        return pltpu.make_async_copy(
            down_ref.at[:, pl.ds(column, width)], buffer.at[slot], arrived.at[slot]
        )

    if first:
        copy(0).start()

    def step(at, carry):
        @pl.when(at + 1 < targets + (0 if last else 1))
        def _():
            copy(at + 1).start()

        @pl.when(at >= (0 if first else 1))
        def _():
            copy(at).wait()

        total = jnp.dot(
            hidden_ref[...], buffer[(base + at) % 2], preferred_element_type=jnp.float32
        )
        if sent:

            @pl.when(at < sent)
            def _():
                sent_ref[jnp.minimum(at, sent - 1)] = total.astype(jnp.bfloat16)

        if kept:

            @pl.when(at >= sent)
            def _():
                kept_ref[jnp.maximum(at - sent, 0)] = total

        return carry

    lax.fori_loop(0, targets, step, 0)
    if not last:
        copy(targets).wait()


def product(table, hidden, down_matrix, buffer, base, sent, kept, width, last, earlier):
    rows, depth = hidden.shape
    first = buffer is None
    vmem = pl.BlockSpec(memory_space=pltpu.VMEM)
    anywhere = pl.BlockSpec(memory_space=pl.ANY)
    out_shape = []
    if sent:
        out_shape.append(jax.ShapeDtypeStruct((sent, rows, width), jnp.bfloat16))
    if kept:
        out_shape.append(jax.ShapeDtypeStruct((kept, rows, width), jnp.float32))
    place = len(out_shape)
    out_shape.append(jax.ShapeDtypeStruct((2, depth, width), jnp.bfloat16))
    results = pl.pallas_call(
        functools.partial(
            product_body, base=base, sent=sent, kept=kept, first=first, last=last,
            earlier=len(earlier),
        ),
        in_specs=[
            pl.BlockSpec(memory_space=pltpu.SMEM),
            vmem,
            pl.BlockSpec(memory_space=pltpu.HBM),
        ]
        + ([] if first else [vmem])
        + [anywhere] * len(earlier),
        out_specs=[vmem] * len(out_shape),
        out_shape=out_shape,
        scratch_shapes=[pltpu.SemaphoreType.DMA((2,))],
        input_output_aliases={} if first else {3: place},
        compiler_params=pltpu.CompilerParams(vmem_limit_bytes=VMEM_LIMIT),
        cost_estimate=pl.CostEstimate(flops=FLOPS, bytes_accessed=1024, transcendentals=0),
    )(table, hidden, down_matrix, *([] if first else [buffer]), *earlier)
    return results[0] if sent else None, results[place - 1] if kept else None, results[place]


def swap(value, bit, total):
    return lax.ppermute(value, "tensor", [(place, place ^ bit) for place in range(total)])


def attach(value, packed):
    below = jnp.pad(packed.astype(jnp.bfloat16), ((0, 0), (0, value.shape[1] - packed.shape[1])))
    return jnp.concatenate([value, below])


def detach(value, packed):
    height, columns = packed.shape
    above = value.shape[0] - height
    return value[:above], value[above:, :columns].astype(jnp.float32)


def for_each_window(first_ref, length_ref, group, rows, body):
    window = min(WINDOW, rows)
    adapters = [group * TOGETHER + at for at in range(TOGETHER)]
    begins = [first_ref[adapter] for adapter in adapters]
    ends = [first_ref[adapter] + length_ref[adapter] for adapter in adapters]
    base = begins[0] // 16 * 16

    def step(at, carry):
        low = base + at * window
        start = pl.multiple_of(jnp.minimum(low, rows - window), 16)
        places = start + lax.broadcasted_iota(jnp.int32, (window, 1), 0)
        masks = [
            (places >= jnp.maximum(begin, low)) & (places < end) for begin, end in zip(begins, ends)
        ]
        body(pl.ds(start, window), masks)
        return carry

    lax.fori_loop(0, (ends[-1] - base + window - 1) // window, step, 0)


def shrink(hidden, shrink_matrices, row_adapter_index):
    adapters = shrink_matrices.shape[0]
    every_adapter = jnp.einsum(
        "hq,gqu->hgu", hidden, shrink_matrices, preferred_element_type=jnp.float32
    )
    picked = row_adapter_index[:, None] == jnp.arange(adapters, dtype=jnp.int32)[None, :]
    partial = jnp.sum(jnp.where(picked[:, :, None], every_adapter, 0.0), axis=1)
    return jnp.swapaxes(partial, 0, 1)


def expand_body(first_ref, length_ref, packed_ref, table_ref, result_ref, shrunk_ref):
    group = pl.program_id(0)

    @pl.when(group == 0)
    def _():
        shrunk_ref[...] = packed_ref[...].T.astype(jnp.bfloat16)
        result_ref[...] = jnp.zeros_like(result_ref)

    def body(window, masks):
        shrunk = shrunk_ref[window, :]
        spread = [jnp.where(mask, shrunk, jnp.zeros((), jnp.bfloat16)) for mask in masks]
        part = jnp.dot(
            jnp.concatenate(spread, axis=1), table_ref[...], preferred_element_type=jnp.float32
        )
        result_ref[window, :] = result_ref[window, :] + part

    for_each_window(first_ref, length_ref, group, shrunk_ref.shape[0], body)


def expand(packed, expand_matrices, segment_first_row, segment_length):
    rows = packed.shape[1]
    adapters, rank, width = expand_matrices.shape
    table = expand_matrices.reshape(adapters * rank, width)
    return pl.pallas_call(
        expand_body,
        grid_spec=pltpu.PrefetchScalarGridSpec(
            num_scalar_prefetch=2,
            grid=(adapters // TOGETHER,),
            in_specs=[
                pl.BlockSpec((rank, rows), lambda group, *_: (0, 0)),
                pl.BlockSpec((TOGETHER * rank, width), lambda group, *_: (group, 0)),
            ],
            out_specs=pl.BlockSpec((rows, width), lambda group, *_: (0, 0)),
            scratch_shapes=[pltpu.VMEM((rows, rank), jnp.bfloat16)],
        ),
        out_shape=jax.ShapeDtypeStruct((rows, width), jnp.float32),
        compiler_params=pltpu.CompilerParams(vmem_limit_bytes=VMEM_LIMIT),
        cost_estimate=pl.CostEstimate(flops=EXPAND_FLOPS, bytes_accessed=1, transcendentals=0),
    )(segment_first_row, segment_length, packed, table)


def on_device(
    total,
    hidden,
    down_matrix,
    shrink_matrices,
    expand_matrices,
    row_adapter_index,
    segment_first_row,
    segment_length,
):
    me = lax.axis_index("tensor").astype(jnp.int32)
    width = down_matrix.shape[1] // total
    core, near = 1, 2
    units = total // 4

    kept_home, crossed, incoming = {}, {}, {}

    packed, steps = None, [*(4 << at for at in reversed(range((units - 1).bit_length()))), near, core]

    def send(value, bit, carry):
        nonlocal packed
        if not carry or packed is None or steps[:1] != [bit]:
            return swap(value, bit, total), None
        steps.pop(0)
        own, packed = packed, None
        arrived, shrinks = detach(swap(attach(value, own), bit, total), own)
        return arrived, own + shrinks

    def settle(unit, arrived):
        nonlocal packed
        value = kept_home[unit] + arrived.astype(jnp.float32) + crossed[unit].astype(jnp.float32)
        for moved, shrinks in incoming.pop(unit, []):
            value = value + moved.astype(jnp.float32)
            packed = packed if shrinks is None else shrinks
        if not unit:
            return value
        bit = unit & -unit
        moving = value.astype(jnp.bfloat16)
        incoming.setdefault(unit ^ bit, []).append(send(moving, 4 * bit, unit == top))
        return moving

    top = units - 1
    order = [top * 4 | near | core]
    for unit in reversed(range(units)):
        order += [(unit - 1) * 4 | near | core] * (unit > 0) + [unit * 4 | core, unit * 4 | near]
        order += [(unit + 1) * 4] * (unit < top) + [0] * (not unit)
    table = jnp.array(order, dtype=jnp.int32) ^ me

    values, _, buffer = product(table, hidden, down_matrix, None, 0, 1, 0, width, False, [])
    base, ready = 1, []
    for unit in reversed(range(units)):
        arrived = swap(values, core, total)
        sent, kept = 1 + (unit > 0), 1 + (unit < top) + (not unit)
        values, results, buffer = product(
            table, hidden, down_matrix, buffer, base, sent, kept, width, not unit, ready
        )
        base += sent + kept
        if packed is not None and steps and steps[0] != core:
            moved, results = lax.optimization_barrier((swap(packed, steps.pop(0), total), results))
            packed = packed + moved
        if unit < top:
            kept_home[unit + 1] = results[1]
        if not unit:
            kept_home[0] = results[-1]
        leaving = (results[0] + arrived[0].astype(jnp.float32)).astype(jnp.bfloat16)
        if unit == top:
            late, leaving = lax.optimization_barrier((hidden, leaving))
        ready = [leaving]
        if unit < top:
            leaving, arrived = lax.optimization_barrier((leaving, arrived))
            ready.append(settle(unit + 1, arrived[1]))
        if unit == top:
            packed = shrink(late, shrink_matrices, row_adapter_index)
        if packed is not None:
            ready.append(packed)
        crossed[unit] = swap(leaving, near, total)
    kept = [settle(0, swap(values, core, total)[0])]

    for bit in steps:
        packed = packed + swap(packed, bit, total)
    adapter_output = expand(packed, expand_matrices, segment_first_row, segment_length)
    return (kept[0] + adapter_output).astype(jnp.bfloat16)


def solution(mesh):
    in_specs = (
        P("groups", "tensor"),
        P("tensor", None),
        P(None, "tensor", None),
        P(None, None, "tensor"),
        P("groups"),
        P("groups"),
        P("groups"),
    )
    out_specs = P("groups", "tensor")
    return jax.shard_map(
        functools.partial(on_device, mesh.shape["tensor"]),
        mesh=mesh,
        in_specs=in_specs,
        out_specs=out_specs,
        check_vma=False,
    )
```

```python
import functools

import jax
import jax.numpy as jnp
from jax import lax
from jax.experimental import pallas as pl
from jax.experimental.pallas import tpu as pltpu
from jax.sharding import PartitionSpec as P

VMEM_LIMIT = 39 * 1024 * 1024
WINDOW = 128
TOGETHER = 4
FLOPS = 2_500_000_000
FIRST_FLOPS = 10_000_000_000
EXPAND_FLOPS = 1_000_000


def product_body(table_ref, hidden_ref, down_ref, *refs, base, sent, kept, first, last, earlier):
    sent_ref = kept_ref = None
    refs = list(refs[earlier + (0 if first else 1):])
    if sent:
        sent_ref = refs.pop(0)
    if kept:
        kept_ref = refs.pop(0)
    buffer = refs.pop(0)
    arrived = refs.pop()
    width = buffer.shape[2]
    targets = sent + kept

    def copy(at):
        column = pl.multiple_of(table_ref[base + at] * width, width)
        slot = (base + at) % 2
        return pltpu.make_async_copy(
            down_ref.at[:, pl.ds(column, width)], buffer.at[slot], arrived.at[slot]
        )

    if first:
        copy(0).start()

    def step(at, carry):
        @pl.when(at + 1 < targets + (0 if last else 1))
        def _():
            copy(at + 1).start()

        @pl.when(at >= (0 if first else 1))
        def _():
            copy(at).wait()

        total = jnp.dot(
            hidden_ref[...], buffer[(base + at) % 2], preferred_element_type=jnp.float32
        )
        if sent:

            @pl.when(at < sent)
            def _():
                sent_ref[jnp.minimum(at, sent - 1)] = total.astype(jnp.bfloat16)

        if kept:

            @pl.when(at >= sent)
            def _():
                kept_ref[jnp.maximum(at - sent, 0)] = total

        return carry

    lax.fori_loop(0, targets, step, 0)
    if not last:
        copy(targets).wait()


def product(table, hidden, down_matrix, buffer, base, sent, kept, width, last, flops, earlier):
    rows, depth = hidden.shape
    first = buffer is None
    vmem = pl.BlockSpec(memory_space=pltpu.VMEM)
    anywhere = pl.BlockSpec(memory_space=pl.ANY)
    out_shape = []
    if sent:
        out_shape.append(jax.ShapeDtypeStruct((sent, rows, width), jnp.bfloat16))
    if kept:
        out_shape.append(jax.ShapeDtypeStruct((kept, rows, width), jnp.float32))
    place = len(out_shape)
    out_shape.append(jax.ShapeDtypeStruct((2, depth, width), jnp.bfloat16))
    results = pl.pallas_call(
        functools.partial(
            product_body, base=base, sent=sent, kept=kept, first=first, last=last,
            earlier=len(earlier),
        ),
        in_specs=[
            pl.BlockSpec(memory_space=pltpu.SMEM),
            vmem,
            pl.BlockSpec(memory_space=pltpu.HBM),
        ]
        + ([] if first else [vmem])
        + [anywhere] * len(earlier),
        out_specs=[vmem] * len(out_shape),
        out_shape=out_shape,
        scratch_shapes=[pltpu.SemaphoreType.DMA((2,))],
        input_output_aliases={} if first else {3: place},
        compiler_params=pltpu.CompilerParams(vmem_limit_bytes=VMEM_LIMIT),
        cost_estimate=pl.CostEstimate(flops=flops, bytes_accessed=1024, transcendentals=0),
    )(table, hidden, down_matrix, *([] if first else [buffer]), *earlier)
    return results[0] if sent else None, results[place - 1] if kept else None, results[place]


def swap(value, bit, total):
    return lax.ppermute(value, "tensor", [(place, place ^ bit) for place in range(total)])


def attach(value, packed):
    below = jnp.pad(packed.astype(jnp.bfloat16), ((0, 0), (0, value.shape[1] - packed.shape[1])))
    return jnp.concatenate([value, below])


def detach(value, packed):
    height, columns = packed.shape
    above = value.shape[0] - height
    return value[:above], value[above:, :columns].astype(jnp.float32)


def for_each_window(first_ref, length_ref, group, rows, body):
    window = min(WINDOW, rows)
    adapters = [group * TOGETHER + at for at in range(TOGETHER)]
    begins = [first_ref[adapter] for adapter in adapters]
    ends = [first_ref[adapter] + length_ref[adapter] for adapter in adapters]
    base = begins[0] // 16 * 16

    def step(at, carry):
        low = base + at * window
        start = pl.multiple_of(jnp.minimum(low, rows - window), 16)
        places = start + lax.broadcasted_iota(jnp.int32, (window, 1), 0)
        masks = [
            (places >= jnp.maximum(begin, low)) & (places < end) for begin, end in zip(begins, ends)
        ]
        body(pl.ds(start, window), masks)
        return carry

    lax.fori_loop(0, (ends[-1] - base + window - 1) // window, step, 0)


def shrink(hidden, shrink_matrices, row_adapter_index):
    adapters = shrink_matrices.shape[0]
    every_adapter = jnp.einsum(
        "hq,gqu->hgu", hidden, shrink_matrices, preferred_element_type=jnp.float32
    )
    picked = row_adapter_index[:, None] == jnp.arange(adapters, dtype=jnp.int32)[None, :]
    partial = jnp.sum(jnp.where(picked[:, :, None], every_adapter, 0.0), axis=1)
    return jnp.swapaxes(partial, 0, 1)


def expand_body(first_ref, length_ref, packed_ref, table_ref, result_ref, shrunk_ref):
    group = pl.program_id(0)

    @pl.when(group == 0)
    def _():
        shrunk_ref[...] = packed_ref[...].T.astype(jnp.bfloat16)
        result_ref[...] = jnp.zeros_like(result_ref)

    def body(window, masks):
        shrunk = shrunk_ref[window, :]
        spread = [jnp.where(mask, shrunk, jnp.zeros((), jnp.bfloat16)) for mask in masks]
        part = jnp.dot(
            jnp.concatenate(spread, axis=1), table_ref[...], preferred_element_type=jnp.float32
        )
        result_ref[window, :] = result_ref[window, :] + part

    for_each_window(first_ref, length_ref, group, shrunk_ref.shape[0], body)


def expand(packed, expand_matrices, segment_first_row, segment_length):
    rows = packed.shape[1]
    adapters, rank, width = expand_matrices.shape
    table = expand_matrices.reshape(adapters * rank, width)
    return pl.pallas_call(
        expand_body,
        grid_spec=pltpu.PrefetchScalarGridSpec(
            num_scalar_prefetch=2,
            grid=(adapters // TOGETHER,),
            in_specs=[
                pl.BlockSpec((rank, rows), lambda group, *_: (0, 0)),
                pl.BlockSpec((TOGETHER * rank, width), lambda group, *_: (group, 0)),
            ],
            out_specs=pl.BlockSpec((rows, width), lambda group, *_: (0, 0)),
            scratch_shapes=[pltpu.VMEM((rows, rank), jnp.bfloat16)],
        ),
        out_shape=jax.ShapeDtypeStruct((rows, width), jnp.float32),
        compiler_params=pltpu.CompilerParams(vmem_limit_bytes=VMEM_LIMIT),
        cost_estimate=pl.CostEstimate(flops=EXPAND_FLOPS, bytes_accessed=1, transcendentals=0),
    )(segment_first_row, segment_length, packed, table)


def on_device(
    total,
    hidden,
    down_matrix,
    shrink_matrices,
    expand_matrices,
    row_adapter_index,
    segment_first_row,
    segment_length,
):
    me = lax.axis_index("tensor").astype(jnp.int32)
    width = down_matrix.shape[1] // total
    core, near = 1, 2
    units = total // 4

    kept_home, crossed, incoming = {}, {}, {}

    packed, steps = None, [near, *(4 << at for at in range((units - 1).bit_length())), core]

    def send(value, bit, carry):
        nonlocal packed
        fits = packed is not None and packed.shape[1] <= value.shape[1]
        if not carry or not fits or steps[:1] != [bit]:
            return swap(value, bit, total), None
        steps.pop(0)
        own, packed = packed, None
        arrived, shrinks = detach(swap(attach(value, own), bit, total), own)
        return arrived, own + shrinks

    def settle(unit, arrived):
        nonlocal packed
        value = kept_home[unit] + arrived.astype(jnp.float32) + crossed[unit].astype(jnp.float32)
        for moved, shrinks in incoming.pop(unit, []):
            value = value + moved.astype(jnp.float32)
            packed = packed if shrinks is None else shrinks
        if not unit:
            return value
        bit = unit & -unit
        moving = value.astype(jnp.bfloat16)
        incoming.setdefault(unit ^ bit, []).append(send(moving, 4 * bit, unit == top))
        return moving

    top = units - 1
    order = [top * 4 | near | core]
    for unit in reversed(range(units)):
        order += [(unit - 1) * 4 | near | core] * (unit > 0) + [unit * 4 | core, unit * 4 | near]
        order += [(unit + 1) * 4] * (unit < top) + [0] * (not unit)
    table = jnp.array(order, dtype=jnp.int32) ^ me

    values, _, buffer = product(table, hidden, down_matrix, None, 0, 1, 0, width, False, FLOPS, [])
    base, ready = 1, []
    for unit in reversed(range(units)):
        arrived = swap(values, core, total)
        sent, kept = 1 + (unit > 0), 1 + (unit < top) + (not unit)
        values, results, buffer = product(
            table, hidden, down_matrix, buffer, base, sent, kept, width, not unit,
            FIRST_FLOPS if unit == top - 1 else FLOPS, ready,
        )
        base += sent + kept
        if packed is not None and steps and steps[0] != core:
            moved, results = lax.optimization_barrier((swap(packed, steps.pop(0), total), results))
            packed = packed + moved
        if unit < top:
            kept_home[unit + 1] = results[1]
        if not unit:
            kept_home[0] = results[-1]
        leaving = (results[0] + arrived[0].astype(jnp.float32)).astype(jnp.bfloat16)
        if unit == top:
            late, leaving = lax.optimization_barrier((hidden, leaving))
        ready = [leaving]
        if unit < top:
            leaving, arrived = lax.optimization_barrier((leaving, arrived))
            ready.append(settle(unit + 1, arrived[1]))
        if unit == top:
            packed = shrink(late, shrink_matrices, row_adapter_index)
        if packed is not None:
            ready.append(packed)
        crossed[unit] = swap(leaving, near, total)
    kept = [settle(0, swap(values, core, total)[0])]

    for bit in steps:
        packed = packed + swap(packed, bit, total)
    adapter_output = expand(packed, expand_matrices, segment_first_row, segment_length)
    return (kept[0] + adapter_output).astype(jnp.bfloat16)


def solution(mesh):
    in_specs = (
        P("groups", "tensor"),
        P("tensor", None),
        P(None, "tensor", None),
        P(None, None, "tensor"),
        P("groups"),
        P("groups"),
        P("groups"),
    )
    out_specs = P("groups", "tensor")
    return jax.shard_map(
        functools.partial(on_device, mesh.shape["tensor"]),
        mesh=mesh,
        in_specs=in_specs,
        out_specs=out_specs,
        check_vma=False,
    )
```

```python
import functools

import jax
import jax.numpy as jnp
from jax import lax
from jax.experimental import pallas as pl
from jax.experimental.pallas import tpu as pltpu
from jax.sharding import PartitionSpec as P

VMEM_LIMIT = 39 * 1024 * 1024
WINDOW = 128
TOGETHER = 4
FLOPS = 2_500_000_000
FIRST_FLOPS = 10_000_000_000
EXPAND_FLOPS = 1_000_000


def product_body(table_ref, hidden_ref, down_ref, *refs, base, sent, kept, first, last, earlier):
    sent_ref = kept_ref = None
    refs = list(refs[earlier + (0 if first else 1):])
    if sent:
        sent_ref = refs.pop(0)
    if kept:
        kept_ref = refs.pop(0)
    buffer = refs.pop(0)
    arrived = refs.pop()
    width = buffer.shape[2]
    targets = sent + kept

    def copy(at):
        column = pl.multiple_of(table_ref[base + at] * width, width)
        slot = (base + at) % 2
        return pltpu.make_async_copy(
            down_ref.at[:, pl.ds(column, width)], buffer.at[slot], arrived.at[slot]
        )

    if first:
        copy(0).start()

    def step(at, carry):
        @pl.when(at + 1 < targets + (0 if last else 1))
        def _():
            copy(at + 1).start()

        @pl.when(at >= (0 if first else 1))
        def _():
            copy(at).wait()

        total = jnp.dot(
            hidden_ref[...], buffer[(base + at) % 2], preferred_element_type=jnp.float32
        )
        if sent:

            @pl.when(at < sent)
            def _():
                sent_ref[jnp.minimum(at, sent - 1)] = total.astype(jnp.bfloat16)

        if kept:

            @pl.when(at >= sent)
            def _():
                kept_ref[jnp.maximum(at - sent, 0)] = total

        return carry

    lax.fori_loop(0, targets, step, 0)
    if not last:
        copy(targets).wait()


def product(table, hidden, down_matrix, buffer, base, sent, kept, width, last, flops, earlier):
    rows, depth = hidden.shape
    first = buffer is None
    vmem = pl.BlockSpec(memory_space=pltpu.VMEM)
    anywhere = pl.BlockSpec(memory_space=pl.ANY)
    out_shape = []
    if sent:
        out_shape.append(jax.ShapeDtypeStruct((sent, rows, width), jnp.bfloat16))
    if kept:
        out_shape.append(jax.ShapeDtypeStruct((kept, rows, width), jnp.float32))
    place = len(out_shape)
    out_shape.append(jax.ShapeDtypeStruct((2, depth, width), jnp.bfloat16))
    results = pl.pallas_call(
        functools.partial(
            product_body, base=base, sent=sent, kept=kept, first=first, last=last,
            earlier=len(earlier),
        ),
        in_specs=[
            pl.BlockSpec(memory_space=pltpu.SMEM),
            vmem,
            pl.BlockSpec(memory_space=pltpu.HBM),
        ]
        + ([] if first else [vmem])
        + [anywhere] * len(earlier),
        out_specs=[vmem] * len(out_shape),
        out_shape=out_shape,
        scratch_shapes=[pltpu.SemaphoreType.DMA((2,))],
        input_output_aliases={} if first else {3: place},
        compiler_params=pltpu.CompilerParams(vmem_limit_bytes=VMEM_LIMIT),
        cost_estimate=pl.CostEstimate(flops=flops, bytes_accessed=1024, transcendentals=0),
    )(table, hidden, down_matrix, *([] if first else [buffer]), *earlier)
    return results[0] if sent else None, results[place - 1] if kept else None, results[place]


def swap(value, bit, total):
    return lax.ppermute(value, "tensor", [(place, place ^ bit) for place in range(total)])


def for_each_window(first_ref, length_ref, group, rows, body):
    window = min(WINDOW, rows)
    adapters = [group * TOGETHER + at for at in range(TOGETHER)]
    begins = [first_ref[adapter] for adapter in adapters]
    ends = [first_ref[adapter] + length_ref[adapter] for adapter in adapters]
    base = begins[0] // 16 * 16

    def step(at, carry):
        low = base + at * window
        start = pl.multiple_of(jnp.minimum(low, rows - window), 16)
        places = start + lax.broadcasted_iota(jnp.int32, (window, 1), 0)
        masks = [
            (places >= jnp.maximum(begin, low)) & (places < end) for begin, end in zip(begins, ends)
        ]
        body(pl.ds(start, window), masks)
        return carry

    lax.fori_loop(0, (ends[-1] - base + window - 1) // window, step, 0)


def shrink(hidden, shrink_matrices, row_adapter_index):
    adapters = shrink_matrices.shape[0]
    every_adapter = jnp.einsum(
        "hq,gqu->hgu", hidden, shrink_matrices, preferred_element_type=jnp.float32
    )
    picked = row_adapter_index[:, None] == jnp.arange(adapters, dtype=jnp.int32)[None, :]
    partial = jnp.sum(jnp.where(picked[:, :, None], every_adapter, 0.0), axis=1)
    return jnp.swapaxes(partial, 0, 1)


def expand_body(first_ref, length_ref, packed_ref, table_ref, result_ref, shrunk_ref):
    group = pl.program_id(0)

    @pl.when(group == 0)
    def _():
        shrunk_ref[...] = packed_ref[...].T.astype(jnp.bfloat16)
        result_ref[...] = jnp.zeros_like(result_ref)

    def body(window, masks):
        shrunk = shrunk_ref[window, :]
        spread = [jnp.where(mask, shrunk, jnp.zeros((), jnp.bfloat16)) for mask in masks]
        part = jnp.dot(
            jnp.concatenate(spread, axis=1), table_ref[...], preferred_element_type=jnp.float32
        )
        result_ref[window, :] = result_ref[window, :] + part

    for_each_window(first_ref, length_ref, group, shrunk_ref.shape[0], body)


def expand(packed, expand_matrices, segment_first_row, segment_length):
    rows = packed.shape[1]
    adapters, rank, width = expand_matrices.shape
    table = expand_matrices.reshape(adapters * rank, width)
    return pl.pallas_call(
        expand_body,
        grid_spec=pltpu.PrefetchScalarGridSpec(
            num_scalar_prefetch=2,
            grid=(adapters // TOGETHER,),
            in_specs=[
                pl.BlockSpec((rank, rows), lambda group, *_: (0, 0)),
                pl.BlockSpec((TOGETHER * rank, width), lambda group, *_: (group, 0)),
            ],
            out_specs=pl.BlockSpec((rows, width), lambda group, *_: (0, 0)),
            scratch_shapes=[pltpu.VMEM((rows, rank), jnp.bfloat16)],
        ),
        out_shape=jax.ShapeDtypeStruct((rows, width), jnp.float32),
        compiler_params=pltpu.CompilerParams(vmem_limit_bytes=VMEM_LIMIT),
        cost_estimate=pl.CostEstimate(flops=EXPAND_FLOPS, bytes_accessed=1, transcendentals=0),
    )(segment_first_row, segment_length, packed, table)


def on_device(
    total,
    hidden,
    down_matrix,
    shrink_matrices,
    expand_matrices,
    row_adapter_index,
    segment_first_row,
    segment_length,
):
    me = lax.axis_index("tensor").astype(jnp.int32)
    width = down_matrix.shape[1] // total
    core, near = 1, 2
    units = total // 4

    kept_home, crossed, incoming = {}, {}, {}

    packed, steps = None, [near, *(4 << at for at in range((units - 1).bit_length())), core]

    def settle(unit, arrived):
        value = kept_home[unit] + arrived.astype(jnp.float32) + crossed[unit].astype(jnp.float32)
        for moved in incoming.pop(unit, []):
            value = value + moved.astype(jnp.float32)
        if not unit:
            return value
        bit = unit & -unit
        moving = value.astype(jnp.bfloat16)
        incoming.setdefault(unit ^ bit, []).append(swap(moving, 4 * bit, total))
        return moving

    top = units - 1
    order = [top * 4 | near | core]
    for unit in reversed(range(units)):
        order += [(unit - 1) * 4 | near | core] * (unit > 0) + [unit * 4 | core, unit * 4 | near]
        order += [(unit + 1) * 4] * (unit < top) + [0] * (not unit)
    table = jnp.array(order, dtype=jnp.int32) ^ me

    values, _, buffer = product(table, hidden, down_matrix, None, 0, 1, 0, width, False, FLOPS, [])
    base, ready = 1, []
    for unit in reversed(range(units)):
        arrived = swap(values, core, total)
        sent, kept = 1 + (unit > 0), 1 + (unit < top) + (not unit)
        values, results, buffer = product(
            table, hidden, down_matrix, buffer, base, sent, kept, width, not unit,
            FIRST_FLOPS if unit == top - 1 else FLOPS, ready,
        )
        base += sent + kept
        if packed is not None and steps and steps[0] != core:
            moved, results = lax.optimization_barrier((swap(packed, steps.pop(0), total), results))
            packed = packed + moved
        if unit < top:
            kept_home[unit + 1] = results[1]
        if not unit:
            kept_home[0] = results[-1]
        leaving = (results[0] + arrived[0].astype(jnp.float32)).astype(jnp.bfloat16)
        if unit == max(top - 1, 0):
            late, leaving = lax.optimization_barrier((hidden, leaving))
        ready = [leaving]
        if unit < top:
            leaving, arrived = lax.optimization_barrier((leaving, arrived))
            ready.append(settle(unit + 1, arrived[1]))
        if unit == max(top - 1, 0):
            packed = shrink(late, shrink_matrices, row_adapter_index)
        if packed is not None:
            ready.append(packed)
        crossed[unit] = swap(leaving, near, total)
    kept = [settle(0, swap(values, core, total)[0])]

    for bit in steps:
        kind = jnp.bfloat16 if bit > near else jnp.float32
        packed = packed + swap(packed.astype(kind), bit, total).astype(jnp.float32)
    adapter_output = expand(packed, expand_matrices, segment_first_row, segment_length)
    return (kept[0] + adapter_output).astype(jnp.bfloat16)


def solution(mesh):
    in_specs = (
        P("groups", "tensor"),
        P("tensor", None),
        P(None, "tensor", None),
        P(None, None, "tensor"),
        P("groups"),
        P("groups"),
        P("groups"),
    )
    out_specs = P("groups", "tensor")
    return jax.shard_map(
        functools.partial(on_device, mesh.shape["tensor"]),
        mesh=mesh,
        in_specs=in_specs,
        out_specs=out_specs,
        check_vma=False,
    )
```

```python
import functools

import jax
import jax.numpy as jnp
from jax import lax
from jax.experimental import pallas as pl
from jax.experimental.pallas import tpu as pltpu
from jax.sharding import PartitionSpec as P

VMEM_LIMIT = 39 * 1024 * 1024
WINDOW = 128
TOGETHER = 4
FLOPS = 10_000_000_000
FIRST_FLOPS = 10_000_000_000
EXPAND_FLOPS = 1_000_000


def product_body(table_ref, hidden_ref, down_ref, *refs, base, sent, kept, first, last, earlier):
    sent_ref = kept_ref = None
    refs = list(refs[earlier + (0 if first else 1):])
    if sent:
        sent_ref = refs.pop(0)
    if kept:
        kept_ref = refs.pop(0)
    buffer = refs.pop(0)
    arrived = refs.pop()
    width = buffer.shape[2]
    targets = sent + kept

    def copy(at):
        column = pl.multiple_of(table_ref[base + at] * width, width)
        slot = (base + at) % 2
        return pltpu.make_async_copy(
            down_ref.at[:, pl.ds(column, width)], buffer.at[slot], arrived.at[slot]
        )

    if first:
        copy(0).start()

    def step(at, carry):
        @pl.when(at + 1 < targets + (0 if last else 1))
        def _():
            copy(at + 1).start()

        @pl.when(at >= (0 if first else 1))
        def _():
            copy(at).wait()

        total = jnp.dot(
            hidden_ref[...], buffer[(base + at) % 2], preferred_element_type=jnp.float32
        )
        if sent:

            @pl.when(at < sent)
            def _():
                sent_ref[jnp.minimum(at, sent - 1)] = total.astype(jnp.bfloat16)

        if kept:

            @pl.when(at >= sent)
            def _():
                kept_ref[jnp.maximum(at - sent, 0)] = total

        return carry

    lax.fori_loop(0, targets, step, 0)
    if not last:
        copy(targets).wait()


def product(table, hidden, down_matrix, buffer, base, sent, kept, width, last, flops, earlier):
    rows, depth = hidden.shape
    first = buffer is None
    vmem = pl.BlockSpec(memory_space=pltpu.VMEM)
    anywhere = pl.BlockSpec(memory_space=pl.ANY)
    out_shape = []
    if sent:
        out_shape.append(jax.ShapeDtypeStruct((sent, rows, width), jnp.bfloat16))
    if kept:
        out_shape.append(jax.ShapeDtypeStruct((kept, rows, width), jnp.float32))
    place = len(out_shape)
    out_shape.append(jax.ShapeDtypeStruct((2, depth, width), jnp.bfloat16))
    results = pl.pallas_call(
        functools.partial(
            product_body, base=base, sent=sent, kept=kept, first=first, last=last,
            earlier=len(earlier),
        ),
        in_specs=[
            pl.BlockSpec(memory_space=pltpu.SMEM),
            vmem,
            pl.BlockSpec(memory_space=pltpu.HBM),
        ]
        + ([] if first else [vmem])
        + [anywhere] * len(earlier),
        out_specs=[vmem] * len(out_shape),
        out_shape=out_shape,
        scratch_shapes=[pltpu.SemaphoreType.DMA((2,))],
        input_output_aliases={} if first else {3: place},
        compiler_params=pltpu.CompilerParams(vmem_limit_bytes=VMEM_LIMIT),
        cost_estimate=pl.CostEstimate(flops=flops, bytes_accessed=1024, transcendentals=0),
    )(table, hidden, down_matrix, *([] if first else [buffer]), *earlier)
    return results[0] if sent else None, results[place - 1] if kept else None, results[place]


def swap(value, bit, total):
    return lax.ppermute(value, "tensor", [(place, place ^ bit) for place in range(total)])


def for_each_window(first_ref, length_ref, group, rows, body):
    window = min(WINDOW, rows)
    adapters = [group * TOGETHER + at for at in range(TOGETHER)]
    begins = [first_ref[adapter] for adapter in adapters]
    ends = [first_ref[adapter] + length_ref[adapter] for adapter in adapters]
    base = begins[0] // 16 * 16

    def step(at, carry):
        low = base + at * window
        start = pl.multiple_of(jnp.minimum(low, rows - window), 16)
        places = start + lax.broadcasted_iota(jnp.int32, (window, 1), 0)
        masks = [
            (places >= jnp.maximum(begin, low)) & (places < end) for begin, end in zip(begins, ends)
        ]
        body(pl.ds(start, window), masks)
        return carry

    lax.fori_loop(0, (ends[-1] - base + window - 1) // window, step, 0)


def shrink(hidden, shrink_matrices, row_adapter_index):
    adapters = shrink_matrices.shape[0]
    every_adapter = jnp.einsum(
        "hq,gqu->hgu", hidden, shrink_matrices, preferred_element_type=jnp.float32
    )
    picked = row_adapter_index[:, None] == jnp.arange(adapters, dtype=jnp.int32)[None, :]
    partial = jnp.sum(jnp.where(picked[:, :, None], every_adapter, 0.0), axis=1)
    return jnp.swapaxes(partial, 0, 1)


def expand_body(first_ref, length_ref, packed_ref, table_ref, result_ref, shrunk_ref):
    group = pl.program_id(0)

    @pl.when(group == 0)
    def _():
        shrunk_ref[...] = packed_ref[...].T.astype(jnp.bfloat16)
        result_ref[...] = jnp.zeros_like(result_ref)

    def body(window, masks):
        shrunk = shrunk_ref[window, :]
        spread = [jnp.where(mask, shrunk, jnp.zeros((), jnp.bfloat16)) for mask in masks]
        part = jnp.dot(
            jnp.concatenate(spread, axis=1), table_ref[...], preferred_element_type=jnp.float32
        )
        result_ref[window, :] = result_ref[window, :] + part

    for_each_window(first_ref, length_ref, group, shrunk_ref.shape[0], body)


def expand(packed, expand_matrices, segment_first_row, segment_length):
    rows = packed.shape[1]
    adapters, rank, width = expand_matrices.shape
    table = expand_matrices.reshape(adapters * rank, width)
    return pl.pallas_call(
        expand_body,
        grid_spec=pltpu.PrefetchScalarGridSpec(
            num_scalar_prefetch=2,
            grid=(adapters // TOGETHER,),
            in_specs=[
                pl.BlockSpec((rank, rows), lambda group, *_: (0, 0)),
                pl.BlockSpec((TOGETHER * rank, width), lambda group, *_: (group, 0)),
            ],
            out_specs=pl.BlockSpec((rows, width), lambda group, *_: (0, 0)),
            scratch_shapes=[pltpu.VMEM((rows, rank), jnp.bfloat16)],
        ),
        out_shape=jax.ShapeDtypeStruct((rows, width), jnp.float32),
        compiler_params=pltpu.CompilerParams(vmem_limit_bytes=VMEM_LIMIT),
        cost_estimate=pl.CostEstimate(flops=EXPAND_FLOPS, bytes_accessed=1, transcendentals=0),
    )(segment_first_row, segment_length, packed, table)


def on_device(
    total,
    hidden,
    down_matrix,
    shrink_matrices,
    expand_matrices,
    row_adapter_index,
    segment_first_row,
    segment_length,
):
    me = lax.axis_index("tensor").astype(jnp.int32)
    width = down_matrix.shape[1] // total
    core, near = 1, 2
    units = total // 4

    kept_home, crossed, incoming = {}, {}, {}

    packed, steps = None, [near, *(4 << at for at in range((units - 1).bit_length())), core]

    def settle(unit, arrived):
        value = kept_home[unit] + arrived.astype(jnp.float32) + crossed[unit].astype(jnp.float32)
        for moved in incoming.pop(unit, []):
            value = value + moved.astype(jnp.float32)
        if not unit:
            return value
        bit = unit & -unit
        moving = value.astype(jnp.bfloat16)
        incoming.setdefault(unit ^ bit, []).append(swap(moving, 4 * bit, total))
        return moving

    top = units - 1
    order = [top * 4 | near | core]
    for unit in reversed(range(units)):
        order += [(unit - 1) * 4 | near | core] * (unit > 0) + [unit * 4 | core, unit * 4 | near]
        order += [(unit + 1) * 4] * (unit < top) + [0] * (not unit)
    table = jnp.array(order, dtype=jnp.int32) ^ me

    values, _, buffer = product(table, hidden, down_matrix, None, 0, 1, 0, width, False, FLOPS, [])
    base, ready = 1, []
    for unit in reversed(range(units)):
        arrived = swap(values, core, total)
        sent, kept = 1 + (unit > 0), 1 + (unit < top) + (not unit)
        values, results, buffer = product(
            table, hidden, down_matrix, buffer, base, sent, kept, width, not unit,
            FIRST_FLOPS if unit == top - 1 else FLOPS, ready,
        )
        base += sent + kept
        if packed is not None and steps and steps[0] != core:
            moved, results = lax.optimization_barrier((swap(packed, steps.pop(0), total), results))
            packed = packed + moved
        if unit < top:
            kept_home[unit + 1] = results[1]
        if not unit:
            kept_home[0] = results[-1]
        leaving = (results[0] + arrived[0].astype(jnp.float32)).astype(jnp.bfloat16)
        if unit == max(top - 1, 0):
            late, leaving = lax.optimization_barrier((hidden, leaving))
        ready = [leaving]
        if unit < top:
            leaving, arrived = lax.optimization_barrier((leaving, arrived))
            ready.append(settle(unit + 1, arrived[1]))
        if unit == max(top - 1, 0):
            packed = shrink(late, shrink_matrices, row_adapter_index)
        if packed is not None:
            ready.append(packed)
        crossed[unit] = swap(leaving, near, total)
    kept = [settle(0, swap(values, core, total)[0])]

    for bit in steps:
        kind = jnp.bfloat16 if bit > near else jnp.float32
        packed = packed + swap(packed.astype(kind), bit, total).astype(jnp.float32)
    adapter_output = expand(packed, expand_matrices, segment_first_row, segment_length)
    return (kept[0] + adapter_output).astype(jnp.bfloat16)


def solution(mesh):
    in_specs = (
        P("groups", "tensor"),
        P("tensor", None),
        P(None, "tensor", None),
        P(None, None, "tensor"),
        P("groups"),
        P("groups"),
        P("groups"),
    )
    out_specs = P("groups", "tensor")
    return jax.shard_map(
        functools.partial(on_device, mesh.shape["tensor"]),
        mesh=mesh,
        in_specs=in_specs,
        out_specs=out_specs,
        check_vma=False,
    )
```

```python
import functools

import jax
import jax.numpy as jnp
from jax import lax
from jax.experimental import pallas as pl
from jax.experimental.pallas import tpu as pltpu
from jax.sharding import PartitionSpec as P

VMEM_LIMIT = 39 * 1024 * 1024
WINDOW = 128
TOGETHER = 4
FLOPS = 3_000_000_000
FIRST_FLOPS = 3_000_000_000
EXPAND_FLOPS = 1_000_000


def product_body(table_ref, hidden_ref, down_ref, *refs, base, sent, kept, first, last, earlier):
    sent_ref = kept_ref = None
    refs = list(refs[earlier + (0 if first else 1):])
    if sent:
        sent_ref = refs.pop(0)
    if kept:
        kept_ref = refs.pop(0)
    buffer = refs.pop(0)
    arrived = refs.pop()
    width = buffer.shape[2]
    targets = sent + kept

    def copy(at):
        column = pl.multiple_of(table_ref[base + at] * width, width)
        slot = (base + at) % 2
        return pltpu.make_async_copy(
            down_ref.at[:, pl.ds(column, width)], buffer.at[slot], arrived.at[slot]
        )

    if first:
        copy(0).start()

    def step(at, carry):
        @pl.when(at + 1 < targets + (0 if last else 1))
        def _():
            copy(at + 1).start()

        @pl.when(at >= (0 if first else 1))
        def _():
            copy(at).wait()

        total = jnp.dot(
            hidden_ref[...], buffer[(base + at) % 2], preferred_element_type=jnp.float32
        )
        if sent:

            @pl.when(at < sent)
            def _():
                sent_ref[jnp.minimum(at, sent - 1)] = total.astype(jnp.bfloat16)

        if kept:

            @pl.when(at >= sent)
            def _():
                kept_ref[jnp.maximum(at - sent, 0)] = total

        return carry

    lax.fori_loop(0, targets, step, 0)
    if not last:
        copy(targets).wait()


def product(table, hidden, down_matrix, buffer, base, sent, kept, width, last, flops, earlier):
    rows, depth = hidden.shape
    first = buffer is None
    vmem = pl.BlockSpec(memory_space=pltpu.VMEM)
    anywhere = pl.BlockSpec(memory_space=pl.ANY)
    out_shape = []
    if sent:
        out_shape.append(jax.ShapeDtypeStruct((sent, rows, width), jnp.bfloat16))
    if kept:
        out_shape.append(jax.ShapeDtypeStruct((kept, rows, width), jnp.float32))
    place = len(out_shape)
    out_shape.append(jax.ShapeDtypeStruct((2, depth, width), jnp.bfloat16))
    results = pl.pallas_call(
        functools.partial(
            product_body, base=base, sent=sent, kept=kept, first=first, last=last,
            earlier=len(earlier),
        ),
        in_specs=[
            pl.BlockSpec(memory_space=pltpu.SMEM),
            vmem,
            pl.BlockSpec(memory_space=pltpu.HBM),
        ]
        + ([] if first else [vmem])
        + [anywhere] * len(earlier),
        out_specs=[vmem] * len(out_shape),
        out_shape=out_shape,
        scratch_shapes=[pltpu.SemaphoreType.DMA((2,))],
        input_output_aliases={} if first else {3: place},
        compiler_params=pltpu.CompilerParams(vmem_limit_bytes=VMEM_LIMIT),
        cost_estimate=pl.CostEstimate(flops=flops, bytes_accessed=1024, transcendentals=0),
    )(table, hidden, down_matrix, *([] if first else [buffer]), *earlier)
    return results[0] if sent else None, results[place - 1] if kept else None, results[place]


def swap(value, bit, total):
    return lax.ppermute(value, "tensor", [(place, place ^ bit) for place in range(total)])


def for_each_window(first_ref, length_ref, group, rows, body):
    window = min(WINDOW, rows)
    adapters = [group * TOGETHER + at for at in range(TOGETHER)]
    begins = [first_ref[adapter] for adapter in adapters]
    ends = [first_ref[adapter] + length_ref[adapter] for adapter in adapters]
    base = begins[0] // 16 * 16

    def step(at, carry):
        low = base + at * window
        start = pl.multiple_of(jnp.minimum(low, rows - window), 16)
        places = start + lax.broadcasted_iota(jnp.int32, (window, 1), 0)
        masks = [
            (places >= jnp.maximum(begin, low)) & (places < end) for begin, end in zip(begins, ends)
        ]
        body(pl.ds(start, window), masks)
        return carry

    lax.fori_loop(0, (ends[-1] - base + window - 1) // window, step, 0)


def shrink(hidden, shrink_matrices, row_adapter_index):
    adapters = shrink_matrices.shape[0]
    every_adapter = jnp.einsum(
        "hq,gqu->hgu", hidden, shrink_matrices, preferred_element_type=jnp.float32
    )
    picked = row_adapter_index[:, None] == jnp.arange(adapters, dtype=jnp.int32)[None, :]
    partial = jnp.sum(jnp.where(picked[:, :, None], every_adapter, 0.0), axis=1)
    return jnp.swapaxes(partial, 0, 1)


def expand_body(first_ref, length_ref, packed_ref, table_ref, result_ref, shrunk_ref):
    group = pl.program_id(0)

    @pl.when(group == 0)
    def _():
        shrunk_ref[...] = packed_ref[...].T.astype(jnp.bfloat16)
        result_ref[...] = jnp.zeros_like(result_ref)

    def body(window, masks):
        shrunk = shrunk_ref[window, :]
        spread = [jnp.where(mask, shrunk, jnp.zeros((), jnp.bfloat16)) for mask in masks]
        part = jnp.dot(
            jnp.concatenate(spread, axis=1), table_ref[...], preferred_element_type=jnp.float32
        )
        result_ref[window, :] = result_ref[window, :] + part

    for_each_window(first_ref, length_ref, group, shrunk_ref.shape[0], body)


def expand(packed, expand_matrices, segment_first_row, segment_length):
    rows = packed.shape[1]
    adapters, rank, width = expand_matrices.shape
    table = expand_matrices.reshape(adapters * rank, width)
    return pl.pallas_call(
        expand_body,
        grid_spec=pltpu.PrefetchScalarGridSpec(
            num_scalar_prefetch=2,
            grid=(adapters // TOGETHER,),
            in_specs=[
                pl.BlockSpec((rank, rows), lambda group, *_: (0, 0)),
                pl.BlockSpec((TOGETHER * rank, width), lambda group, *_: (group, 0)),
            ],
            out_specs=pl.BlockSpec((rows, width), lambda group, *_: (0, 0)),
            scratch_shapes=[pltpu.VMEM((rows, rank), jnp.bfloat16)],
        ),
        out_shape=jax.ShapeDtypeStruct((rows, width), jnp.float32),
        compiler_params=pltpu.CompilerParams(vmem_limit_bytes=VMEM_LIMIT),
        cost_estimate=pl.CostEstimate(flops=EXPAND_FLOPS, bytes_accessed=1, transcendentals=0),
    )(segment_first_row, segment_length, packed, table)


def on_device(
    total,
    hidden,
    down_matrix,
    shrink_matrices,
    expand_matrices,
    row_adapter_index,
    segment_first_row,
    segment_length,
):
    me = lax.axis_index("tensor").astype(jnp.int32)
    width = down_matrix.shape[1] // total
    core, near = 1, 2
    units = total // 4

    kept_home, crossed, incoming = {}, {}, {}

    packed, steps = None, [near, *(4 << at for at in range((units - 1).bit_length())), core]

    def settle(unit, arrived):
        value = kept_home[unit] + arrived.astype(jnp.float32) + crossed[unit].astype(jnp.float32)
        for moved in incoming.pop(unit, []):
            value = value + moved.astype(jnp.float32)
        return value.astype(jnp.bfloat16) if unit else value

    def send_on(unit, moving):
        bit = unit & -unit
        incoming.setdefault(unit ^ bit, []).append(swap(moving, 4 * bit, total))
        return moving

    top = units - 1
    order = [top * 4 | near | core]
    for unit in reversed(range(units)):
        order += [(unit - 1) * 4 | near | core] * (unit > 0) + [unit * 4 | core, unit * 4 | near]
        order += [(unit + 1) * 4] * (unit < top) + [0] * (not unit)
    table = jnp.array(order, dtype=jnp.int32) ^ me

    values, _, buffer = product(table, hidden, down_matrix, None, 0, 1, 0, width, False, FLOPS, [])
    base, ready = 1, []
    for unit in reversed(range(units)):
        arrived = swap(values, core, total)
        sent, kept = 1 + (unit > 0), 1 + (unit < top) + (not unit)
        values, results, buffer = product(
            table, hidden, down_matrix, buffer, base, sent, kept, width, not unit,
            FIRST_FLOPS if unit == top - 1 else FLOPS, ready,
        )
        base += sent + kept
        if packed is not None and steps and steps[0] != core:
            moved, results = lax.optimization_barrier((swap(packed, steps.pop(0), total), results))
            packed = packed + moved
        if unit < top:
            kept_home[unit + 1] = results[1]
        if not unit:
            kept_home[0] = results[-1]
        ready = []
        if unit < top:
            moving, arrived = lax.optimization_barrier((settle(unit + 1, arrived[1]), arrived))
            ready.append(send_on(unit + 1, moving))
        leaving = (results[0] + arrived[0].astype(jnp.float32)).astype(jnp.bfloat16)
        if unit == max(top - 1, 0):
            late, results = lax.optimization_barrier((hidden, results))
            packed = shrink(late, shrink_matrices, row_adapter_index)
        ready.append(leaving)
        if packed is not None:
            ready.append(packed)
        crossed[unit] = swap(leaving, near, total)
    kept = [settle(0, swap(values, core, total)[0])]

    for bit in steps:
        kind = jnp.bfloat16 if bit > near else jnp.float32
        packed = packed + swap(packed.astype(kind), bit, total).astype(jnp.float32)
    adapter_output = expand(packed, expand_matrices, segment_first_row, segment_length)
    return (kept[0] + adapter_output).astype(jnp.bfloat16)


def solution(mesh):
    in_specs = (
        P("groups", "tensor"),
        P("tensor", None),
        P(None, "tensor", None),
        P(None, None, "tensor"),
        P("groups"),
        P("groups"),
        P("groups"),
    )
    out_specs = P("groups", "tensor")
    return jax.shard_map(
        functools.partial(on_device, mesh.shape["tensor"]),
        mesh=mesh,
        in_specs=in_specs,
        out_specs=out_specs,
        check_vma=False,
    )
```

```python
import functools

import jax
import jax.numpy as jnp
from jax import lax
from jax.experimental import pallas as pl
from jax.experimental.pallas import tpu as pltpu
from jax.sharding import PartitionSpec as P

VMEM_LIMIT = 39 * 1024 * 1024
WINDOW = 128
TOGETHER = 4
FLOPS = 3_000_000_000
EXPAND_FLOPS = 1_000_000


def product_body(table_ref, hidden_ref, down_ref, *refs, base, sent, kept, first, last, earlier):
    sent_ref = kept_ref = None
    refs = list(refs[earlier + (0 if first else 1):])
    if sent:
        sent_ref = refs.pop(0)
    if kept:
        kept_ref = refs.pop(0)
    buffer = refs.pop(0)
    arrived = refs.pop()
    width = buffer.shape[2]
    targets = sent + kept

    def copy(at):
        column = pl.multiple_of(table_ref[base + at] * width, width)
        slot = (base + at) % 2
        return pltpu.make_async_copy(
            down_ref.at[:, pl.ds(column, width)], buffer.at[slot], arrived.at[slot]
        )

    if first:
        copy(0).start()

    def step(at, carry):
        @pl.when(at + 1 < targets + (0 if last else 1))
        def _():
            copy(at + 1).start()

        @pl.when(at >= (0 if first else 1))
        def _():
            copy(at).wait()

        total = jnp.dot(
            hidden_ref[...], buffer[(base + at) % 2], preferred_element_type=jnp.float32
        )
        if sent:

            @pl.when(at < sent)
            def _():
                sent_ref[jnp.minimum(at, sent - 1)] = total.astype(jnp.bfloat16)

        if kept:

            @pl.when(at >= sent)
            def _():
                kept_ref[jnp.maximum(at - sent, 0)] = total

        return carry

    lax.fori_loop(0, targets, step, 0)
    if not last:
        copy(targets).wait()


def product(table, hidden, down_matrix, buffer, base, sent, kept, width, last, flops, earlier):
    rows, depth = hidden.shape
    first = buffer is None
    vmem = pl.BlockSpec(memory_space=pltpu.VMEM)
    anywhere = pl.BlockSpec(memory_space=pl.ANY)
    out_shape = []
    if sent:
        out_shape.append(jax.ShapeDtypeStruct((sent, rows, width), jnp.bfloat16))
    if kept:
        out_shape.append(jax.ShapeDtypeStruct((kept, rows, width), jnp.float32))
    place = len(out_shape)
    out_shape.append(jax.ShapeDtypeStruct((2, depth, width), jnp.bfloat16))
    results = pl.pallas_call(
        functools.partial(
            product_body, base=base, sent=sent, kept=kept, first=first, last=last,
            earlier=len(earlier),
        ),
        in_specs=[
            pl.BlockSpec(memory_space=pltpu.SMEM),
            vmem,
            pl.BlockSpec(memory_space=pltpu.HBM),
        ]
        + ([] if first else [vmem])
        + [anywhere] * len(earlier),
        out_specs=[vmem] * len(out_shape),
        out_shape=out_shape,
        scratch_shapes=[pltpu.SemaphoreType.DMA((2,))],
        input_output_aliases={} if first else {3: place},
        compiler_params=pltpu.CompilerParams(vmem_limit_bytes=VMEM_LIMIT),
        cost_estimate=pl.CostEstimate(flops=flops, bytes_accessed=1024, transcendentals=0),
    )(table, hidden, down_matrix, *([] if first else [buffer]), *earlier)
    return results[0] if sent else None, results[place - 1] if kept else None, results[place]


def swap(value, bit, total):
    return lax.ppermute(value, "tensor", [(place, place ^ bit) for place in range(total)])


def for_each_window(first_ref, length_ref, group, rows, body):
    window = min(WINDOW, rows)
    adapters = [group * TOGETHER + at for at in range(TOGETHER)]
    begins = [first_ref[adapter] for adapter in adapters]
    ends = [first_ref[adapter] + length_ref[adapter] for adapter in adapters]
    base = begins[0] // 16 * 16

    def step(at, carry):
        low = base + at * window
        start = pl.multiple_of(jnp.minimum(low, rows - window), 16)
        places = start + lax.broadcasted_iota(jnp.int32, (window, 1), 0)
        masks = [
            (places >= jnp.maximum(begin, low)) & (places < end) for begin, end in zip(begins, ends)
        ]
        body(pl.ds(start, window), masks)
        return carry

    lax.fori_loop(0, (ends[-1] - base + window - 1) // window, step, 0)


def shrink(hidden, shrink_matrices, row_adapter_index):
    adapters = shrink_matrices.shape[0]
    every_adapter = jnp.einsum(
        "hq,gqu->hgu", hidden, shrink_matrices, preferred_element_type=jnp.float32
    )
    picked = row_adapter_index[:, None] == jnp.arange(adapters, dtype=jnp.int32)[None, :]
    partial = jnp.sum(jnp.where(picked[:, :, None], every_adapter, 0.0), axis=1)
    return jnp.swapaxes(partial, 0, 1)


def expand_body(first_ref, length_ref, packed_ref, table_ref, result_ref, shrunk_ref):
    rows, rank = shrunk_ref.shape
    span = TOGETHER * rank
    shrunk_ref[...] = packed_ref[...].T.astype(jnp.bfloat16)
    result_ref[...] = jnp.zeros_like(result_ref)

    def step(group, carry):
        def body(window, masks):
            shrunk = shrunk_ref[window, :]
            spread = [jnp.where(mask, shrunk, jnp.zeros((), jnp.bfloat16)) for mask in masks]
            part = jnp.dot(
                jnp.concatenate(spread, axis=1),
                table_ref[pl.ds(pl.multiple_of(group * span, span), span), :],
                preferred_element_type=jnp.float32,
            )
            result_ref[window, :] = result_ref[window, :] + part

        for_each_window(first_ref, length_ref, group, rows, body)
        return carry

    lax.fori_loop(0, table_ref.shape[0] // span, step, 0)


def expand(packed, expand_matrices, segment_first_row, segment_length):
    rows = packed.shape[1]
    adapters, rank, width = expand_matrices.shape
    table = expand_matrices.reshape(adapters * rank, width)
    vmem = pl.BlockSpec(memory_space=pltpu.VMEM)
    return pl.pallas_call(
        expand_body,
        in_specs=[pl.BlockSpec(memory_space=pltpu.SMEM)] * 2 + [vmem] * 2,
        out_specs=vmem,
        out_shape=jax.ShapeDtypeStruct((rows, width), jnp.float32),
        scratch_shapes=[pltpu.VMEM((rows, rank), jnp.bfloat16)],
        compiler_params=pltpu.CompilerParams(vmem_limit_bytes=VMEM_LIMIT),
        cost_estimate=pl.CostEstimate(flops=EXPAND_FLOPS, bytes_accessed=1, transcendentals=0),
    )(segment_first_row, segment_length, packed, table)


def on_device(
    total,
    hidden,
    down_matrix,
    shrink_matrices,
    expand_matrices,
    row_adapter_index,
    segment_first_row,
    segment_length,
):
    me = lax.axis_index("tensor").astype(jnp.int32)
    width = down_matrix.shape[1] // total
    core, near = 1, 2
    units = total // 4

    kept_home, crossed, incoming = {}, {}, {}

    packed, steps = None, [core, *(4 << at for at in range((units - 1).bit_length())), near]

    def settle(unit, arrived):
        value = kept_home[unit] + arrived.astype(jnp.float32) + crossed[unit].astype(jnp.float32)
        for moved in incoming.pop(unit, []):
            value = value + moved.astype(jnp.float32)
        return value.astype(jnp.bfloat16) if unit else value

    def send_on(unit, moving):
        bit = unit & -unit
        incoming.setdefault(unit ^ bit, []).append(swap(moving, 4 * bit, total))
        return moving

    top = units - 1
    order = [top * 4 | near | core]
    for unit in reversed(range(units)):
        order += [(unit - 1) * 4 | near | core] * (unit > 0) + [unit * 4 | core, unit * 4 | near]
        order += [(unit + 1) * 4] * (unit < top) + [0] * (not unit)
    table = jnp.array(order, dtype=jnp.int32) ^ me

    values, _, buffer = product(table, hidden, down_matrix, None, 0, 1, 0, width, False, FLOPS, [])
    base, ready = 1, []
    for unit in reversed(range(units)):
        arrived = swap(values, core, total)
        sent, kept = 1 + (unit > 0), 1 + (unit < top) + (not unit)
        values, results, buffer = product(
            table, hidden, down_matrix, buffer, base, sent, kept, width, not unit,
            FLOPS, ready,
        )
        base += sent + kept
        if packed is not None and steps and steps[0] != near:
            moved, results = lax.optimization_barrier((swap(packed, steps.pop(0), total), results))
            packed = packed + moved
        if unit < top:
            kept_home[unit + 1] = results[1]
        if not unit:
            kept_home[0] = results[-1]
        ready = []
        if unit < top:
            moving, arrived = lax.optimization_barrier((settle(unit + 1, arrived[1]), arrived))
            ready.append(send_on(unit + 1, moving))
        leaving = (results[0] + arrived[0].astype(jnp.float32)).astype(jnp.bfloat16)
        if unit == max(top - 1, 0):
            late, results = lax.optimization_barrier((hidden, results))
            packed = shrink(late, shrink_matrices, row_adapter_index)
        ready.append(leaving)
        if packed is not None:
            ready.append(packed)
        crossed[unit] = swap(leaving, near, total)
    kept = [settle(0, swap(values, core, total)[0])]

    for bit in steps:
        kind = jnp.bfloat16 if bit > near else jnp.float32
        packed = packed + swap(packed.astype(kind), bit, total).astype(jnp.float32)
    adapter_output = expand(packed, expand_matrices, segment_first_row, segment_length)
    return (kept[0] + adapter_output).astype(jnp.bfloat16)


def solution(mesh):
    in_specs = (
        P("groups", "tensor"),
        P("tensor", None),
        P(None, "tensor", None),
        P(None, None, "tensor"),
        P("groups"),
        P("groups"),
        P("groups"),
    )
    out_specs = P("groups", "tensor")
    return jax.shard_map(
        functools.partial(on_device, mesh.shape["tensor"]),
        mesh=mesh,
        in_specs=in_specs,
        out_specs=out_specs,
        check_vma=False,
    )
```

```python
import functools

import jax
import jax.numpy as jnp
from jax import lax
from jax.experimental import pallas as pl
from jax.experimental.pallas import tpu as pltpu
from jax.sharding import PartitionSpec as P

VMEM_LIMIT = 39 * 1024 * 1024
WINDOW = 128
TOGETHER = 4
FLOPS = 3_000_000_000
EXPAND_FLOPS = 1_000_000


def product_body(table_ref, hidden_ref, down_ref, *refs, base, sent, kept, first, last, earlier):
    sent_ref = kept_ref = None
    refs = list(refs[earlier + (0 if first else 1):])
    if sent:
        sent_ref = refs.pop(0)
    if kept:
        kept_ref = refs.pop(0)
    buffer = refs.pop(0)
    arrived = refs.pop()
    width = buffer.shape[2]
    targets = sent + kept

    def copy(at):
        column = pl.multiple_of(table_ref[base + at] * width, width)
        slot = (base + at) % 2
        return pltpu.make_async_copy(
            down_ref.at[:, pl.ds(column, width)], buffer.at[slot], arrived.at[slot]
        )

    if first:
        copy(0).start()

    def step(at, carry):
        @pl.when(at + 1 < targets + (0 if last else 1))
        def _():
            copy(at + 1).start()

        @pl.when(at >= (0 if first else 1))
        def _():
            copy(at).wait()

        total = jnp.dot(
            hidden_ref[...], buffer[(base + at) % 2], preferred_element_type=jnp.float32
        )
        if sent:

            @pl.when(at < sent)
            def _():
                sent_ref[jnp.minimum(at, sent - 1)] = total.astype(jnp.bfloat16)

        if kept:

            @pl.when(at >= sent)
            def _():
                kept_ref[jnp.maximum(at - sent, 0)] = total

        return carry

    lax.fori_loop(0, targets, step, 0)
    if not last:
        copy(targets).wait()


def product(table, hidden, down_matrix, buffer, base, sent, kept, width, last, flops, earlier):
    rows, depth = hidden.shape
    first = buffer is None
    vmem = pl.BlockSpec(memory_space=pltpu.VMEM)
    anywhere = pl.BlockSpec(memory_space=pl.ANY)
    out_shape = []
    if sent:
        out_shape.append(jax.ShapeDtypeStruct((sent, rows, width), jnp.bfloat16))
    if kept:
        out_shape.append(jax.ShapeDtypeStruct((kept, rows, width), jnp.float32))
    place = len(out_shape)
    out_shape.append(jax.ShapeDtypeStruct((2, depth, width), jnp.bfloat16))
    results = pl.pallas_call(
        functools.partial(
            product_body, base=base, sent=sent, kept=kept, first=first, last=last,
            earlier=len(earlier),
        ),
        in_specs=[
            pl.BlockSpec(memory_space=pltpu.SMEM),
            vmem,
            pl.BlockSpec(memory_space=pltpu.HBM),
        ]
        + ([] if first else [vmem])
        + [anywhere] * len(earlier),
        out_specs=[vmem] * len(out_shape),
        out_shape=out_shape,
        scratch_shapes=[pltpu.SemaphoreType.DMA((2,))],
        input_output_aliases={} if first else {3: place},
        compiler_params=pltpu.CompilerParams(vmem_limit_bytes=VMEM_LIMIT),
        cost_estimate=pl.CostEstimate(flops=flops, bytes_accessed=1024, transcendentals=0),
    )(table, hidden, down_matrix, *([] if first else [buffer]), *earlier)
    return results[0] if sent else None, results[place - 1] if kept else None, results[place]


def swap(value, bit, total):
    return lax.ppermute(value, "tensor", [(place, place ^ bit) for place in range(total)])


def for_each_window(first_ref, length_ref, group, rows, body):
    window = min(WINDOW, rows)
    adapters = [group * TOGETHER + at for at in range(TOGETHER)]
    begins = [first_ref[adapter] for adapter in adapters]
    ends = [first_ref[adapter] + length_ref[adapter] for adapter in adapters]
    base = begins[0] // 16 * 16

    def step(at, carry):
        low = base + at * window
        start = pl.multiple_of(jnp.minimum(low, rows - window), 16)
        places = start + lax.broadcasted_iota(jnp.int32, (window, 1), 0)
        masks = [
            (places >= jnp.maximum(begin, low)) & (places < end) for begin, end in zip(begins, ends)
        ]
        body(pl.ds(start, window), masks)
        return carry

    lax.fori_loop(0, (ends[-1] - base + window - 1) // window, step, 0)


def shrink(hidden, shrink_matrices, row_adapter_index):
    adapters = shrink_matrices.shape[0]
    every_adapter = jnp.einsum(
        "hq,gqu->hgu", hidden, shrink_matrices, preferred_element_type=jnp.float32
    )
    picked = row_adapter_index[:, None] == jnp.arange(adapters, dtype=jnp.int32)[None, :]
    partial = jnp.sum(jnp.where(picked[:, :, None], every_adapter, 0.0), axis=1)
    return jnp.swapaxes(partial, 0, 1)


def expand_body(first_ref, length_ref, packed_ref, table_ref, result_ref, shrunk_ref):
    rows, rank = shrunk_ref.shape
    span = TOGETHER * rank
    shrunk_ref[...] = packed_ref[...].T.astype(jnp.bfloat16)
    result_ref[...] = jnp.zeros_like(result_ref)

    def step(group, carry):
        def body(window, masks):
            shrunk = shrunk_ref[window, :]
            spread = [jnp.where(mask, shrunk, jnp.zeros((), jnp.bfloat16)) for mask in masks]
            part = jnp.dot(
                jnp.concatenate(spread, axis=1),
                table_ref[pl.ds(pl.multiple_of(group * span, span), span), :],
                preferred_element_type=jnp.float32,
            )
            result_ref[window, :] = result_ref[window, :] + part

        for_each_window(first_ref, length_ref, group, rows, body)
        return carry

    lax.fori_loop(0, table_ref.shape[0] // span, step, 0)


def expand(packed, expand_matrices, segment_first_row, segment_length):
    rows = packed.shape[1]
    adapters, rank, width = expand_matrices.shape
    table = expand_matrices.reshape(adapters * rank, width)
    vmem = pl.BlockSpec(memory_space=pltpu.VMEM)
    return pl.pallas_call(
        expand_body,
        in_specs=[pl.BlockSpec(memory_space=pltpu.SMEM)] * 2 + [vmem] * 2,
        out_specs=vmem,
        out_shape=jax.ShapeDtypeStruct((rows, width), jnp.float32),
        scratch_shapes=[pltpu.VMEM((rows, rank), jnp.bfloat16)],
        compiler_params=pltpu.CompilerParams(vmem_limit_bytes=VMEM_LIMIT),
        cost_estimate=pl.CostEstimate(flops=EXPAND_FLOPS, bytes_accessed=1, transcendentals=0),
    )(segment_first_row, segment_length, packed, table)


def on_device(
    total,
    hidden,
    down_matrix,
    shrink_matrices,
    expand_matrices,
    row_adapter_index,
    segment_first_row,
    segment_length,
):
    me = lax.axis_index("tensor").astype(jnp.int32)
    width = down_matrix.shape[1] // total
    core, near = 1, 2
    units = total // 4

    kept_home, crossed, incoming = {}, {}, {}

    packed, steps = None, [core, *(4 << at for at in reversed(range((units - 1).bit_length()))), near]

    def step(value, bit):
        return swap(value.astype(jnp.bfloat16 if bit > near else jnp.float32), bit, total)

    def settle(unit, arrived):
        value = kept_home[unit] + arrived.astype(jnp.float32) + crossed[unit].astype(jnp.float32)
        for moved in incoming.pop(unit, []):
            value = value + moved.astype(jnp.float32)
        return value.astype(jnp.bfloat16) if unit else value

    def send_on(unit, moving):
        bit = unit & -unit
        incoming.setdefault(unit ^ bit, []).append(swap(moving, 4 * bit, total))
        return moving

    top = units - 1
    order = [top * 4 | near | core]
    for unit in reversed(range(units)):
        order += [(unit - 1) * 4 | near | core] * (unit > 0) + [unit * 4 | core, unit * 4 | near]
        order += [(unit + 1) * 4] * (unit < top) + [0] * (not unit)
    table = jnp.array(order, dtype=jnp.int32) ^ me

    values, _, buffer = product(table, hidden, down_matrix, None, 0, 1, 0, width, False, FLOPS, [])
    base, ready = 1, []
    for unit in reversed(range(units)):
        arrived = swap(values, core, total)
        sent, kept = 1 + (unit > 0), 1 + (unit < top) + (not unit)
        values, results, buffer = product(
            table, hidden, down_matrix, buffer, base, sent, kept, width, not unit,
            FLOPS, ready,
        )
        base += sent + kept
        if packed is not None and steps and steps[0] != near:
            moved, results = lax.optimization_barrier((step(packed, steps.pop(0)), results))
            packed = packed + moved.astype(jnp.float32)
        if unit < top:
            kept_home[unit + 1] = results[1]
        if not unit:
            kept_home[0] = results[-1]
        ready = []
        if unit < top:
            moving, arrived = lax.optimization_barrier((settle(unit + 1, arrived[1]), arrived))
            ready.append(send_on(unit + 1, moving))
        leaving = (results[0] + arrived[0].astype(jnp.float32)).astype(jnp.bfloat16)
        if unit == max(top - 1, 0):
            late, results = lax.optimization_barrier((hidden, results))
            packed = shrink(late, shrink_matrices, row_adapter_index)
        ready.append(leaving)
        if packed is not None:
            ready.append(packed)
        crossed[unit] = swap(leaving, near, total)
    kept = [settle(0, swap(values, core, total)[0])]

    for bit in steps:
        packed = packed + step(packed, bit).astype(jnp.float32)
    adapter_output = expand(packed, expand_matrices, segment_first_row, segment_length)
    return (kept[0] + adapter_output).astype(jnp.bfloat16)


def solution(mesh):
    in_specs = (
        P("groups", "tensor"),
        P("tensor", None),
        P(None, "tensor", None),
        P(None, None, "tensor"),
        P("groups"),
        P("groups"),
        P("groups"),
    )
    out_specs = P("groups", "tensor")
    return jax.shard_map(
        functools.partial(on_device, mesh.shape["tensor"]),
        mesh=mesh,
        in_specs=in_specs,
        out_specs=out_specs,
        check_vma=False,
    )
```

```python
import functools

import jax
import jax.numpy as jnp
from jax import lax
from jax.experimental import pallas as pl
from jax.experimental.pallas import tpu as pltpu
from jax.sharding import PartitionSpec as P

VMEM_LIMIT = 39 * 1024 * 1024
WINDOW = 128
TOGETHER = 4
FLOPS = 3_000_000_000
EXPAND_FLOPS = 1_000_000


def product_body(table_ref, hidden_ref, down_ref, *refs, base, sent, kept, first, last, earlier):
    sent_ref = kept_ref = None
    refs = list(refs[earlier + (0 if first else 1):])
    if sent:
        sent_ref = refs.pop(0)
    if kept:
        kept_ref = refs.pop(0)
    buffer = refs.pop(0)
    arrived = refs.pop()
    width = buffer.shape[2]
    targets = sent + kept

    def copy(at):
        column = pl.multiple_of(table_ref[base + at] * width, width)
        slot = (base + at) % 2
        return pltpu.make_async_copy(
            down_ref.at[:, pl.ds(column, width)], buffer.at[slot], arrived.at[slot]
        )

    if first:
        copy(0).start()

    def step(at, carry):
        @pl.when(at + 1 < targets + (0 if last else 1))
        def _():
            copy(at + 1).start()

        @pl.when(at >= (0 if first else 1))
        def _():
            copy(at).wait()

        total = jnp.dot(
            hidden_ref[...], buffer[(base + at) % 2], preferred_element_type=jnp.float32
        )
        if sent:

            @pl.when(at < sent)
            def _():
                sent_ref[jnp.minimum(at, sent - 1)] = total.astype(jnp.bfloat16)

        if kept:

            @pl.when(at >= sent)
            def _():
                kept_ref[jnp.maximum(at - sent, 0)] = total

        return carry

    lax.fori_loop(0, targets, step, 0)
    if not last:
        copy(targets).wait()


def product(table, hidden, down_matrix, buffer, base, sent, kept, width, last, earlier):
    rows, depth = hidden.shape
    first = buffer is None
    vmem = pl.BlockSpec(memory_space=pltpu.VMEM)
    anywhere = pl.BlockSpec(memory_space=pl.ANY)
    out_shape = []
    if sent:
        out_shape.append(jax.ShapeDtypeStruct((sent, rows, width), jnp.bfloat16))
    if kept:
        out_shape.append(jax.ShapeDtypeStruct((kept, rows, width), jnp.float32))
    place = len(out_shape)
    out_shape.append(jax.ShapeDtypeStruct((2, depth, width), jnp.bfloat16))
    results = pl.pallas_call(
        functools.partial(
            product_body, base=base, sent=sent, kept=kept, first=first, last=last,
            earlier=len(earlier),
        ),
        in_specs=[
            pl.BlockSpec(memory_space=pltpu.SMEM),
            vmem,
            pl.BlockSpec(memory_space=pltpu.HBM),
        ]
        + ([] if first else [vmem])
        + [anywhere] * len(earlier),
        out_specs=[vmem] * len(out_shape),
        out_shape=out_shape,
        scratch_shapes=[pltpu.SemaphoreType.DMA((2,))],
        input_output_aliases={} if first else {3: place},
        compiler_params=pltpu.CompilerParams(vmem_limit_bytes=VMEM_LIMIT),
        cost_estimate=pl.CostEstimate(flops=FLOPS, bytes_accessed=1024, transcendentals=0),
    )(table, hidden, down_matrix, *([] if first else [buffer]), *earlier)
    return results[0] if sent else None, results[place - 1] if kept else None, results[place]


def swap(value, bit, total):
    return lax.ppermute(value, "tensor", [(place, place ^ bit) for place in range(total)])


def attach(value, packed):
    below = jnp.pad(packed.astype(jnp.bfloat16), ((0, 0), (0, value.shape[1] - packed.shape[1])))
    return jnp.concatenate([value, below])


def detach(value, packed):
    height, columns = packed.shape
    above = value.shape[0] - height
    return value[:above], value[above:, :columns].astype(jnp.float32)


def for_each_window(first_ref, length_ref, group, rows, body):
    window = min(WINDOW, rows)
    adapters = [group * TOGETHER + at for at in range(TOGETHER)]
    begins = [first_ref[adapter] for adapter in adapters]
    ends = [first_ref[adapter] + length_ref[adapter] for adapter in adapters]
    base = begins[0] // 16 * 16

    def step(at, carry):
        low = base + at * window
        start = pl.multiple_of(jnp.minimum(low, rows - window), 16)
        places = start + lax.broadcasted_iota(jnp.int32, (window, 1), 0)
        masks = [
            (places >= jnp.maximum(begin, low)) & (places < end) for begin, end in zip(begins, ends)
        ]
        body(pl.ds(start, window), masks)
        return carry

    lax.fori_loop(0, (ends[-1] - base + window - 1) // window, step, 0)


def shrink(hidden, shrink_matrices, row_adapter_index):
    adapters = shrink_matrices.shape[0]
    every_adapter = jnp.einsum(
        "hq,gqu->hgu", hidden, shrink_matrices, preferred_element_type=jnp.float32
    )
    picked = row_adapter_index[:, None] == jnp.arange(adapters, dtype=jnp.int32)[None, :]
    partial = jnp.sum(jnp.where(picked[:, :, None], every_adapter, 0.0), axis=1)
    return jnp.swapaxes(partial, 0, 1)


def expand_body(first_ref, length_ref, packed_ref, table_ref, result_ref, shrunk_ref):
    rows, rank = shrunk_ref.shape
    span = TOGETHER * rank
    shrunk_ref[...] = packed_ref[...].T.astype(jnp.bfloat16)
    result_ref[...] = jnp.zeros_like(result_ref)

    def step(group, carry):
        def body(window, masks):
            shrunk = shrunk_ref[window, :]
            spread = [jnp.where(mask, shrunk, jnp.zeros((), jnp.bfloat16)) for mask in masks]
            part = jnp.dot(
                jnp.concatenate(spread, axis=1),
                table_ref[pl.ds(pl.multiple_of(group * span, span), span), :],
                preferred_element_type=jnp.float32,
            )
            result_ref[window, :] = result_ref[window, :] + part

        for_each_window(first_ref, length_ref, group, rows, body)
        return carry

    lax.fori_loop(0, table_ref.shape[0] // span, step, 0)


def expand(packed, expand_matrices, segment_first_row, segment_length):
    rows = packed.shape[1]
    adapters, rank, width = expand_matrices.shape
    table = expand_matrices.reshape(adapters * rank, width)
    vmem = pl.BlockSpec(memory_space=pltpu.VMEM)
    return pl.pallas_call(
        expand_body,
        in_specs=[pl.BlockSpec(memory_space=pltpu.SMEM)] * 2 + [vmem] * 2,
        out_specs=vmem,
        out_shape=jax.ShapeDtypeStruct((rows, width), jnp.float32),
        scratch_shapes=[pltpu.VMEM((rows, rank), jnp.bfloat16)],
        compiler_params=pltpu.CompilerParams(vmem_limit_bytes=VMEM_LIMIT),
        cost_estimate=pl.CostEstimate(flops=EXPAND_FLOPS, bytes_accessed=1, transcendentals=0),
    )(segment_first_row, segment_length, packed, table)


def on_device(
    total,
    hidden,
    down_matrix,
    shrink_matrices,
    expand_matrices,
    row_adapter_index,
    segment_first_row,
    segment_length,
):
    me = lax.axis_index("tensor").astype(jnp.int32)
    width = down_matrix.shape[1] // total
    core, near = 1, 2
    units = total // 4

    kept_home, crossed, incoming = {}, {}, {}

    far = [4 << at for at in range((units - 1).bit_length())]
    packed, steps = None, [*far[:1], near, *far[1:], core]

    def send(value, bit):
        nonlocal packed
        if packed is None or steps[:1] != [bit] or packed.shape[1] > value.shape[1]:
            return value, swap(value, bit, total), None
        steps.pop(0)
        own, packed = packed, None
        leaving = attach(value, own)
        arrived, shrinks = detach(swap(leaving, bit, total), own)
        return leaving, arrived, own + shrinks

    def settle(unit, arrived):
        nonlocal packed
        value = kept_home[unit] + arrived.astype(jnp.float32) + crossed[unit].astype(jnp.float32)
        for moved, shrinks in incoming.pop(unit, []):
            value = value + moved.astype(jnp.float32)
            packed = packed if shrinks is None else shrinks
        return value.astype(jnp.bfloat16) if unit else value

    top = units - 1
    order = [top * 4 | near | core]
    for unit in reversed(range(units)):
        order += [(unit - 1) * 4 | near | core] * (unit > 0) + [unit * 4 | core, unit * 4 | near]
        order += [(unit + 1) * 4] * (unit < top) + [0] * (not unit)
    table = jnp.array(order, dtype=jnp.int32) ^ me

    values, _, buffer = product(table, hidden, down_matrix, None, 0, 1, 0, width, False, [])
    base, ready = 1, []
    for unit in reversed(range(units)):
        arrived = swap(values, core, total)
        sent, kept = 1 + (unit > 0), 1 + (unit < top) + (not unit)
        values, results, buffer = product(
            table, hidden, down_matrix, buffer, base, sent, kept, width, not unit,
            ready,
        )
        base += sent + kept
        if unit < top:
            kept_home[unit + 1] = results[1]
        if not unit:
            kept_home[0] = results[-1]
        if unit == max(top - 1, 0):
            late, results = lax.optimization_barrier((hidden, results))
            packed = shrink(late, shrink_matrices, row_adapter_index)
        ready = []
        if unit < top:
            moving, arrived = lax.optimization_barrier((settle(unit + 1, arrived[1]), arrived))
            bit = (unit + 1) & -(unit + 1)
            moving, *came = send(moving, 4 * bit)
            incoming.setdefault((unit + 1) ^ bit, []).append(came)
            ready.append(moving)
        leaving = (results[0] + arrived[0].astype(jnp.float32)).astype(jnp.bfloat16)
        leaving, crossed[unit], shrinks = send(leaving, near)
        packed = packed if shrinks is None else shrinks
        ready.append(leaving)
    kept = [settle(0, swap(values, core, total)[0])]

    for bit in steps:
        kind = jnp.bfloat16 if bit > near else jnp.float32
        packed = packed + swap(packed.astype(kind), bit, total).astype(jnp.float32)
    adapter_output = expand(packed, expand_matrices, segment_first_row, segment_length)
    return (kept[0] + adapter_output).astype(jnp.bfloat16)


def solution(mesh):
    in_specs = (
        P("groups", "tensor"),
        P("tensor", None),
        P(None, "tensor", None),
        P(None, None, "tensor"),
        P("groups"),
        P("groups"),
        P("groups"),
    )
    out_specs = P("groups", "tensor")
    return jax.shard_map(
        functools.partial(on_device, mesh.shape["tensor"]),
        mesh=mesh,
        in_specs=in_specs,
        out_specs=out_specs,
        check_vma=False,
    )
```

```python
import functools

import jax
import jax.numpy as jnp
from jax import lax
from jax.experimental import pallas as pl
from jax.experimental.pallas import tpu as pltpu
from jax.sharding import PartitionSpec as P

VMEM_LIMIT = 39 * 1024 * 1024
WINDOW = 128
TOGETHER = 4
FLOPS = 20_000_000_000
EXPAND_FLOPS = 1_000_000


def product_body(table_ref, hidden_ref, down_ref, *refs, base, sent, kept, first, last, earlier):
    sent_ref = kept_ref = None
    refs = list(refs[earlier + (0 if first else 1):])
    if sent:
        sent_ref = refs.pop(0)
    if kept:
        kept_ref = refs.pop(0)
    buffer = refs.pop(0)
    arrived = refs.pop()
    width = buffer.shape[2]
    targets = sent + kept

    def copy(at):
        column = pl.multiple_of(table_ref[base + at] * width, width)
        slot = (base + at) % 2
        return pltpu.make_async_copy(
            down_ref.at[:, pl.ds(column, width)], buffer.at[slot], arrived.at[slot]
        )

    if first:
        copy(0).start()

    def step(at, carry):
        @pl.when(at + 1 < targets + (0 if last else 1))
        def _():
            copy(at + 1).start()

        @pl.when(at >= (0 if first else 1))
        def _():
            copy(at).wait()

        total = jnp.dot(
            hidden_ref[...], buffer[(base + at) % 2], preferred_element_type=jnp.float32
        )
        if sent:

            @pl.when(at < sent)
            def _():
                sent_ref[jnp.minimum(at, sent - 1)] = total.astype(jnp.bfloat16)

        if kept:

            @pl.when(at >= sent)
            def _():
                kept_ref[jnp.maximum(at - sent, 0)] = total

        return carry

    lax.fori_loop(0, targets, step, 0)
    if not last:
        copy(targets).wait()


def product(table, hidden, down_matrix, buffer, base, sent, kept, width, last, earlier):
    rows, depth = hidden.shape
    first = buffer is None
    vmem = pl.BlockSpec(memory_space=pltpu.VMEM)
    anywhere = pl.BlockSpec(memory_space=pl.ANY)
    out_shape = []
    if sent:
        out_shape.append(jax.ShapeDtypeStruct((sent, rows, width), jnp.bfloat16))
    if kept:
        out_shape.append(jax.ShapeDtypeStruct((kept, rows, width), jnp.float32))
    place = len(out_shape)
    out_shape.append(jax.ShapeDtypeStruct((2, depth, width), jnp.bfloat16))
    results = pl.pallas_call(
        functools.partial(
            product_body, base=base, sent=sent, kept=kept, first=first, last=last,
            earlier=len(earlier),
        ),
        in_specs=[
            pl.BlockSpec(memory_space=pltpu.SMEM),
            vmem,
            pl.BlockSpec(memory_space=pltpu.HBM),
        ]
        + ([] if first else [vmem])
        + [anywhere] * len(earlier),
        out_specs=[vmem] * len(out_shape),
        out_shape=out_shape,
        scratch_shapes=[pltpu.SemaphoreType.DMA((2,))],
        input_output_aliases={} if first else {3: place},
        compiler_params=pltpu.CompilerParams(vmem_limit_bytes=VMEM_LIMIT),
        cost_estimate=pl.CostEstimate(flops=FLOPS, bytes_accessed=1024, transcendentals=0),
    )(table, hidden, down_matrix, *([] if first else [buffer]), *earlier)
    return results[0] if sent else None, results[place - 1] if kept else None, results[place]


def swap(value, bit, total):
    return lax.ppermute(value, "tensor", [(place, place ^ bit) for place in range(total)])


def attach(value, packed):
    below = jnp.pad(packed.astype(jnp.bfloat16), ((0, 0), (0, value.shape[1] - packed.shape[1])))
    return jnp.concatenate([value, below])


def detach(value, packed):
    height, columns = packed.shape
    above = value.shape[0] - height
    return value[:above], value[above:, :columns].astype(jnp.float32)


def for_each_window(first_ref, length_ref, group, rows, body):
    window = min(WINDOW, rows)
    adapters = [group * TOGETHER + at for at in range(TOGETHER)]
    begins = [first_ref[adapter] for adapter in adapters]
    ends = [first_ref[adapter] + length_ref[adapter] for adapter in adapters]
    base = begins[0] // 16 * 16

    def step(at, carry):
        low = base + at * window
        start = pl.multiple_of(jnp.minimum(low, rows - window), 16)
        places = start + lax.broadcasted_iota(jnp.int32, (window, 1), 0)
        masks = [
            (places >= jnp.maximum(begin, low)) & (places < end) for begin, end in zip(begins, ends)
        ]
        body(pl.ds(start, window), masks)
        return carry

    lax.fori_loop(0, (ends[-1] - base + window - 1) // window, step, 0)


def shrink(hidden, shrink_matrices, row_adapter_index):
    adapters = shrink_matrices.shape[0]
    every_adapter = jnp.einsum(
        "hq,gqu->hgu", hidden, shrink_matrices, preferred_element_type=jnp.float32
    )
    picked = row_adapter_index[:, None] == jnp.arange(adapters, dtype=jnp.int32)[None, :]
    partial = jnp.sum(jnp.where(picked[:, :, None], every_adapter, 0.0), axis=1)
    return jnp.swapaxes(partial, 0, 1)


def expand_body(first_ref, length_ref, packed_ref, table_ref, result_ref, shrunk_ref):
    rows, rank = shrunk_ref.shape
    span = TOGETHER * rank
    shrunk_ref[...] = packed_ref[...].T.astype(jnp.bfloat16)
    result_ref[...] = jnp.zeros_like(result_ref)

    def step(group, carry):
        def body(window, masks):
            shrunk = shrunk_ref[window, :]
            spread = [jnp.where(mask, shrunk, jnp.zeros((), jnp.bfloat16)) for mask in masks]
            part = jnp.dot(
                jnp.concatenate(spread, axis=1),
                table_ref[pl.ds(pl.multiple_of(group * span, span), span), :],
                preferred_element_type=jnp.float32,
            )
            result_ref[window, :] = result_ref[window, :] + part

        for_each_window(first_ref, length_ref, group, rows, body)
        return carry

    lax.fori_loop(0, table_ref.shape[0] // span, step, 0)


def expand(packed, expand_matrices, segment_first_row, segment_length):
    rows = packed.shape[1]
    adapters, rank, width = expand_matrices.shape
    table = expand_matrices.reshape(adapters * rank, width)
    vmem = pl.BlockSpec(memory_space=pltpu.VMEM)
    return pl.pallas_call(
        expand_body,
        in_specs=[pl.BlockSpec(memory_space=pltpu.SMEM)] * 2 + [vmem] * 2,
        out_specs=vmem,
        out_shape=jax.ShapeDtypeStruct((rows, width), jnp.float32),
        scratch_shapes=[pltpu.VMEM((rows, rank), jnp.bfloat16)],
        compiler_params=pltpu.CompilerParams(vmem_limit_bytes=VMEM_LIMIT),
        cost_estimate=pl.CostEstimate(flops=EXPAND_FLOPS, bytes_accessed=1, transcendentals=0),
    )(segment_first_row, segment_length, packed, table)


def on_device(
    total,
    hidden,
    down_matrix,
    shrink_matrices,
    expand_matrices,
    row_adapter_index,
    segment_first_row,
    segment_length,
):
    me = lax.axis_index("tensor").astype(jnp.int32)
    width = down_matrix.shape[1] // total
    core, near = 1, 2
    units = total // 4

    kept_home, crossed, incoming = {}, {}, {}

    far = [4 << at for at in range((units - 1).bit_length())]
    packed, steps = None, [*far[:1], near, *far[1:], core]

    def send(value, bit):
        nonlocal packed
        if packed is None or steps[:1] != [bit] or packed.shape[1] > value.shape[1]:
            return value, swap(value, bit, total), None
        steps.pop(0)
        own, packed = packed, None
        leaving = attach(value, own)
        arrived, shrinks = detach(swap(leaving, bit, total), own)
        return leaving, arrived, own + shrinks

    def settle(unit, arrived):
        nonlocal packed
        value = kept_home[unit] + arrived.astype(jnp.float32) + crossed[unit].astype(jnp.float32)
        for moved, shrinks in incoming.pop(unit, []):
            value = value + moved.astype(jnp.float32)
            packed = packed if shrinks is None else shrinks
        return value.astype(jnp.bfloat16) if unit else value

    top = units - 1
    order = [top * 4 | near | core]
    for unit in reversed(range(units)):
        order += [(unit - 1) * 4 | near | core] * (unit > 0) + [unit * 4 | core, unit * 4 | near]
        order += [(unit + 1) * 4] * (unit < top) + [0] * (not unit)
    table = jnp.array(order, dtype=jnp.int32) ^ me

    values, _, buffer = product(table, hidden, down_matrix, None, 0, 1, 0, width, False, [])
    base, ready = 1, []
    for unit in reversed(range(units)):
        arrived = swap(values, core, total)
        sent, kept = 1 + (unit > 0), 1 + (unit < top) + (not unit)
        values, results, buffer = product(
            table, hidden, down_matrix, buffer, base, sent, kept, width, not unit,
            ready,
        )
        base += sent + kept
        if unit < top:
            kept_home[unit + 1] = results[1]
        if not unit:
            kept_home[0] = results[-1]
        early = unit == max(top - 1, 0)
        ready = []
        if early:
            leaving = (results[0] + arrived[0].astype(jnp.float32)).astype(jnp.bfloat16)
            leaving, arrived, late = lax.optimization_barrier((leaving, arrived, hidden))
            packed = shrink(late, shrink_matrices, row_adapter_index)
        if unit < top:
            moving, arrived = lax.optimization_barrier((settle(unit + 1, arrived[1]), arrived))
            bit = (unit + 1) & -(unit + 1)
            moving, *came = send(moving, 4 * bit)
            incoming.setdefault((unit + 1) ^ bit, []).append(came)
            ready.append(moving)
        if not early:
            leaving = (results[0] + arrived[0].astype(jnp.float32)).astype(jnp.bfloat16)
        leaving, crossed[unit], shrinks = send(leaving, near)
        packed = packed if shrinks is None else shrinks
        ready.append(leaving)
    kept = [settle(0, swap(values, core, total)[0])]

    for bit in steps:
        kind = jnp.bfloat16 if bit > near else jnp.float32
        packed = packed + swap(packed.astype(kind), bit, total).astype(jnp.float32)
    adapter_output = expand(packed, expand_matrices, segment_first_row, segment_length)
    return (kept[0] + adapter_output).astype(jnp.bfloat16)


def solution(mesh):
    in_specs = (
        P("groups", "tensor"),
        P("tensor", None),
        P(None, "tensor", None),
        P(None, None, "tensor"),
        P("groups"),
        P("groups"),
        P("groups"),
    )
    out_specs = P("groups", "tensor")
    return jax.shard_map(
        functools.partial(on_device, mesh.shape["tensor"]),
        mesh=mesh,
        in_specs=in_specs,
        out_specs=out_specs,
        check_vma=False,
    )
```

```python
import functools

import jax
import jax.numpy as jnp
from jax import lax
from jax.experimental import pallas as pl
from jax.experimental.pallas import tpu as pltpu
from jax.sharding import PartitionSpec as P

VMEM_LIMIT = 39 * 1024 * 1024
WINDOW = 128
TOGETHER = 4
FLOPS = 10_000_000_000
EXPAND_FLOPS = 1_000_000


def product_body(table_ref, hidden_ref, down_ref, *refs, base, sent, kept, first, last, earlier):
    sent_ref = kept_ref = None
    refs = list(refs[earlier + (0 if first else 1):])
    if sent:
        sent_ref = refs.pop(0)
    if kept:
        kept_ref = refs.pop(0)
    buffer = refs.pop(0)
    arrived = refs.pop()
    width = buffer.shape[2]
    targets = sent + kept

    def copy(at):
        column = pl.multiple_of(table_ref[base + at] * width, width)
        slot = (base + at) % 2
        return pltpu.make_async_copy(
            down_ref.at[:, pl.ds(column, width)], buffer.at[slot], arrived.at[slot]
        )

    if first:
        copy(0).start()

    def step(at, carry):
        @pl.when(at + 1 < targets + (0 if last else 1))
        def _():
            copy(at + 1).start()

        @pl.when(at >= (0 if first else 1))
        def _():
            copy(at).wait()

        total = jnp.dot(
            hidden_ref[...], buffer[(base + at) % 2], preferred_element_type=jnp.float32
        )
        if sent:

            @pl.when(at < sent)
            def _():
                sent_ref[jnp.minimum(at, sent - 1)] = total.astype(jnp.bfloat16)

        if kept:

            @pl.when(at >= sent)
            def _():
                kept_ref[jnp.maximum(at - sent, 0)] = total

        return carry

    lax.fori_loop(0, targets, step, 0)
    if not last:
        copy(targets).wait()


def product(table, hidden, down_matrix, buffer, base, sent, kept, width, last, earlier):
    rows, depth = hidden.shape
    first = buffer is None
    vmem = pl.BlockSpec(memory_space=pltpu.VMEM)
    anywhere = pl.BlockSpec(memory_space=pl.ANY)
    out_shape = []
    if sent:
        out_shape.append(jax.ShapeDtypeStruct((sent, rows, width), jnp.bfloat16))
    if kept:
        out_shape.append(jax.ShapeDtypeStruct((kept, rows, width), jnp.float32))
    place = len(out_shape)
    out_shape.append(jax.ShapeDtypeStruct((2, depth, width), jnp.bfloat16))
    results = pl.pallas_call(
        functools.partial(
            product_body, base=base, sent=sent, kept=kept, first=first, last=last,
            earlier=len(earlier),
        ),
        in_specs=[
            pl.BlockSpec(memory_space=pltpu.SMEM),
            vmem,
            pl.BlockSpec(memory_space=pltpu.HBM),
        ]
        + ([] if first else [vmem])
        + [anywhere] * len(earlier),
        out_specs=[vmem] * len(out_shape),
        out_shape=out_shape,
        scratch_shapes=[pltpu.SemaphoreType.DMA((2,))],
        input_output_aliases={} if first else {3: place},
        compiler_params=pltpu.CompilerParams(vmem_limit_bytes=VMEM_LIMIT),
        cost_estimate=pl.CostEstimate(flops=FLOPS, bytes_accessed=1024, transcendentals=0),
    )(table, hidden, down_matrix, *([] if first else [buffer]), *earlier)
    return results[0] if sent else None, results[place - 1] if kept else None, results[place]


def swap(value, bit, total):
    return lax.ppermute(value, "tensor", [(place, place ^ bit) for place in range(total)])


def attach(value, packed):
    below = jnp.pad(packed.astype(jnp.bfloat16), ((0, 0), (0, value.shape[1] - packed.shape[1])))
    return jnp.concatenate([value, below])


def detach(value, packed):
    height, columns = packed.shape
    above = value.shape[0] - height
    return value[:above], value[above:, :columns].astype(jnp.float32)


def for_each_window(first_ref, length_ref, group, rows, body):
    window = min(WINDOW, rows)
    adapters = [group * TOGETHER + at for at in range(TOGETHER)]
    begins = [first_ref[adapter] for adapter in adapters]
    ends = [first_ref[adapter] + length_ref[adapter] for adapter in adapters]
    base = begins[0] // 16 * 16

    def step(at, carry):
        low = base + at * window
        start = pl.multiple_of(jnp.minimum(low, rows - window), 16)
        places = start + lax.broadcasted_iota(jnp.int32, (window, 1), 0)
        masks = [
            (places >= jnp.maximum(begin, low)) & (places < end) for begin, end in zip(begins, ends)
        ]
        body(pl.ds(start, window), masks)
        return carry

    lax.fori_loop(0, (ends[-1] - base + window - 1) // window, step, 0)


def shrink(hidden, shrink_matrices, row_adapter_index):
    adapters = shrink_matrices.shape[0]
    every_adapter = jnp.einsum(
        "hq,gqu->hgu", hidden, shrink_matrices, preferred_element_type=jnp.float32
    )
    picked = row_adapter_index[:, None] == jnp.arange(adapters, dtype=jnp.int32)[None, :]
    partial = jnp.sum(jnp.where(picked[:, :, None], every_adapter, 0.0), axis=1)
    return jnp.swapaxes(partial, 0, 1)


def expand_body(first_ref, length_ref, packed_ref, table_ref, result_ref, shrunk_ref):
    rows, rank = shrunk_ref.shape
    span = TOGETHER * rank
    shrunk_ref[...] = packed_ref[...].T.astype(jnp.bfloat16)
    result_ref[...] = jnp.zeros_like(result_ref)

    def step(group, carry):
        def body(window, masks):
            shrunk = shrunk_ref[window, :]
            spread = [jnp.where(mask, shrunk, jnp.zeros((), jnp.bfloat16)) for mask in masks]
            part = jnp.dot(
                jnp.concatenate(spread, axis=1),
                table_ref[pl.ds(pl.multiple_of(group * span, span), span), :],
                preferred_element_type=jnp.float32,
            )
            result_ref[window, :] = result_ref[window, :] + part

        for_each_window(first_ref, length_ref, group, rows, body)
        return carry

    lax.fori_loop(0, table_ref.shape[0] // span, step, 0)


def expand(packed, expand_matrices, segment_first_row, segment_length):
    rows = packed.shape[1]
    adapters, rank, width = expand_matrices.shape
    table = expand_matrices.reshape(adapters * rank, width)
    vmem = pl.BlockSpec(memory_space=pltpu.VMEM)
    return pl.pallas_call(
        expand_body,
        in_specs=[pl.BlockSpec(memory_space=pltpu.SMEM)] * 2 + [vmem] * 2,
        out_specs=vmem,
        out_shape=jax.ShapeDtypeStruct((rows, width), jnp.float32),
        scratch_shapes=[pltpu.VMEM((rows, rank), jnp.bfloat16)],
        compiler_params=pltpu.CompilerParams(vmem_limit_bytes=VMEM_LIMIT),
        cost_estimate=pl.CostEstimate(flops=EXPAND_FLOPS, bytes_accessed=1, transcendentals=0),
    )(segment_first_row, segment_length, packed, table)


def on_device(
    total,
    hidden,
    down_matrix,
    shrink_matrices,
    expand_matrices,
    row_adapter_index,
    segment_first_row,
    segment_length,
):
    me = lax.axis_index("tensor").astype(jnp.int32)
    width = down_matrix.shape[1] // total
    core, near = 1, 2
    units = total // 4

    kept_home, crossed, incoming = {}, {}, {}

    far = [4 << at for at in range((units - 1).bit_length())]
    packed, steps = None, [*far[:1], near, *far[1:], core]

    def send(value, bit):
        nonlocal packed
        if packed is None or steps[:1] != [bit] or packed.shape[1] > value.shape[1]:
            return value, swap(value, bit, total), None
        steps.pop(0)
        own, packed = packed, None
        leaving = attach(value, own)
        arrived, shrinks = detach(swap(leaving, bit, total), own)
        return leaving, arrived, own + shrinks

    def settle(unit, arrived):
        nonlocal packed
        value = kept_home[unit] + arrived.astype(jnp.float32) + crossed[unit].astype(jnp.float32)
        for moved, shrinks in incoming.pop(unit, []):
            value = value + moved.astype(jnp.float32)
            packed = packed if shrinks is None else shrinks
        return value.astype(jnp.bfloat16) if unit else value

    top = units - 1
    order = [top * 4 | near | core]
    for unit in reversed(range(units)):
        order += [(unit - 1) * 4 | near | core] * (unit > 0) + [unit * 4 | core, unit * 4 | near]
        order += [(unit + 1) * 4] * (unit < top) + [0] * (not unit)
    table = jnp.array(order, dtype=jnp.int32) ^ me

    values, _, buffer = product(table, hidden, down_matrix, None, 0, 1, 0, width, False, [])
    base, ready = 1, []
    for unit in reversed(range(units)):
        arrived = swap(values, core, total)
        sent, kept = 1 + (unit > 0), 1 + (unit < top) + (not unit)
        values, results, buffer = product(
            table, hidden, down_matrix, buffer, base, sent, kept, width, not unit,
            ready,
        )
        base += sent + kept
        if unit < top:
            kept_home[unit + 1] = results[1]
        if not unit:
            kept_home[0] = results[-1]
        if unit == max(top - 1, 0):
            late, results = lax.optimization_barrier((hidden, results))
            packed = shrink(late, shrink_matrices, row_adapter_index)
        ready = []
        if not unit:
            leaving = (results[0] + arrived[0].astype(jnp.float32)).astype(jnp.bfloat16)
            leaving, arrived = lax.optimization_barrier((leaving, arrived))
        if unit < top:
            moving, arrived = lax.optimization_barrier((settle(unit + 1, arrived[1]), arrived))
            bit = (unit + 1) & -(unit + 1)
            moving, *came = send(moving, 4 * bit)
            incoming.setdefault((unit + 1) ^ bit, []).append(came)
            ready.append(moving)
        if unit:
            leaving = (results[0] + arrived[0].astype(jnp.float32)).astype(jnp.bfloat16)
        leaving, crossed[unit], shrinks = send(leaving, near)
        packed = packed if shrinks is None else shrinks
        ready.append(leaving)
    arrived = swap(values, core, total)[0]

    for bit in steps:
        kind = jnp.bfloat16 if bit > near else jnp.float32
        packed = packed + swap(packed.astype(kind), bit, total).astype(jnp.float32)
    adapter_output = expand(packed, expand_matrices, segment_first_row, segment_length)
    return (settle(0, arrived) + adapter_output).astype(jnp.bfloat16)


def solution(mesh):
    in_specs = (
        P("groups", "tensor"),
        P("tensor", None),
        P(None, "tensor", None),
        P(None, None, "tensor"),
        P("groups"),
        P("groups"),
        P("groups"),
    )
    out_specs = P("groups", "tensor")
    return jax.shard_map(
        functools.partial(on_device, mesh.shape["tensor"]),
        mesh=mesh,
        in_specs=in_specs,
        out_specs=out_specs,
        check_vma=False,
    )
```

```python
import functools

import jax
import jax.numpy as jnp
from jax import lax
from jax.experimental import pallas as pl
from jax.experimental.pallas import tpu as pltpu
from jax.sharding import PartitionSpec as P

VMEM_LIMIT = 39 * 1024 * 1024
WINDOW = 128
TOGETHER = 4
FLOPS = 3_000_000_000
EXPAND_FLOPS = 1_000_000


def product_body(table_ref, hidden_ref, down_ref, *refs, base, sent, kept, first, last, earlier):
    sent_ref = kept_ref = None
    refs = list(refs[earlier + (0 if first else 1):])
    if sent:
        sent_ref = refs.pop(0)
    if kept:
        kept_ref = refs.pop(0)
    buffer = refs.pop(0)
    arrived = refs.pop()
    width = buffer.shape[2]
    targets = sent + kept

    def copy(at):
        column = pl.multiple_of(table_ref[base + at] * width, width)
        slot = (base + at) % 2
        return pltpu.make_async_copy(
            down_ref.at[:, pl.ds(column, width)], buffer.at[slot], arrived.at[slot]
        )

    if first:
        copy(0).start()

    def step(at, carry):
        @pl.when(at + 1 < targets + (0 if last else 1))
        def _():
            copy(at + 1).start()

        @pl.when(at >= (0 if first else 1))
        def _():
            copy(at).wait()

        total = jnp.dot(
            hidden_ref[...], buffer[(base + at) % 2], preferred_element_type=jnp.float32
        )
        if sent:

            @pl.when(at < sent)
            def _():
                sent_ref[jnp.minimum(at, sent - 1)] = total.astype(jnp.bfloat16)

        if kept:

            @pl.when(at >= sent)
            def _():
                kept_ref[jnp.maximum(at - sent, 0)] = total

        return carry

    lax.fori_loop(0, targets, step, 0)
    if not last:
        copy(targets).wait()


def product(table, hidden, down_matrix, buffer, base, sent, kept, width, last, earlier):
    rows, depth = hidden.shape
    first = buffer is None
    vmem = pl.BlockSpec(memory_space=pltpu.VMEM)
    anywhere = pl.BlockSpec(memory_space=pl.ANY)
    out_shape = []
    if sent:
        out_shape.append(jax.ShapeDtypeStruct((sent, rows, width), jnp.bfloat16))
    if kept:
        out_shape.append(jax.ShapeDtypeStruct((kept, rows, width), jnp.float32))
    place = len(out_shape)
    out_shape.append(jax.ShapeDtypeStruct((2, depth, width), jnp.bfloat16))
    results = pl.pallas_call(
        functools.partial(
            product_body, base=base, sent=sent, kept=kept, first=first, last=last,
            earlier=len(earlier),
        ),
        in_specs=[
            pl.BlockSpec(memory_space=pltpu.SMEM),
            vmem,
            pl.BlockSpec(memory_space=pltpu.HBM),
        ]
        + ([] if first else [vmem])
        + [anywhere] * len(earlier),
        out_specs=[vmem] * len(out_shape),
        out_shape=out_shape,
        scratch_shapes=[pltpu.SemaphoreType.DMA((2,))],
        input_output_aliases={} if first else {3: place},
        compiler_params=pltpu.CompilerParams(vmem_limit_bytes=VMEM_LIMIT),
        cost_estimate=pl.CostEstimate(flops=FLOPS, bytes_accessed=1024, transcendentals=0),
    )(table, hidden, down_matrix, *([] if first else [buffer]), *earlier)
    return results[0] if sent else None, results[place - 1] if kept else None, results[place]


def swap(value, bit, total):
    return lax.ppermute(value, "tensor", [(place, place ^ bit) for place in range(total)])


def attach(value, packed):
    below = jnp.pad(packed.astype(jnp.bfloat16), ((0, 0), (0, value.shape[1] - packed.shape[1])))
    return jnp.concatenate([value, below])


def detach(value, packed):
    height, columns = packed.shape
    above = value.shape[0] - height
    return value[:above], value[above:, :columns].astype(jnp.float32)


def for_each_window(first_ref, length_ref, group, rows, body):
    window = min(WINDOW, rows)
    adapters = [group * TOGETHER + at for at in range(TOGETHER)]
    begins = [first_ref[adapter] for adapter in adapters]
    ends = [first_ref[adapter] + length_ref[adapter] for adapter in adapters]
    base = begins[0] // 16 * 16

    def step(at, carry):
        low = base + at * window
        start = pl.multiple_of(jnp.minimum(low, rows - window), 16)
        places = start + lax.broadcasted_iota(jnp.int32, (window, 1), 0)
        masks = [
            (places >= jnp.maximum(begin, low)) & (places < end) for begin, end in zip(begins, ends)
        ]
        body(pl.ds(start, window), masks)
        return carry

    lax.fori_loop(0, (ends[-1] - base + window - 1) // window, step, 0)


def shrink(hidden, shrink_matrices, row_adapter_index):
    adapters = shrink_matrices.shape[0]
    every_adapter = jnp.einsum(
        "hq,gqu->hgu", hidden, shrink_matrices, preferred_element_type=jnp.float32
    )
    picked = row_adapter_index[:, None] == jnp.arange(adapters, dtype=jnp.int32)[None, :]
    partial = jnp.sum(jnp.where(picked[:, :, None], every_adapter, 0.0), axis=1)
    return jnp.swapaxes(partial, 0, 1)


def expand_body(first_ref, length_ref, packed_ref, table_ref, result_ref, shrunk_ref):
    rows, rank = shrunk_ref.shape
    span = TOGETHER * rank
    shrunk_ref[...] = packed_ref[...].T.astype(jnp.bfloat16)
    result_ref[...] = jnp.zeros_like(result_ref)

    def step(group, carry):
        def body(window, masks):
            shrunk = shrunk_ref[window, :]
            spread = [jnp.where(mask, shrunk, jnp.zeros((), jnp.bfloat16)) for mask in masks]
            part = jnp.dot(
                jnp.concatenate(spread, axis=1),
                table_ref[pl.ds(pl.multiple_of(group * span, span), span), :],
                preferred_element_type=jnp.float32,
            )
            result_ref[window, :] = result_ref[window, :] + part

        for_each_window(first_ref, length_ref, group, rows, body)
        return carry

    lax.fori_loop(0, table_ref.shape[0] // span, step, 0)


def expand(packed, expand_matrices, segment_first_row, segment_length):
    rows = packed.shape[1]
    adapters, rank, width = expand_matrices.shape
    table = expand_matrices.reshape(adapters * rank, width)
    vmem = pl.BlockSpec(memory_space=pltpu.VMEM)
    return pl.pallas_call(
        expand_body,
        in_specs=[pl.BlockSpec(memory_space=pltpu.SMEM)] * 2 + [vmem] * 2,
        out_specs=vmem,
        out_shape=jax.ShapeDtypeStruct((rows, width), jnp.float32),
        scratch_shapes=[pltpu.VMEM((rows, rank), jnp.bfloat16)],
        compiler_params=pltpu.CompilerParams(vmem_limit_bytes=VMEM_LIMIT),
        cost_estimate=pl.CostEstimate(flops=EXPAND_FLOPS, bytes_accessed=1, transcendentals=0),
    )(segment_first_row, segment_length, packed, table)


def on_device(
    total,
    hidden,
    down_matrix,
    shrink_matrices,
    expand_matrices,
    row_adapter_index,
    segment_first_row,
    segment_length,
):
    me = lax.axis_index("tensor").astype(jnp.int32)
    width = down_matrix.shape[1] // total
    core, near = 1, 2
    units = total // 4

    kept_home, crossed, incoming = {}, {}, {}

    far = [4 << at for at in range((units - 1).bit_length())]
    packed, steps = None, [*far[:1], near, *far[1:], core]

    def send(value, bit):
        nonlocal packed
        if packed is None or steps[:1] != [bit] or packed.shape[1] > value.shape[1]:
            return value, swap(value, bit, total), None
        steps.pop(0)
        own, packed = packed, None
        leaving = attach(value, own)
        arrived, shrinks = detach(swap(leaving, bit, total), own)
        return leaving, arrived, own + shrinks

    def settle(unit, arrived):
        nonlocal packed
        value = kept_home[unit] + arrived.astype(jnp.float32) + crossed[unit].astype(jnp.float32)
        for moved, shrinks in incoming.pop(unit, []):
            value = value + moved.astype(jnp.float32)
            packed = packed if shrinks is None else shrinks
        return value.astype(jnp.bfloat16) if unit else value

    top = units - 1
    order = [top * 4 | near | core]
    for unit in reversed(range(units)):
        order += [(unit - 1) * 4 | near | core] * (unit > 0) + [unit * 4 | core, unit * 4 | near]
        order += [(unit + 1) * 4] * (unit < top) + [0] * (not unit)
    table = jnp.array(order, dtype=jnp.int32) ^ me

    values, _, buffer = product(table, hidden, down_matrix, None, 0, 1, 0, width, False, [])
    base, ready = 1, []
    for unit in reversed(range(units)):
        arrived = swap(values, core, total)
        sent, kept = 1 + (unit > 0), 1 + (unit < top) + (not unit)
        values, results, buffer = product(
            table, hidden, down_matrix, buffer, base, sent, kept, width, not unit,
            ready,
        )
        base += sent + kept
        if unit < top:
            kept_home[unit + 1] = results[1]
        if not unit:
            kept_home[0] = results[-1]
        if unit == max(top - 1, 0):
            late, results = lax.optimization_barrier((hidden, results))
            packed = shrink(late, shrink_matrices, row_adapter_index)
        ready = []
        if not unit:
            leaving = (results[0] + arrived[0].astype(jnp.float32)).astype(jnp.bfloat16)
            leaving, arrived = lax.optimization_barrier((leaving, arrived))
        if unit < top:
            moving, arrived = lax.optimization_barrier((settle(unit + 1, arrived[1]), arrived))
            bit = (unit + 1) & -(unit + 1)
            moving, *came = send(moving, 4 * bit)
            incoming.setdefault((unit + 1) ^ bit, []).append(came)
            ready.append(moving)
        if unit:
            leaving = (results[0] + arrived[0].astype(jnp.float32)).astype(jnp.bfloat16)
        leaving, crossed[unit], shrinks = send(leaving, near)
        packed = packed if shrinks is None else shrinks
        ready.append(leaving)
    arrived = swap(values, core, total)[0]

    for bit in steps:
        kind = jnp.bfloat16 if bit > near else jnp.float32
        packed = packed + swap(packed.astype(kind), bit, total).astype(jnp.float32)
    adapter_output = expand(packed, expand_matrices, segment_first_row, segment_length)
    return (settle(0, arrived) + adapter_output).astype(jnp.bfloat16)


def solution(mesh):
    in_specs = (
        P("groups", "tensor"),
        P("tensor", None),
        P(None, "tensor", None),
        P(None, None, "tensor"),
        P("groups"),
        P("groups"),
        P("groups"),
    )
    out_specs = P("groups", "tensor")
    return jax.shard_map(
        functools.partial(on_device, mesh.shape["tensor"]),
        mesh=mesh,
        in_specs=in_specs,
        out_specs=out_specs,
        check_vma=False,
    )
```

```python
import functools

import jax
import jax.numpy as jnp
from jax import lax
from jax.experimental import pallas as pl
from jax.experimental.pallas import tpu as pltpu
from jax.sharding import PartitionSpec as P

VMEM_LIMIT = 39 * 1024 * 1024
WINDOW = 128
TOGETHER = 4
FLOPS = 3_000_000_000
EXPAND_FLOPS = 1_000_000


def product_body(table_ref, hidden_ref, down_ref, *refs, base, sent, kept, first, last, earlier):
    sent_ref = kept_ref = None
    refs = list(refs[earlier + (0 if first else 1):])
    if sent:
        sent_ref = refs.pop(0)
    if kept:
        kept_ref = refs.pop(0)
    buffer = refs.pop(0)
    arrived = refs.pop()
    width = buffer.shape[2]
    targets = sent + kept

    def copy(at):
        column = pl.multiple_of(table_ref[base + at] * width, width)
        slot = (base + at) % 2
        return pltpu.make_async_copy(
            down_ref.at[:, pl.ds(column, width)], buffer.at[slot], arrived.at[slot]
        )

    if first:
        copy(0).start()

    def step(at, carry):
        @pl.when(at + 1 < targets + (0 if last else 1))
        def _():
            copy(at + 1).start()

        @pl.when(at >= (0 if first else 1))
        def _():
            copy(at).wait()

        total = jnp.dot(
            hidden_ref[...], buffer[(base + at) % 2], preferred_element_type=jnp.float32
        )
        if sent:

            @pl.when(at < sent)
            def _():
                sent_ref[jnp.minimum(at, sent - 1)] = total.astype(jnp.bfloat16)

        if kept:

            @pl.when(at >= sent)
            def _():
                kept_ref[jnp.maximum(at - sent, 0)] = total

        return carry

    lax.fori_loop(0, targets, step, 0)
    if not last:
        copy(targets).wait()


def product(table, hidden, down_matrix, buffer, base, sent, kept, width, last, earlier):
    rows, depth = hidden.shape
    first = buffer is None
    vmem = pl.BlockSpec(memory_space=pltpu.VMEM)
    anywhere = pl.BlockSpec(memory_space=pl.ANY)
    out_shape = []
    if sent:
        out_shape.append(jax.ShapeDtypeStruct((sent, rows, width), jnp.bfloat16))
    if kept:
        out_shape.append(jax.ShapeDtypeStruct((kept, rows, width), jnp.float32))
    place = len(out_shape)
    out_shape.append(jax.ShapeDtypeStruct((2, depth, width), jnp.bfloat16))
    results = pl.pallas_call(
        functools.partial(
            product_body, base=base, sent=sent, kept=kept, first=first, last=last,
            earlier=len(earlier),
        ),
        in_specs=[
            pl.BlockSpec(memory_space=pltpu.SMEM),
            vmem,
            pl.BlockSpec(memory_space=pltpu.HBM),
        ]
        + ([] if first else [vmem])
        + [anywhere] * len(earlier),
        out_specs=[vmem] * len(out_shape),
        out_shape=out_shape,
        scratch_shapes=[pltpu.SemaphoreType.DMA((2,))],
        input_output_aliases={} if first else {3: place},
        compiler_params=pltpu.CompilerParams(vmem_limit_bytes=VMEM_LIMIT),
        cost_estimate=pl.CostEstimate(flops=FLOPS, bytes_accessed=1024, transcendentals=0),
    )(table, hidden, down_matrix, *([] if first else [buffer]), *earlier)
    return results[0] if sent else None, results[place - 1] if kept else None, results[place]


def swap(value, bit, total):
    return lax.ppermute(value, "tensor", [(place, place ^ bit) for place in range(total)])


def attach(value, packed):
    below = jnp.pad(packed.astype(jnp.bfloat16), ((0, 0), (0, value.shape[1] - packed.shape[1])))
    return jnp.concatenate([value, below])


def detach(value, packed):
    height, columns = packed.shape
    above = value.shape[0] - height
    return value[:above], value[above:, :columns].astype(jnp.float32)


def for_each_window(first_ref, length_ref, group, rows, body):
    window = min(WINDOW, rows)
    adapters = [group * TOGETHER + at for at in range(TOGETHER)]
    begins = [first_ref[adapter] for adapter in adapters]
    ends = [first_ref[adapter] + length_ref[adapter] for adapter in adapters]
    base = begins[0] // 16 * 16

    def step(at, carry):
        low = base + at * window
        start = pl.multiple_of(jnp.minimum(low, rows - window), 16)
        places = start + lax.broadcasted_iota(jnp.int32, (window, 1), 0)
        masks = [
            (places >= jnp.maximum(begin, low)) & (places < end) for begin, end in zip(begins, ends)
        ]
        body(pl.ds(start, window), masks)
        return carry

    lax.fori_loop(0, (ends[-1] - base + window - 1) // window, step, 0)


def shrink(hidden, shrink_matrices, row_adapter_index):
    adapters = shrink_matrices.shape[0]
    every_adapter = jnp.einsum(
        "hq,gqu->hgu", hidden, shrink_matrices, preferred_element_type=jnp.float32
    )
    picked = row_adapter_index[:, None] == jnp.arange(adapters, dtype=jnp.int32)[None, :]
    partial = jnp.sum(jnp.where(picked[:, :, None], every_adapter, 0.0), axis=1)
    return jnp.swapaxes(partial, 0, 1)


def expand_body(first_ref, length_ref, packed_ref, table_ref, result_ref, shrunk_ref):
    rows, rank = shrunk_ref.shape
    span = TOGETHER * rank
    shrunk_ref[...] = packed_ref[...].T.astype(jnp.bfloat16)
    result_ref[...] = jnp.zeros_like(result_ref)

    def step(group, carry):
        def body(window, masks):
            shrunk = shrunk_ref[window, :]
            spread = [jnp.where(mask, shrunk, jnp.zeros((), jnp.bfloat16)) for mask in masks]
            part = jnp.dot(
                jnp.concatenate(spread, axis=1),
                table_ref[pl.ds(pl.multiple_of(group * span, span), span), :],
                preferred_element_type=jnp.float32,
            )
            result_ref[window, :] = result_ref[window, :] + part

        for_each_window(first_ref, length_ref, group, rows, body)
        return carry

    lax.fori_loop(0, table_ref.shape[0] // span, step, 0)


def expand(packed, expand_matrices, segment_first_row, segment_length):
    rows = packed.shape[1]
    adapters, rank, width = expand_matrices.shape
    table = expand_matrices.reshape(adapters * rank, width)
    vmem = pl.BlockSpec(memory_space=pltpu.VMEM)
    return pl.pallas_call(
        expand_body,
        in_specs=[pl.BlockSpec(memory_space=pltpu.SMEM)] * 2 + [vmem] * 2,
        out_specs=vmem,
        out_shape=jax.ShapeDtypeStruct((rows, width), jnp.float32),
        scratch_shapes=[pltpu.VMEM((rows, rank), jnp.bfloat16)],
        compiler_params=pltpu.CompilerParams(vmem_limit_bytes=VMEM_LIMIT),
        cost_estimate=pl.CostEstimate(flops=EXPAND_FLOPS, bytes_accessed=1, transcendentals=0),
    )(segment_first_row, segment_length, packed, table)


def on_device(
    total,
    hidden,
    down_matrix,
    shrink_matrices,
    expand_matrices,
    row_adapter_index,
    segment_first_row,
    segment_length,
):
    me = lax.axis_index("tensor").astype(jnp.int32)
    width = down_matrix.shape[1] // total
    core, near = 1, 2
    units = total // 4

    kept_home, crossed, incoming = {}, {}, {}

    far = [4 << at for at in range((units - 1).bit_length())]
    packed, steps = None, [*far[:1], core, *far[1:], near]

    def send(value, bit):
        nonlocal packed
        if packed is None or steps[:1] != [bit] or packed.shape[1] > value.shape[1]:
            return value, swap(value, bit, total), None
        steps.pop(0)
        own, packed = packed, None
        leaving = attach(value, own)
        arrived, shrinks = detach(swap(leaving, bit, total), own)
        return leaving, arrived, own + shrinks

    def settle(unit, arrived):
        nonlocal packed
        value = kept_home[unit] + arrived.astype(jnp.float32) + crossed[unit].astype(jnp.float32)
        for moved, shrinks in incoming.pop(unit, []):
            value = value + moved.astype(jnp.float32)
            packed = packed if shrinks is None else shrinks
        return value.astype(jnp.bfloat16) if unit else value

    top = units - 1
    order = [top * 4 | near | core]
    for unit in reversed(range(units)):
        order += [(unit - 1) * 4 | near | core] * (unit > 0) + [unit * 4 | core, unit * 4 | near]
        order += [(unit + 1) * 4] * (unit < top) + [0] * (not unit)
    table = jnp.array(order, dtype=jnp.int32) ^ me

    values, _, buffer = product(table, hidden, down_matrix, None, 0, 1, 0, width, False, [])
    base, ready = 1, []
    for unit in reversed(range(units)):
        arrived = swap(values, core, total)
        sent, kept = 1 + (unit > 0), 1 + (unit < top) + (not unit)
        values, results, buffer = product(
            table, hidden, down_matrix, buffer, base, sent, kept, width, not unit,
            ready,
        )
        base += sent + kept
        if packed is not None and steps[:1] == [core]:
            steps.pop(0)
            moved, results = lax.optimization_barrier((swap(packed, core, total), results))
            packed = packed + moved
        if unit < top:
            kept_home[unit + 1] = results[1]
        if not unit:
            kept_home[0] = results[-1]
        if unit == max(top - 1, 0):
            late, results = lax.optimization_barrier((hidden, results))
            packed = shrink(late, shrink_matrices, row_adapter_index)
        ready = []
        if unit < top:
            moving, arrived = lax.optimization_barrier((settle(unit + 1, arrived[1]), arrived))
            bit = (unit + 1) & -(unit + 1)
            moving, *came = send(moving, 4 * bit)
            incoming.setdefault((unit + 1) ^ bit, []).append(came)
            ready.append(moving)
        leaving = (results[0] + arrived[0].astype(jnp.float32)).astype(jnp.bfloat16)
        leaving, crossed[unit], shrinks = send(leaving, near)
        packed = packed if shrinks is None else shrinks
        ready.append(leaving)
    kept = [settle(0, swap(values, core, total)[0])]

    for bit in steps:
        kind = jnp.bfloat16 if bit > near else jnp.float32
        packed = packed + swap(packed.astype(kind), bit, total).astype(jnp.float32)
    adapter_output = expand(packed, expand_matrices, segment_first_row, segment_length)
    return (kept[0] + adapter_output).astype(jnp.bfloat16)


def solution(mesh):
    in_specs = (
        P("groups", "tensor"),
        P("tensor", None),
        P(None, "tensor", None),
        P(None, None, "tensor"),
        P("groups"),
        P("groups"),
        P("groups"),
    )
    out_specs = P("groups", "tensor")
    return jax.shard_map(
        functools.partial(on_device, mesh.shape["tensor"]),
        mesh=mesh,
        in_specs=in_specs,
        out_specs=out_specs,
        check_vma=False,
    )
```
